128 devices in a mesh: wide: 32 (over z_hi, y, x), narrow: 4 (over z_lo, core).
Axes of the slice: x: 4, y: 4, z: 4 (z_hi: 2, z_lo: 2; z = z_hi * 2 + z_lo), core: 2. Of those that a mesh axis runs over, the one named last changes fastest.
Arguments:
- tokens: bfloat16 [32768, 768], P('wide'), may hold values from -6 to 6
- cotangent: bfloat16 [32768, 768], P('wide'), may hold values from -6 to 6
- seg_ids: int32 [32, 1024], P('wide'), may hold values from 0 to 23, never falling along the last dimension, each value on 1 to 256 neighbouring positions
- pad_len: int32 [32], P('wide'), may hold values from 0 to 255
- qkv_weight: bfloat16 [3, 768, 768], P(None, None, 'narrow'), may hold values from -0.21875 to 0.21875
- query_gain: float32 [768], P('narrow'), may hold values from 0.1 to 1.9
- key_gain: float32 [768], P('narrow'), may hold values from 0.1 to 1.9
- out_weight: bfloat16 [768, 768], P('narrow'), may hold values from -0.625 to 0.625
- up_weight: bfloat16 [768, 3072], P(None, 'narrow'), may hold values from -0.21875 to 0.21875
- down_weight: bfloat16 [3072, 768], P('narrow'), may hold values from -0.21875 to 0.21875
- attn_gain: float32 [768], replicated, may hold values from 0.1 to 1.9
- attn_shift: float32 [768], replicated, may hold values from -3 to 3
- mlp_gain: float32 [768], replicated, may hold values from 0.1 to 1.9
- mlp_shift: float32 [768], replicated, may hold values from -3 to 3
Outputs:
- layer_out: bfloat16 [32768, 768], P('wide')
- grad_tokens: bfloat16 [32768, 768], P('wide')
- grad_qkv: float32 [3, 768, 768], P(None, None, 'narrow')
- grad_query_gain: float32 [768], P('narrow')
- grad_key_gain: float32 [768], P('narrow')
- grad_out_weight: float32 [768, 768], P('narrow')
- grad_up: float32 [768, 3072], P(None, 'narrow')
- grad_down: float32 [3072, 768], P('narrow')
- grad_attn_gain: float32 [768], replicated
- grad_attn_shift: float32 [768], replicated
- grad_mlp_gain: float32 [768], replicated
- grad_mlp_shift: float32 [768], replicated
The draws below stay inside these ranges and needn't reach their ends.
Inputs may be any that keep to these rules, and one draw needn't show every extreme that they name: `seg_ids`: within each sequence the image numbers never fall, each image has 1 to 256 patches and some image has exactly 256.
All inputs are finite; a program needn't handle non-finite values.
Results may differ from the reference program's by a relative error of at most 0.03.
Values may be sent and summed in bfloat16 or wider, within the bound.
A program may use at most 128 MiB of HBM per device.

```python
import math
import jax
import jax.numpy as jnp
import numpy as np
from jax import lax

D = 768
HEADS = 12
FF = 3072
LEN = 1024
IMGS = 24
MOST_IMG = 256
NSEQ = 32
TOKENS = 32768
N_NARROW = 4


def plant(drawn, own_key, low, high):
    dims = drawn.shape
    spot = [jax.random.randint(jax.random.fold_in(own_key, axis), (), 0, dims[axis]) for axis in range(len(dims))]
    drawn = drawn.at[tuple(spot)].set(low)
    longest = dims.index(max(dims))
    spot[longest] = (spot[longest] + 1) % dims[longest]
    return drawn.at[tuple(spot)].set(high)


def steps_of(own_key, dims, split, low, high):
    level, own = 1.0, jax.random.fold_in(own_key, 6)
    for axis_at, shards_of in split:
        heights = jnp.exp(jax.random.uniform(jax.random.fold_in(own, axis_at), (shards_of,), jnp.float32, low / len(split), high / len(split)))
        level = level * jnp.repeat(heights, dims[axis_at] // shards_of).reshape([-1 if axis == axis_at else 1 for axis in range(len(dims))])
    return level


def length_profile(count, total, most, lean):
    portions = [(1 << 20) // math.isqrt(grade ** lean) + 1 for grade in range(2, count + 1)]
    rest, counts = total - most - (count - 1), [1] * (count - 1)
    while rest > 0:
        free = [i for i in range(count - 1) if counts[i] < most]
        whole, remaining = sum([portions[i] for i in free]), rest
        for i in free:
            addition = min(most - counts[i], max(1, remaining * portions[i] // whole), rest)
            counts[i] = counts[i] + addition
            rest = rest - addition
    return np.array([most] + counts)


def uneven(stream_key, count, total, most, slope):
    if count == 2:
        one = jax.random.randint(stream_key, (), max(1, total - most), min(most, total - 1) + 1)
        return jnp.stack([one, total - one])
    tallies = jnp.asarray(length_profile(count, total, most, slope), jnp.int32)
    couples = (count - 1) // 2
    giver, receiver = tallies[1:1 + 2 * couples:2], tallies[2:2 + 2 * couples:2]
    slack = jnp.minimum(giver - 1, most - receiver)
    moved = jax.random.randint(jax.random.fold_in(stream_key, 1), (couples,), 0, 1 << 20) % (slack + 1)
    tallies = tallies.at[1:1 + 2 * couples:2].set(giver - moved).at[2:2 + 2 * couples:2].set(receiver + moved)
    return tallies[jax.random.permutation(jax.random.fold_in(stream_key, 2), count)]


def gaussian(own_key, shape, scale, most, pieces=(), held_as=jnp.bfloat16):
    factor_of = steps_of(own_key, shape, pieces, -0.22, 0.18) if pieces else 1.0
    values = jax.random.normal(own_key, shape, jnp.float32) * scale * factor_of
    return jnp.minimum(jnp.maximum(values, -most), most).astype(held_as)


def setup_inputs(seed: int = 0) -> dict:
    key_of = jax.random.split(jax.random.key(seed), 15)
    return {
        "tokens": gaussian(key_of[0], (TOKENS, D), 1.0, 6.0, ((0, 32),)),
        "cotangent": gaussian(key_of[1], (TOKENS, D), 1.0, 6.0, ((0, 32),)),
        "seg_ids": jax.vmap(lambda own: jnp.searchsorted(jnp.cumsum(uneven(own, IMGS, LEN, MOST_IMG, 2)), jnp.arange(LEN), side="right"))(jax.random.split(key_of[2], NSEQ)).reshape((NSEQ, LEN)).astype(jnp.int32),
        "pad_len": plant(jax.random.randint(key_of[3], (NSEQ,), 0, LEN // 4), jax.random.fold_in(key_of[3], 1), 0, (LEN // 4) - 1).astype(jnp.int32),
        "qkv_weight": gaussian(key_of[4], (3, D, D), D ** -0.5, 0.21875, ((2, 4),)),
        "query_gain": jnp.clip(1.0 + 0.18 * jax.random.normal(key_of[5], (D,), jnp.float32), 0.1, 1.9),
        "key_gain": jnp.clip(1.0 + 0.18 * jax.random.normal(key_of[6], (D,), jnp.float32), 0.1, 1.9),
        "out_weight": gaussian(key_of[7], (D, D), (D // 8) ** -0.5, 0.625, ((0, 4),)),
        "up_weight": gaussian(key_of[8], (D, FF), D ** -0.5, 0.21875, ((1, 4),)),
        "down_weight": gaussian(key_of[9], (FF, D), (FF // 4) ** -0.5, 0.21875, ((0, 4),)),
        "attn_gain": jnp.clip(1.0 + 0.18 * jax.random.normal(key_of[10], (D,), jnp.float32), 0.1, 1.9),
        "attn_shift": gaussian(key_of[11], (D,), 0.5, 3.0, (), jnp.float32),
        "mlp_gain": jnp.clip(1.0 + 0.18 * jax.random.normal(key_of[12], (D,), jnp.float32), 0.1, 1.9),
        "mlp_shift": gaussian(key_of[13], (D,), 0.5, 3.0, (), jnp.float32),
    }


@jax.custom_vjp
def low(v):
    return lax.optimization_barrier(v.astype(jnp.bfloat16)).astype(jnp.float32)

@jax.custom_vjp
def low_back(v):
    return v

def low_keep(v):
    return (low(v), None)

def low_pass(kept, grad):
    return (grad,)

def back_keep(v):
    return (v, None)

def back_low(kept, grad):
    return (low(grad),)
low.defvjp(low_keep, low_pass)
low_back.defvjp(back_keep, back_low)

def layer_norm(values, gain, shift):
    centre = values - lax.optimization_barrier(jnp.mean(values, axis=-1, keepdims=True))
    spread = lax.optimization_barrier(jnp.mean(centre * centre, axis=-1, keepdims=True))
    return centre * lax.rsqrt(spread + 1e-06) * gain + shift

def head_norm(values, gain, heads):
    count = values.shape[0]
    shaped = values.reshape(count, heads, -1)
    centre = shaped - lax.optimization_barrier(jnp.mean(shaped, axis=-1, keepdims=True))
    spread = lax.optimization_barrier(jnp.mean(centre * centre, axis=-1, keepdims=True))
    normed = centre * lax.rsqrt(spread + 1e-06) * gain.reshape(heads, -1)
    return normed.reshape(count, -1)

def allowed_keys(segment, valid, start, block):
    length = segment.shape[0]
    places = jnp.arange(length, dtype=jnp.int32)
    query_seg = lax.dynamic_slice_in_dim(segment, start, block)
    query_pos = start + jnp.arange(block, dtype=jnp.int32)
    same = (query_seg[:, None] == segment[None, :]) & valid[None, :]
    return same | (query_pos[:, None] == places[None, :])

def attend(queries, keys, values, segment, valid, heads):
    length, width = queries.shape
    block = min(512, length)
    scale = (width // heads) ** (-0.5)
    key_heads = keys.reshape(length, heads, -1)
    value_heads = values.reshape(length, heads, -1)
    query_blocks = queries.reshape(length // block, block, heads, -1)
    starts = jnp.arange(length // block, dtype=jnp.int32) * block

    def one_block(pair):
        query_block, start = pair
        scores = jnp.einsum('qhd,khd->hqk', query_block, key_heads, precision=lax.Precision.HIGHEST) * scale
        scores = low_back(scores)
        scores = jnp.where(allowed_keys(segment, valid, start, block)[None], scores, -1e+30)
        top = lax.optimization_barrier(jnp.max(scores, axis=-1, keepdims=True))
        weights = jnp.exp(scores - top)
        probs = low(weights / lax.optimization_barrier(jnp.sum(weights, axis=-1, keepdims=True)))
        mixed = jnp.einsum('hqk,khd->qhd', probs, value_heads, precision=lax.Precision.HIGHEST)
        return mixed.reshape(block, width)
    return lax.map(jax.checkpoint(one_block), (query_blocks, starts)).reshape(length, width)

def forward(params, values, segment, padding):
    qkv_weight, query_gain, key_gain, out_weight, up_weight, down_weight, attn_gain, attn_shift, mlp_gain, mlp_shift = params
    length = values.shape[0]
    valid = jnp.arange(length, dtype=jnp.int32) < length - padding
    heads_local = HEADS // N_NARROW
    width_local = D // N_NARROW
    hidden_local = FF // N_NARROW
    highest = lax.Precision.HIGHEST
    normed = low(layer_norm(values, attn_gain, attn_shift))
    attn_total = jnp.zeros((length, D), jnp.float32)
    for group in range(N_NARROW):
        lower = group * width_local
        upper = lower + width_local
        local_in = low_back(normed)
        query_raw = low_back(jnp.dot(local_in, qkv_weight[0][:, lower:upper], precision=highest))
        key_raw = low_back(jnp.dot(local_in, qkv_weight[1][:, lower:upper], precision=highest))
        value_raw = jnp.dot(local_in, qkv_weight[2][:, lower:upper], precision=highest)
        queries = low(head_norm(query_raw, query_gain[lower:upper], heads_local))
        keys = low(head_norm(key_raw, key_gain[lower:upper], heads_local))
        vals = low(low_back(value_raw))
        mixed = low(low_back(attend(queries, keys, vals, segment, valid, heads_local)))
        attn_total = attn_total + low(jnp.dot(mixed, out_weight[lower:upper], precision=highest))
    middle = values + low_back(attn_total)
    normed_two = low(layer_norm(middle, mlp_gain, mlp_shift))
    mlp_total = jnp.zeros((length, D), jnp.float32)
    for group in range(N_NARROW):
        lower = group * hidden_local
        upper = lower + hidden_local
        local_two = low_back(normed_two)
        pre_act = low_back(jnp.dot(local_two, up_weight[:, lower:upper], precision=highest))
        active = low(jax.nn.gelu(pre_act))
        mlp_total = mlp_total + low(jnp.dot(active, down_weight[lower:upper], precision=highest))
    return middle + mlp_total

def reference(tokens, cotangent, seg_ids, pad_len, qkv_weight, query_gain, key_gain, out_weight, up_weight, down_weight, attn_gain, attn_shift, mlp_gain, mlp_shift):
    params = tuple((item.astype(jnp.float32) for item in (qkv_weight, query_gain, key_gain, out_weight, up_weight, down_weight, attn_gain, attn_shift, mlp_gain, mlp_shift)))
    inputs = tokens.astype(jnp.float32).reshape(NSEQ, LEN, D)
    grads_in = cotangent.astype(jnp.float32).reshape(NSEQ, LEN, D)

    def one_sequence(totals, item):
        values, grad_seq, segment, padding = item
        result, backward = jax.vjp(lambda pars, vals: forward(pars, vals, segment, padding), params, values)
        grad_params, grad_values = backward(grad_seq)
        totals = jax.tree.map(lambda left, right: left + right, totals, grad_params)
        return (totals, (result.astype(jnp.bfloat16), grad_values.astype(jnp.bfloat16)))
    zeros = tuple((jnp.zeros_like(item) for item in params))
    totals, (outputs, grad_inputs) = lax.scan(one_sequence, zeros, (inputs, grads_in, seg_ids, pad_len))
    return (outputs.reshape(TOKENS, D), grad_inputs.reshape(TOKENS, D), totals[0], totals[1], totals[2], totals[3], totals[4], totals[5], totals[6], totals[7], totals[8], totals[9])
```

```python
import functools

import jax
import jax.numpy as jnp
from jax import lax
from jax.experimental import pallas as pl
from jax.experimental.pallas import tpu as pltpu
from jax.sharding import PartitionSpec as P

T = 1024
D = 768
HEADS = 3
HD = 64
W = HEADS * HD
F = 768
BLK = 256
CH = T // BLK
HALF = BLK // 2
BIG = 2048.0
SC = 0.125 * 1.4426950408889634
EPS = 1e-06
GELU_A = 0.7978845608028654
GELU_B = 0.044715 * GELU_A

BF = jnp.bfloat16
F32 = jnp.float32
MESH = pl.DeviceIdType.MESH


def nn(a, b):
    return lax.dot_general(a, b, (((1,), (0,)), ((), ())), preferred_element_type=F32)


def nt(a, b):
    return lax.dot_general(a, b, (((1,), (1,)), ((), ())), preferred_element_type=F32)


def tn(a, b):
    return lax.dot_general(a, b, (((0,), (0,)), ((), ())), preferred_element_type=F32)


def at(start, size, unit):
    return pl.ds(pl.multiple_of(start, unit), size)


def chunk(b):
    return at(b * BLK, BLK, BLK)


def moments(values):
    centre = values - jnp.mean(values, axis=-1, keepdims=True)
    rstd = lax.rsqrt(jnp.mean(centre * centre, axis=-1, keepdims=True) + EPS)
    return centre * rstd, rstd


def norm_back(grad, hat, rstd):
    return rstd * (
        grad
        - jnp.mean(grad, axis=-1, keepdims=True)
        - hat * jnp.mean(grad * hat, axis=-1, keepdims=True)
    )


SCRATCH = dict(
    x=((T, D), BF),
    dy=((T, D), BF),
    wraw=((3, D, W), BF),
    wt=((3 * W, D), BF),
    wo=((4 * W, D), BF),
    up=((D, F), BF),
    dn=((F, D), BF),
    normed=((T, D), BF),
    qta=((HEADS, 2 * HD, T), BF),
    kta=((HEADS, 2 * HD, T), BF),
    vt=((W, T), BF),
    qn=((HEADS, T, 2 * HD), BF),
    kn=((HEADS, T, 2 * HD), BF),
    vn=((HEADS, T, 2 * HD), BF),
    hat=((2 * W, T), F32),
    rstd=((6, 1, T), F32),
    lse=((HEADS, 1, T), F32),
    gcol=((2 * W, 128), F32),
    mixed=((4 * W, T), BF),
    mixf=((W, T), F32),
    mid=((T, D), F32),
    normed2=((T, D), BF),
    active=((T, F), BF),
    gpre=((T, F), BF),
    big0=((BLK, D), F32),
    big1=((BLK, D), F32),
    p2=((T, D), BF),
    p3=((T, D), BF),
    p4=((T, D), BF),
    r12=((CH, HALF, D), BF),
    r13=((CH, HALF, D), BF),
    r14=((CH, HALF, D), BF),
    c2=((CH, HALF, D), BF),
    c3=((CH, HALF, D), BF),
    c4=((CH, HALF, D), BF),
    r22=((CH, HALF, D), BF),
    r23=((CH, HALF, D), BF),
    r24=((CH, HALF, D), BF),
    lo=((CH, HALF, D), BF),
    gt=((CH, HALF, D), BF),
    gm=((CH, HALF, D), F32),
    gattn=((T, D), BF),
    gmt=((W, BLK), F32),
    dk=((HEADS, T, 2 * HD), F32),
    dv=((HEADS, T, 2 * HD), F32),
    dkx=((W, T), F32),
    dvx=((W, T), F32),
    gproj=((3 * W, T), BF),
    gacc=((2 * W, BLK), F32),
    m0=((D, F), BF),
    m1=((F, D), BF),
    m2=((4 * W, D), BF),
    vec=((8, D), F32),
    vecs=((8, D), F32),
    rvx=((4, 8, D), F32),
    rvy=((4, 8, D), F32),
    rvz=((3, 8, D), F32),
    v1=((8, D), F32),
    v2=((8, D), F32),
    v3=((8, D), F32),
    v4=((8, D), F32),
)
for _s, _w in (("a", D), ("b", D), ("c", D // 2), ("d", D // 2)):
    SCRATCH["rs1" + _s] = ((3, 192, _w), BF)
    SCRATCH["s1" + _s] = ((192, _w), BF)
    SCRATCH["rs2" + _s] = ((3, 48, _w), BF)
    SCRATCH["s2" + _s] = ((48, _w), BF)
    SCRATCH["rz" + _s] = ((48, _w), BF)
    SCRATCH["rr" + _s] = ((192, _w), BF)

NSEM = 192
NLOC = 40


class Wide:
    def __init__(self, k, name, mat, cols, out, first, second):
        self.k, self.s, self.mat, self.cols, self.out = k, k.s, mat, cols, out
        self.name = name
        self.first, self.second = first, second
        self.u, self.t = k.coord(first), k.coord(second)
        self.base = k.sems(3 + 3 + 1 + 3 + 3)
        self.local = k.locals(1)

    def ref(self, what):
        return getattr(self.s, what + self.name)

    def rs1(self, d):
        k = self.k
        q = lax.rem(self.u + d, 4)
        return k.remote(
            self.mat.at[at(q * 192, 192, 192), self.cols],
            self.ref("rs1").at[d - 1],
            self.base + d - 1,
            k.along(self.first, d),
        )

    def rs2(self, d):
        k = self.k
        q = lax.rem(self.t + d, 4)
        return k.remote(
            self.ref("s1").at[at(q * 48, 48, 48)],
            self.ref("rs2").at[d - 1],
            self.base + 3 + d - 1,
            k.along(self.second, d),
        )

    def zz(self):
        return self.k.remote(self.ref("s2"), self.ref("rz"), self.base + 6, self.k.zhi)

    def ag2(self, d):
        piece = self.ref("rr").at[at(self.t * 48, 48, 48)]
        return self.k.remote(piece, piece, self.base + 7 + d - 1, self.k.along(self.second, d))

    def ag1(self, d):
        return self.k.remote(
            self.ref("rr"),
            self.out.at[at(self.u * 192, 192, 192), self.cols],
            self.base + 10 + d - 1,
            self.k.along(self.first, d),
        )

    def own(self):
        return self.k.copy(
            self.ref("rr"), self.out.at[at(self.u * 192, 192, 192), self.cols], self.local
        )

    def step1(self):
        for d in (2, 1, 3):
            self.rs1(d).start()

    def step2(self):
        for d in (1, 2, 3):
            self.rs1(d).wait_recv()
        rs1, s1 = self.ref("rs1"), self.ref("s1")

        def strip(i, c):
            rows = at(i * 48, 48, 48)
            total = self.mat[at(self.u * 192 + i * 48, 48, 48), self.cols].astype(F32)
            for d in range(3):
                total = total + rs1[d, rows, :].astype(F32)
            s1[rows, :] = total.astype(BF)
            return c

        lax.fori_loop(0, 4, strip, 0)
        for d in (2, 1, 3):
            self.rs2(d).start()

    def step3(self):
        for d in (1, 2, 3):
            self.rs2(d).wait_recv()
        total = self.ref("s1")[at(self.t * 48, 48, 48), :].astype(F32)
        for d in range(3):
            total = total + self.ref("rs2")[d].astype(F32)
        self.ref("s2")[...] = total.astype(BF)
        self.zz().start()

    def step4(self):
        self.zz().wait_recv()
        total = self.ref("s2")[...].astype(F32) + self.ref("rz")[...].astype(F32)
        self.ref("rr")[at(self.t * 48, 48, 48), :] = total.astype(BF)
        for d in (2, 1, 3):
            self.ag2(d).start()

    def step5(self):
        for d in (1, 2, 3):
            self.ag2(d).wait_recv()
        for d in (2, 1, 3):
            self.ag1(d).start()
        self.own().start()

    def finish(self):
        for d in (1, 2, 3):
            self.ag1(d).wait_recv()
        self.own().wait()
        for d in (1, 2, 3):
            self.rs1(d).wait_send()
            self.rs2(d).wait_send()
            self.ag2(d).wait_send()
            self.ag1(d).wait_send()
        self.zz().wait_send()


class Narrow:
    def __init__(self, k, part, r1, c, r2, result):
        self.k, self.part, self.r1, self.c, self.r2, self.result = k, part, r1, c, r2, result
        self.base = k.sems(3 * CH)

    def mine(self, b):
        return at(b * BLK + self.k.core * HALF, HALF, HALF)

    def theirs(self, b):
        return at(b * BLK + (1 - self.k.core) * HALF, HALF, HALF)

    def d1(self, b):
        return self.k.remote(
            self.part.at[self.theirs(b)], self.r1.at[b], self.base + b, self.k.mate
        )

    def d2(self, b):
        return self.k.remote(self.c.at[b], self.r2.at[b], self.base + CH + b, self.k.zlo)

    def d3(self, b):
        src, dst = self.result(b, self.mine(b))
        return self.k.remote(src, dst, self.base + 2 * CH + b, self.k.mate)

    def s1(self, b):
        self.d1(b).start()

    def s2(self, b):
        self.d1(b).wait_recv()
        total = self.part[self.mine(b), :].astype(F32) + self.r1[b].astype(F32)
        self.c[b] = total.astype(BF)
        self.d2(b).start()

    def total(self, b):
        return self.c[b].astype(F32) + self.r2[b].astype(F32)

    def finish(self, last=True):
        for b in range(CH):
            self.d1(b).wait_send()
            self.d2(b).wait_send()
            self.d3(b).wait_send()


class Names:
    pass


class Kernel:
    def __init__(self, s, send, recv, loc):
        self.s, self.send, self.recv, self.loc = s, send, recv, loc
        self.nsem = self.nloc = 0
        w = lax.axis_index("wide")
        n = lax.axis_index("narrow")
        self.w, self.n = w, n
        self.x = lax.rem(w, 4)
        self.y = lax.rem(lax.div(w, 4), 4)
        self.z = lax.div(w, 16)
        self.core = lax.rem(n, 2)
        self.n1 = n + 1 - 2 * self.core
        self.n2 = lax.rem(n + 2, 4)
        self.mate = (w, self.n1)
        self.zlo = (w, self.n2)
        self.zhi = (lax.rem(w + 16, 32), n)
        self.side = (lax.rem(w + 16, 32), self.n2)

    def coord(self, axis):
        return self.x if axis == "x" else self.y

    def along(self, axis, d):
        if axis == "x":
            return (self.w - self.x + lax.rem(self.x + d, 4), self.n)
        return (self.w - 4 * self.y + 4 * lax.rem(self.y + d, 4), self.n)

    def sems(self, count):
        self.nsem += count
        assert self.nsem <= NSEM
        return self.nsem - count

    def locals(self, count):
        self.nloc += count
        assert self.nloc <= NLOC
        return self.nloc - count

    def remote(self, src, dst, sem, device):
        return pltpu.make_async_remote_copy(
            src_ref=src,
            dst_ref=dst,
            send_sem=self.send.at[sem],
            recv_sem=self.recv.at[sem],
            device_id=device,
            device_id_type=MESH,
        )

    def copy(self, src, dst, sem):
        return pltpu.make_async_copy(src, dst, self.loc.at[sem])


def kernel(
    x_in,
    dy_in,
    seg_in,
    pad_in,
    wqkv_in,
    qg_in,
    kg_in,
    wo_in,
    up_in,
    dn_in,
    ag_in,
    as_in,
    mg_in,
    ms_in,
    lo_out,
    gt_out,
    gup_out,
    gdn_out,
    g2_out,
    vec_out,
    *scratch,
):
    s = Names()
    for name, ref in zip(SCRATCH, scratch):
        setattr(s, name, ref)
    k = Kernel(s, *scratch[len(SCRATCH) :])
    n, core = k.n, k.core

    own_wo = s.wo.at[at(n * W, W, W)]
    loads = [
        (x_in, s.x),
        (wqkv_in, s.wraw),
        (wo_in, own_wo),
        (up_in, s.up),
        (dn_in, s.dn),
        (dy_in, s.dy),
    ]
    load_sem = k.locals(len(loads))
    loads = [k.copy(src, dst, load_sem + i) for i, (src, dst) in enumerate(loads)]
    for load in loads:
        load.start()
    load_x, load_w, load_wo, load_up, load_dn, load_dy = loads

    barrier = pltpu.get_barrier_semaphore()
    peers = [k.mate, k.zlo, k.zhi, k.side]
    peers += [k.along(axis, d) for axis in "xy" for d in (1, 2, 3)]
    for peer in peers:
        pl.semaphore_signal(barrier, inc=1, device_id=peer, device_id_type=MESH)

    sem = k.sems(3)
    wo_mate = k.remote(own_wo, own_wo, sem, k.mate)
    wo_side = k.remote(own_wo, own_wo, sem + 1, k.side)
    other_wo = s.wo.at[at(k.n2 * W, W, W)]
    wo_pass = k.remote(other_wo, other_wo, sem + 2, k.mate)
    mix_sem = k.sems(3 * CH)

    def mix_mate(b):
        ref = s.mixed.at[at(n * W, W, W), chunk(b)]
        return k.remote(ref, ref, mix_sem + b, k.mate)

    def mix_z(b):
        ref = s.mixed.at[at(n * W, W, W), chunk(b)]
        return k.remote(ref, ref, mix_sem + CH + b, k.zlo)

    def mix_pass(b):
        ref = s.mixed.at[at(k.n2 * W, W, W), chunk(b)]
        return k.remote(ref, ref, mix_sem + 2 * CH + b, k.mate)

    ar2 = Narrow(k, s.p2, s.r12, s.c2, s.r22, lambda b, rows: (s.lo.at[b], lo_out.at[rows]))
    ar3 = Narrow(k, s.p3, s.r13, s.c3, s.r23, lambda b, rows: (s.gattn.at[rows], s.gattn.at[rows]))
    ar4 = Narrow(k, s.p4, s.r14, s.c4, s.r24, lambda b, rows: (s.gt.at[b], gt_out.at[rows]))
    full = pl.ds(0, D)
    wide_a = Wide(k, "a", s.m0, full, gup_out, "x", "y")
    wide_b = Wide(k, "b", s.m1, full, gdn_out, "y", "x")
    wide_c = Wide(k, "c", s.m2, pl.ds(0, D // 2), g2_out, "x", "y")
    wide_d = Wide(k, "d", s.m2, pl.ds(D // 2, D // 2), g2_out, "y", "x")
    vec_sem = k.sems(3 + 3 + 3)
    vec_x = [
        k.remote(s.vecs, s.rvx.at[k.x], vec_sem + d - 1, k.along("x", d)) for d in (1, 2, 3)
    ]
    vec_y = [
        k.remote(s.v1, s.rvy.at[k.y], vec_sem + 3 + d - 1, k.along("y", d)) for d in (1, 2, 3)
    ]
    vec_z = k.remote(s.v2, s.rvz.at[0], vec_sem + 6, k.zhi)
    vec_c = k.remote(s.v3, s.rvz.at[1], vec_sem + 7, k.mate)
    vec_l = k.remote(s.v4, s.rvz.at[2], vec_sem + 8, k.zlo)
    out_sem = k.locals(2 * CH)

    def lo_copy(b):
        return k.copy(s.lo.at[b], lo_out.at[ar2.mine(b)], out_sem + b)

    def gt_copy(b):
        return k.copy(s.gt.at[b], gt_out.at[ar4.mine(b)], out_sem + CH + b)

    s.vec[...] = jnp.zeros_like(s.vec)
    s.gacc[...] = jnp.zeros_like(s.gacc)

    def clear(b, c):
        for h in range(HEADS):
            s.dk[h, chunk(b), :] = jnp.zeros((BLK, 2 * HD), F32)
            s.dv[h, chunk(b), :] = jnp.zeros((BLK, 2 * HD), F32)
        return c

    lax.fori_loop(0, CH, clear, 0)
    s.gcol[0:W, :] = jnp.transpose(jnp.broadcast_to(qg_in[...].reshape(1, W), (128, W)))
    s.gcol[W:, :] = jnp.transpose(jnp.broadcast_to(kg_in[...].reshape(1, W), (128, W)))
    ag = ag_in[...].reshape(1, D)
    ash = as_in[...].reshape(1, D)
    mg = mg_in[...].reshape(1, D)
    msh = ms_in[...].reshape(1, D)
    limit = T - pad_in[0]

    pl.semaphore_wait(barrier, len(peers))
    load_wo.wait()
    wo_side.start()
    wo_mate.start()

    load_w.wait()
    for c in range(3):
        s.wt[c * W : (c + 1) * W, :] = jnp.transpose(s.wraw[c].astype(F32)).astype(BF)
    load_x.wait()

    def gain_col(c, h):
        col = s.gcol[c * W + h * HD : c * W + (h + 1) * HD, :]
        return jnp.concatenate([col, col], axis=1)

    lanes = lax.broadcasted_iota(jnp.int32, (1, BLK), 1)
    subs = lax.broadcasted_iota(jnp.int32, (HD, BLK), 0)

    def padded(b):
        return jnp.where(lanes + b * BLK >= limit, 1.0, 0.0)

    def project(b, c):
        def strip(i, c):
            rows = at(b * BLK + i * HALF, HALF, HALF)
            hat, _ = moments(s.x[rows, :].astype(F32))
            s.normed[rows, :] = (hat * ag + ash).astype(BF)
            return c

        lax.fori_loop(0, 2, strip, 0)
        raw = nt(s.wt[...], s.normed[chunk(b), :])
        s.big0[0 : 3 * W // 3, 0:BLK] = raw[0:W]
        s.big0[0:W, BLK : 2 * BLK] = raw[W : 2 * W]
        s.big0[0:W, 2 * BLK :] = raw[2 * W :]
        seg = seg_in[:, chunk(b)]
        same = jnp.where(subs == seg, 1.0, 0.0)
        same_valid = same * (1.0 - padded(b))
        ones = jnp.where(subs < 2, 1.0, 0.0)
        for h in range(HEADS):
            rows = slice(h * HD, (h + 1) * HD)
            for which in range(2):
                value = s.big0[rows, which * BLK : (which + 1) * BLK]
                centre = value - jnp.mean(value, axis=0, keepdims=True)
                rstd = lax.rsqrt(jnp.mean(centre * centre, axis=0, keepdims=True) + EPS)
                hat = centre * rstd
                s.hat[which * W + h * HD : which * W + (h + 1) * HD, chunk(b)] = hat
                s.rstd[which * HEADS + h, :, chunk(b)] = rstd
                extra = same * BIG if which == 0 else same_valid
                both = jnp.concatenate([hat * gain_col(which, h), extra], axis=0)
                wide_ref, tall_ref = ((s.qta, s.qn), (s.kta, s.kn))[which]
                wide_ref[h, :, chunk(b)] = both.astype(BF)
                tall_ref[h, chunk(b), :] = jnp.transpose(both).astype(BF)
            value = s.big0[rows, 2 * BLK :]
            s.vt[rows, chunk(b)] = value.astype(BF)
            s.vn[h, chunk(b), :] = jnp.transpose(jnp.concatenate([value, ones], axis=0)).astype(BF)
        return c

    lax.fori_loop(0, CH, project, 0)

    wo_side.wait_recv()
    wo_pass.start()

    def window(b):
        return jnp.minimum(jnp.maximum(b - 1, 0), 1) * BLK

    def self_score(b, h):
        query = s.qta[h, 0:HD, chunk(b)].astype(F32)
        key = s.kta[h, 0:HD, chunk(b)].astype(F32)
        return query, key, jnp.sum(query * key, axis=0, keepdims=True) * SC

    def attend(b, c):
        first = window(b)
        pad_row = padded(b)
        for h in range(HEADS):
            rows = slice(h * HD, (h + 1) * HD)
            _, _, own = self_score(b, h)
            total = jnp.exp2(own) * pad_row
            out = s.vt[rows, chunk(b)].astype(F32) * total
            query = s.qta[h, :, chunk(b)]
            for i in range(3):
                keys = at(first + i * BLK, BLK, BLK)
                score = nn(s.kn[h, keys, :], query)
                weight = jnp.exp2(score * SC - SC * BIG)
                total = total + jnp.sum(weight, axis=0, keepdims=True)
                out = out + nn(s.vt[rows, keys], weight.astype(BF))
            out = out / total
            s.lse[h, :, chunk(b)] = jnp.log(total) * 1.4426950408889634
            s.mixf[rows, chunk(b)] = out
            s.mixed[at(n * W + h * HD, HD, HD), chunk(b)] = out.astype(BF)
        mix_z(b).start()
        mix_mate(b).start()
        return c

    lax.fori_loop(0, CH, attend, 0)

    wo_mate.wait_recv()
    wo_pass.wait_recv()
    mix_z(0).wait_recv()
    mix_pass(0).start()
    load_up.wait()
    load_dn.wait()
    load_dy.wait()

    def mlp(b, c):
        mix_mate(b).wait_recv()
        mix_pass(b).wait_recv()
        s.big0[...] = tn(s.mixed[:, chunk(b)], s.wo[...])

        @pl.when(b < CH - 1)
        def _():
            mix_z(b + 1).wait_recv()
            mix_pass(b + 1).start()

        @pl.when(b > 0)
        def _():
            ar3.s2(b - 1)

        def strip(i, c):
            rows = at(b * BLK + i * HALF, HALF, HALF)
            middle = s.x[rows, :].astype(F32) + s.big0[at(i * HALF, HALF, HALF), :]
            s.mid[rows, :] = middle
            hat, _ = moments(middle)
            s.normed2[rows, :] = (hat * mg + msh).astype(BF)
            return c

        lax.fori_loop(0, 2, strip, 0)
        s.big0[...] = nn(s.normed2[chunk(b), :], s.up[...])
        s.big1[...] = nt(s.dy[chunk(b), :], s.dn[...])

        def gelu(i, c):
            rows = at(i * 32, 32, 32)
            pre = s.big0[rows, :]
            square = pre * pre
            tanh = jnp.tanh(pre * (GELU_A + GELU_B * square))
            half = 0.5 + 0.5 * tanh
            slope = half + (0.5 * pre) * (1.0 - tanh * tanh) * (GELU_A + 3.0 * GELU_B * square)
            out = at(b * BLK + i * 32, 32, 32)
            s.active[out, :] = (pre * half).astype(BF)
            s.gpre[out, :] = (s.big1[rows, :] * slope).astype(BF)
            return c

        lax.fori_loop(0, BLK // 32, gelu, 0)
        s.p3[chunk(b), :] = nt(s.gpre[chunk(b), :], s.up[...]).astype(BF)
        ar3.s1(b)
        s.p2[chunk(b), :] = nn(s.active[chunk(b), :], s.dn[...]).astype(BF)
        ar2.s1(b)
        return c

    lax.fori_loop(0, CH, mlp, 0)
    ar3.s2(CH - 1)

    def grad_cols(i, c):
        cols = at(i * 256, 256, 256)
        s.m0[cols, :] = tn(s.normed2[:, cols], s.gpre[...]).astype(BF)
        s.m1[cols, :] = tn(s.active[:, cols], s.dy[...]).astype(BF)
        return c

    lax.fori_loop(0, 3, grad_cols, 0)
    wide_a.step1()
    wide_b.step1()

    def second_back(b):
        ar3.d2(b).wait_recv()
        total = ar3.total(b)
        hat, rstd = moments(s.mid[ar3.mine(b), :])
        s.vec[2:3, :] += 0.5 * jnp.sum(total * hat, axis=0, keepdims=True)
        s.vec[3:4, :] += 0.5 * jnp.sum(total, axis=0, keepdims=True)
        grad = s.dy[ar3.mine(b), :].astype(F32) + norm_back(total * mg, hat, rstd)
        s.gm[b] = grad
        s.gattn[ar3.mine(b), :] = grad.astype(BF)
        ar3.d3(b).start()

    def head_back(grad, which, h, b):
        rows = slice(which * W + h * HD, which * W + (h + 1) * HD)
        hat = s.hat[rows, chunk(b)]
        s.gacc[rows, :] += grad * hat
        grad = grad * gain_col(which, h)
        grad = (
            grad
            - jnp.mean(grad, axis=0, keepdims=True)
            - hat * jnp.mean(grad * hat, axis=0, keepdims=True)
        )
        s.gproj[rows, chunk(b)] = (grad * s.rstd[which * HEADS + h, :, chunk(b)]).astype(BF)

    def attend_back(b):
        ar3.d3(b).wait_recv()
        s.gmt[...] = nt(s.wo[at(n * W, W, W), :], s.gattn[chunk(b), :])
        first = window(b)
        pad_row = padded(b)
        for h in range(HEADS):
            rows = slice(h * HD, (h + 1) * HD)
            grad_out = s.gmt[rows, :].astype(BF).astype(F32)
            delta = jnp.sum(grad_out * s.mixf[rows, chunk(b)], axis=0, keepdims=True)
            high = delta.astype(BF).astype(F32)
            extra = jnp.where(subs == 0, -high, jnp.where(subs == 1, high - delta, 0.0))
            both = jnp.concatenate([grad_out, extra], axis=0)
            grad_wide = both.astype(BF)
            grad_tall = jnp.transpose(both).astype(BF)
            lse = s.lse[h, :, chunk(b)]
            query = s.qta[h, :, chunk(b)]
            query_tall = s.qn[h, chunk(b), :]
            shift = lse + SC * BIG
            qf, kf, own = self_score(b, h)
            own_prob = jnp.exp2(own - lse) * pad_row
            own_grad = jnp.sum(grad_out * s.vt[rows, chunk(b)].astype(F32), axis=0, keepdims=True)
            own_score = own_prob * (own_grad - delta)
            s.dkx[rows, chunk(b)] = qf * own_score
            s.dvx[rows, chunk(b)] = grad_out * own_prob
            grad_query = kf * own_score
            for i in range(3):
                keys = at(first + i * BLK, BLK, BLK)
                score = nn(s.kn[h, keys, :], query)
                prob = jnp.exp2(score * SC - shift)
                grad_score = (prob * nn(s.vn[h, keys, :], grad_wide)).astype(BF)
                s.dv[h, keys, :] += nn(prob.astype(BF), grad_tall)
                s.dk[h, keys, :] += nn(grad_score, query_tall)
                grad_query = grad_query + nn(s.kta[h, 0:HD, keys], grad_score)
            head_back(grad_query * 0.125, 0, h, b)

    def first_part(b):
        for h in range(HEADS):
            rows = slice(h * HD, (h + 1) * HD)
            grad_key = jnp.transpose(s.dk[h, chunk(b), :])[0:HD, :] + s.dkx[rows, chunk(b)]
            head_back(grad_key * 0.125, 1, h, b)
            grad_value = jnp.transpose(s.dv[h, chunk(b), :])[0:HD, :] + s.dvx[rows, chunk(b)]
            s.gproj[2 * W + h * HD : 2 * W + (h + 1) * HD, chunk(b)] = grad_value.astype(BF)
        s.big0[...] = tn(s.gproj[:, chunk(b)], s.wt[...])

        def strip(i, c):
            rows = at(b * BLK + i * HALF, HALF, HALF)
            part = s.big0[at(i * HALF, HALF, HALF), :]
            s.p4[rows, :] = part.astype(BF)
            hat, _ = moments(s.x[rows, :].astype(F32))
            s.vec[0:1, :] += jnp.sum(part * hat, axis=0, keepdims=True)
            s.vec[1:2, :] += jnp.sum(part, axis=0, keepdims=True)
            return c

        lax.fori_loop(0, 2, strip, 0)
        ar4.s1(b)

    def back(b, c):
        @pl.when(b < CH)
        def _():
            second_back(b)

        @pl.when(b >= 1)
        def _():
            ar2.s2(b - 1)

        @pl.when(b >= 2)
        def _():
            ar4.s2(b - 2)

        @pl.when(b < CH)
        def _():
            attend_back(b)

        @pl.when(b >= 1)
        def _():
            first_part(b - 1)

        return c

    lax.fori_loop(0, CH + 1, back, 0)
    wide_a.step2()
    wide_b.step2()
    ar4.s2(CH - 1)

    def grad_rows(i, c):
        rows = at(i * 192, 192, 192)
        s.m2[rows, :] = nn(s.gproj[rows, :], s.normed[...]).astype(BF)
        return c

    lax.fori_loop(0, 3, grad_rows, 0)
    s.m2[3 * W :, :] = nn(s.mixed[at(n * W, W, W), :], s.gattn[...]).astype(BF)
    wide_c.step1()
    wide_d.step1()
    for which in range(2):
        rows = slice(which * W, (which + 1) * W)
        both = s.gacc[rows, 0:128] + s.gacc[rows, 128:256]
        s.vec[4 + which : 5 + which, 0:W] = jnp.sum(jnp.transpose(both), axis=0, keepdims=True)
    s.vecs[...] = s.vec[...]
    s.rvx[k.x] = s.vec[...]
    for copy in vec_x:
        copy.start()

    def layer_out(b):
        ar2.d2(b).wait_recv()
        s.lo[b] = (s.mid[ar2.mine(b), :] + ar2.total(b)).astype(BF)
        ar2.d3(b).start()
        lo_copy(b).start()

    def grad_tokens(b):
        ar4.d2(b).wait_recv()
        hat, rstd = moments(s.x[ar4.mine(b), :].astype(F32))
        s.gt[b] = (s.gm[b] + norm_back(ar4.total(b) * ag, hat, rstd)).astype(BF)
        ar4.d3(b).start()
        gt_copy(b).start()

    layer_out(0)
    wide_a.step3()
    wide_b.step3()
    layer_out(1)
    wide_a.step4()
    wide_b.step4()
    layer_out(2)
    wide_a.step5()
    wide_b.step5()
    layer_out(3)
    grad_tokens(0)
    wide_c.step2()
    wide_d.step2()
    for copy in vec_x:
        copy.wait_recv()
    s.v1[...] = (s.rvx[0] + s.rvx[1]) + (s.rvx[2] + s.rvx[3])
    s.rvy[k.y] = s.v1[...]
    for copy in vec_y:
        copy.start()
    grad_tokens(1)
    wide_c.step3()
    wide_d.step3()
    for copy in vec_y:
        copy.wait_recv()
    s.v2[...] = (s.rvy[0] + s.rvy[1]) + (s.rvy[2] + s.rvy[3])
    vec_z.start()
    grad_tokens(2)
    wide_c.step4()
    wide_d.step4()
    vec_z.wait_recv()
    s.v3[...] = s.v2[...] + s.rvz[0]
    vec_c.start()
    grad_tokens(3)
    wide_c.step5()
    wide_d.step5()
    upper = lax.broadcasted_iota(jnp.int32, (8, D), 0) < 4
    vec_c.wait_recv()
    s.v4[...] = s.v3[...] + jnp.where(upper, s.rvz[1], 0.0)
    vec_l.start()
    vec_l.wait_recv()
    vec_out[...] = s.v4[...] + jnp.where(upper, s.rvz[2], 0.0)

    for b in range(CH):
        ar2.d3(b).wait_recv()
        ar4.d3(b).wait_recv()
        lo_copy(b).wait()
        gt_copy(b).wait()
        mix_mate(b).wait_send()
        mix_z(b).wait_send()
        mix_pass(b).wait_send()
    for item in (ar2, ar3, ar4, wide_a, wide_b, wide_c, wide_d):
        item.finish()
    for copy in [wo_mate, wo_side, wo_pass, *vec_x, *vec_y, vec_z, vec_c, vec_l]:
        copy.wait_send()


def body(*args):
    any_spec = pl.BlockSpec(memory_space=pl.ANY)
    vmem = pl.BlockSpec(memory_space=pltpu.VMEM)
    smem = pl.BlockSpec(memory_space=pltpu.SMEM)
    out = pl.pallas_call(
        kernel,
        out_shape=(
            jax.ShapeDtypeStruct((T, D), BF),
            jax.ShapeDtypeStruct((T, D), BF),
            jax.ShapeDtypeStruct((D, F), BF),
            jax.ShapeDtypeStruct((F, D), BF),
            jax.ShapeDtypeStruct((4 * W, D), BF),
            jax.ShapeDtypeStruct((8, D), F32),
        ),
        in_specs=[
            any_spec,
            any_spec,
            vmem,
            smem,
            any_spec,
            vmem,
            vmem,
            any_spec,
            any_spec,
            any_spec,
            vmem,
            vmem,
            vmem,
            vmem,
        ],
        out_specs=(any_spec, any_spec, any_spec, any_spec, any_spec, vmem),
        scratch_shapes=[pltpu.VMEM(shape, dtype) for shape, dtype in SCRATCH.values()]
        + [
            pltpu.SemaphoreType.DMA((NSEM,)),
            pltpu.SemaphoreType.DMA((NSEM,)),
            pltpu.SemaphoreType.DMA((NLOC,)),
        ],
        compiler_params=pltpu.CompilerParams(
            collective_id=0, has_side_effects=True, vmem_limit_bytes=60 * 1024 * 1024
        ),
        cost_estimate=pl.CostEstimate(
            flops=14 * 10**9, bytes_accessed=20 * 2**20, transcendentals=8 * 2**20
        ),
    )(*args)
    layer, grad_tokens, grad_up, grad_down, rest, vec = out
    grad_qkv = jnp.swapaxes(rest[: 3 * W].reshape(3, W, D), 1, 2).astype(F32)
    return (
        layer,
        grad_tokens,
        grad_qkv,
        vec[4, :W],
        vec[5, :W],
        rest[3 * W :].astype(F32),
        grad_up.astype(F32),
        grad_down.astype(F32),
        vec[0],
        vec[1],
        vec[2],
        vec[3],
    )


def solution(mesh):
    placed = (
        P("wide", None),
        P("wide", None),
        P("wide", None),
        P("wide"),
        P(None, None, "narrow"),
        P("narrow"),
        P("narrow"),
        P("narrow", None),
        P(None, "narrow"),
        P("narrow", None),
        P(),
        P(),
        P(),
        P(),
    )
    return jax.shard_map(
        body,
        mesh=mesh,
        in_specs=placed,
        out_specs=(
            P("wide", None),
            P("wide", None),
            P(None, None, "narrow"),
            P("narrow"),
            P("narrow"),
            P("narrow", None),
            P(None, "narrow"),
            P("narrow", None),
            P(),
            P(),
            P(),
            P(),
        ),
        check_vma=False,
    )
```

```python
import jax
import jax.numpy as jnp
from jax import lax
from jax.experimental import pallas as pl
from jax.experimental.pallas import tpu as pltpu
from jax.sharding import PartitionSpec as P

T = 1024
D = 768
HEADS = 3
HD = 64
W = HEADS * HD
F = 768
BLK = 256
CH = T // BLK
HALF = BLK // 2
BIG = 512.0
MINUS, LSE = 31, 28
LOG2E = 1.4426950408889634
SC = 0.125 * LOG2E
EPS = 1e-06
GELU_A = 0.7978845608028654
GELU_B = 0.044715 * GELU_A

BF = jnp.bfloat16
F32 = jnp.float32
MESH = pl.DeviceIdType.MESH


def nn(a, b):
    return lax.dot_general(a, b, (((1,), (0,)), ((), ())), preferred_element_type=F32)


def nt(a, b):
    return lax.dot_general(a, b, (((1,), (1,)), ((), ())), preferred_element_type=F32)


def tn(a, b):
    return lax.dot_general(a, b, (((0,), (0,)), ((), ())), preferred_element_type=F32)


def at(start, size, unit):
    return pl.ds(pl.multiple_of(start, unit), size)


def chunk(b):
    return at(b * BLK, BLK, BLK)


def moments(values):
    centre = values - jnp.mean(values, axis=-1, keepdims=True)
    rstd = lax.rsqrt(jnp.mean(centre * centre, axis=-1, keepdims=True) + EPS)
    return centre * rstd, rstd


def norm_back(grad, hat, rstd):
    return rstd * (
        grad
        - jnp.mean(grad, axis=-1, keepdims=True)
        - hat * jnp.mean(grad * hat, axis=-1, keepdims=True)
    )


SCRATCH = dict(
    x=((T, D), BF),
    dy=((T, D), BF),
    wt=((3 * W, D), BF),
    wo=((4 * W, D), BF),
    up=((D, F), BF),
    dn=((F, D), BF),
    normed=((T, D), BF),
    qta=((HEADS, 2 * HD, T), BF),
    kta=((HEADS, 2 * HD, T), BF),
    vt=((W, T), BF),
    qn=((HEADS, T, 2 * HD), BF),
    kn=((HEADS, T, 2 * HD), BF),
    vn=((HEADS, T, 2 * HD), BF),
    hat=((2 * W, T), F32),
    rstd=((6, 1, T), F32),
    gcol=((2 * W, 128), F32),
    mixed=((4 * W, T), BF),
    mixf=((W, T), F32),
    mid=((T, D), F32),
    normed2=((T, D), BF),
    active=((T, F), BF),
    gpre=((T, F), BF),
    big0=((BLK, D), F32),
    gact=((T, F), F32),
    big1=((BLK, D), F32),
    p2=((T, D), BF),
    p3=((T, D), BF),
    p4=((T, D), BF),
    r12=((CH, HALF, D), BF),
    r13=((CH, HALF, D), BF),
    r14=((CH, HALF, D), BF),
    c2=((CH, HALF, D), BF),
    c3=((CH, HALF, D), BF),
    c4=((CH, HALF, D), BF),
    r22=((CH, HALF, D), BF),
    r23=((CH, HALF, D), BF),
    r24=((CH, HALF, D), BF),
    lo=((CH, HALF, D), BF),
    gt=((CH, HALF, D), BF),
    gm=((CH, HALF, D), F32),
    gattn=((T, D), BF),
    gmt=((W, BLK), F32),
    dk=((HEADS, T, 2 * HD), F32),
    dv=((HEADS, T, 2 * HD), F32),
    dkx=((W, T), F32),
    dvx=((W, T), F32),
    gproj=((3 * W, T), BF),
    gacc=((2 * W, BLK), F32),
    m0=((D, F), BF),
    m1=((F, D), BF),
    m2=((4 * W, D), BF),
    vec=((8, D), F32),
    vecs=((8, D), F32),
    rvx=((4, 8, D), F32),
    rvy=((4, 8, D), F32),
    rvz=((3, 8, D), F32),
    v1=((8, D), F32),
    v2=((8, D), F32),
    v3=((8, D), F32),
    v4=((8, D), F32),
)
for _s, _w in (("a", D), ("b", D), ("c", D // 2), ("d", D // 2)):
    SCRATCH["rs1" + _s] = ((3, 192, _w), BF)
    SCRATCH["s1" + _s] = ((192, _w), BF)
    SCRATCH["rs2" + _s] = ((3, 48, _w), BF)
    SCRATCH["s2" + _s] = ((48, _w), BF)
    SCRATCH["rz" + _s] = ((48, _w), BF)
    SCRATCH["rr" + _s] = ((192, _w), BF)

NSEM = 192
NLOC = 40


class Wide:
    def __init__(self, k, name, mat, cols, out, first, second):
        self.k, self.s, self.mat, self.cols, self.out = k, k.s, mat, cols, out
        self.name = name
        self.first, self.second = first, second
        self.u, self.t = k.coord(first), k.coord(second)
        self.base = k.sems(3 + 3 + 1 + 3 + 3)
        self.local = k.locals(1)

    def ref(self, what):
        return getattr(self.s, what + self.name)

    def rs1(self, d):
        k = self.k
        q = lax.rem(self.u + d, 4)
        return k.remote(
            self.mat.at[at(q * 192, 192, 192), self.cols],
            self.ref("rs1").at[d - 1],
            self.base + d - 1,
            k.along(self.first, d),
        )

    def rs2(self, d):
        k = self.k
        q = lax.rem(self.t + d, 4)
        return k.remote(
            self.ref("s1").at[at(q * 48, 48, 48)],
            self.ref("rs2").at[d - 1],
            self.base + 3 + d - 1,
            k.along(self.second, d),
        )

    def zz(self):
        return self.k.remote(self.ref("s2"), self.ref("rz"), self.base + 6, self.k.zhi)

    def ag2(self, d):
        piece = self.ref("rr").at[at(self.t * 48, 48, 48)]
        return self.k.remote(piece, piece, self.base + 7 + d - 1, self.k.along(self.second, d))

    def ag1(self, d):
        return self.k.remote(
            self.ref("rr"),
            self.out.at[at(self.u * 192, 192, 192), self.cols],
            self.base + 10 + d - 1,
            self.k.along(self.first, d),
        )

    def own(self):
        return self.k.copy(
            self.ref("rr"), self.out.at[at(self.u * 192, 192, 192), self.cols], self.local
        )

    def step1(self):
        for d in (2, 1, 3):
            self.rs1(d).start()

    def step2(self):
        for d in (1, 2, 3):
            self.rs1(d).wait_recv()
        rs1, s1 = self.ref("rs1"), self.ref("s1")

        def strip(i, c):
            rows = at(i * 48, 48, 48)
            total = self.mat[at(self.u * 192 + i * 48, 48, 48), self.cols].astype(F32)
            for d in range(3):
                total = total + rs1[d, rows, :].astype(F32)
            s1[rows, :] = total.astype(BF)
            return c

        lax.fori_loop(0, 4, strip, 0)
        for d in (2, 1, 3):
            self.rs2(d).start()

    def step3(self):
        for d in (1, 2, 3):
            self.rs2(d).wait_recv()
        total = self.ref("s1")[at(self.t * 48, 48, 48), :].astype(F32)
        for d in range(3):
            total = total + self.ref("rs2")[d].astype(F32)
        self.ref("s2")[...] = total.astype(BF)
        self.zz().start()

    def step4(self):
        self.zz().wait_recv()
        total = self.ref("s2")[...].astype(F32) + self.ref("rz")[...].astype(F32)
        self.ref("rr")[at(self.t * 48, 48, 48), :] = total.astype(BF)
        for d in (2, 1, 3):
            self.ag2(d).start()

    def step5(self):
        for d in (1, 2, 3):
            self.ag2(d).wait_recv()
        for d in (2, 1, 3):
            self.ag1(d).start()
        self.own().start()

    def finish(self):
        for d in (1, 2, 3):
            self.ag1(d).wait_recv()
        self.own().wait()
        for d in (1, 2, 3):
            self.rs1(d).wait_send()
            self.rs2(d).wait_send()
            self.ag2(d).wait_send()
            self.ag1(d).wait_send()
        self.zz().wait_send()


class Narrow:
    def __init__(self, k, part, r1, c, r2, result):
        self.k, self.part, self.r1, self.c, self.r2, self.result = k, part, r1, c, r2, result
        self.base = k.sems(3 * CH)

    def mine(self, b):
        return at(b * BLK + self.k.core * HALF, HALF, HALF)

    def theirs(self, b):
        return at(b * BLK + (1 - self.k.core) * HALF, HALF, HALF)

    def d1(self, b):
        return self.k.remote(
            self.part.at[self.theirs(b)], self.r1.at[b], self.base + b, self.k.mate
        )

    def d2(self, b):
        return self.k.remote(self.c.at[b], self.r2.at[b], self.base + CH + b, self.k.zlo)

    def d3(self, b):
        src, dst = self.result(b, self.mine(b))
        return self.k.remote(src, dst, self.base + 2 * CH + b, self.k.mate)

    def s1(self, b):
        self.d1(b).start()

    def s2(self, b):
        self.d1(b).wait_recv()
        total = self.part[self.mine(b), :].astype(F32) + self.r1[b].astype(F32)
        self.c[b] = total.astype(BF)
        self.d2(b).start()

    def total(self, b):
        return self.c[b].astype(F32) + self.r2[b].astype(F32)

    def finish(self, last=True):
        for b in range(CH):
            self.d1(b).wait_send()
            self.d2(b).wait_send()
            self.d3(b).wait_send()


class Names:
    pass


class Kernel:
    def __init__(self, s, send, recv, loc):
        self.s, self.send, self.recv, self.loc = s, send, recv, loc
        self.nsem = self.nloc = 0
        w = lax.axis_index("wide")
        n = lax.axis_index("narrow")
        self.w, self.n = w, n
        self.x = lax.rem(w, 4)
        self.y = lax.rem(lax.div(w, 4), 4)
        self.z = lax.div(w, 16)
        self.core = lax.rem(n, 2)
        self.n1 = n + 1 - 2 * self.core
        self.n2 = lax.rem(n + 2, 4)
        self.mate = (w, self.n1)
        self.zlo = (w, self.n2)
        self.zhi = (lax.rem(w + 16, 32), n)
        self.side = (lax.rem(w + 16, 32), self.n2)

    def coord(self, axis):
        return self.x if axis == "x" else self.y

    def along(self, axis, d):
        if axis == "x":
            return (self.w - self.x + lax.rem(self.x + d, 4), self.n)
        return (self.w - 4 * self.y + 4 * lax.rem(self.y + d, 4), self.n)

    def sems(self, count):
        self.nsem += count
        assert self.nsem <= NSEM
        return self.nsem - count

    def locals(self, count):
        self.nloc += count
        assert self.nloc <= NLOC
        return self.nloc - count

    def remote(self, src, dst, sem, device):
        return pltpu.make_async_remote_copy(
            src_ref=src,
            dst_ref=dst,
            send_sem=self.send.at[sem],
            recv_sem=self.recv.at[sem],
            device_id=device,
            device_id_type=MESH,
        )

    def copy(self, src, dst, sem):
        return pltpu.make_async_copy(src, dst, self.loc.at[sem])


def kernel(
    x_in,
    dy_in,
    seg_in,
    pad_in,
    wt_in,
    qg_in,
    kg_in,
    wo_in,
    up_in,
    dn_in,
    ag_in,
    as_in,
    mg_in,
    ms_in,
    lo_out,
    gt_out,
    gup_out,
    gdn_out,
    g2_out,
    vec_out,
    *scratch,
):
    s = Names()
    for name, ref in zip(SCRATCH, scratch):
        setattr(s, name, ref)
    k = Kernel(s, *scratch[len(SCRATCH) :])
    n, core = k.n, k.core

    own_wo = s.wo.at[at(n * W, W, W)]
    loads = [
        (x_in, s.x),
        (wt_in, s.wt),
        (wo_in, own_wo),
        (up_in, s.up),
        (dn_in, s.dn),
        (dy_in, s.dy),
    ]
    load_sem = k.locals(len(loads))
    loads = [k.copy(src, dst, load_sem + i) for i, (src, dst) in enumerate(loads)]
    for load in loads:
        load.start()
    load_x, load_w, load_wo, load_up, load_dn, load_dy = loads

    barrier = pltpu.get_barrier_semaphore()
    peers = [k.mate, k.zlo, k.zhi, k.side]
    peers += [k.along(axis, d) for axis in "xy" for d in (1, 2, 3)]
    for peer in peers:
        pl.semaphore_signal(barrier, inc=1, device_id=peer, device_id_type=MESH)

    sem = k.sems(4)
    own_low = s.wo.at[at(n * W, W // 2, W // 2)]
    own_high = s.wo.at[at(n * W + W // 2, W // 2, W // 2)]
    other_wo = s.wo.at[at(k.n2 * W, W, W)]
    wo_sends = [
        k.remote(own_wo, own_wo, sem, k.mate),
        k.remote(own_low, own_low, sem + 1, k.zlo),
        k.remote(own_high, own_high, sem + 2, k.side),
    ]
    wo_pass = k.remote(other_wo, other_wo, sem + 3, k.mate)
    mix_sem = k.sems(3 * CH)

    def mix_mate(b):
        ref = s.mixed.at[at(n * W, W, W), chunk(b)]
        return k.remote(ref, ref, mix_sem + b, k.mate)

    def mix_z(b):
        ref = s.mixed.at[at(n * W, W, W), chunk(b)]
        return k.remote(ref, ref, mix_sem + CH + b, k.zlo)

    def mix_pass(b):
        ref = s.mixed.at[at(k.n2 * W, W, W), chunk(b)]
        return k.remote(ref, ref, mix_sem + 2 * CH + b, k.mate)

    ar2 = Narrow(k, s.p2, s.r12, s.c2, s.r22, lambda b, rows: (s.lo.at[b], lo_out.at[rows]))
    ar3 = Narrow(k, s.p3, s.r13, s.c3, s.r23, lambda b, rows: (s.gattn.at[rows], s.gattn.at[rows]))
    ar4 = Narrow(k, s.p4, s.r14, s.c4, s.r24, lambda b, rows: (s.gt.at[b], gt_out.at[rows]))
    full = pl.ds(0, D)
    wide_a = Wide(k, "a", s.m0, full, gup_out, "x", "y")
    wide_b = Wide(k, "b", s.m1, full, gdn_out, "y", "x")
    wide_c = Wide(k, "c", s.m2, pl.ds(0, D // 2), g2_out, "x", "y")
    wide_d = Wide(k, "d", s.m2, pl.ds(D // 2, D // 2), g2_out, "y", "x")
    vec_sem = k.sems(3 + 3 + 3)
    vec_x = [
        k.remote(s.vecs, s.rvx.at[k.x], vec_sem + d - 1, k.along("x", d)) for d in (1, 2, 3)
    ]
    vec_y = [
        k.remote(s.v1, s.rvy.at[k.y], vec_sem + 3 + d - 1, k.along("y", d)) for d in (1, 2, 3)
    ]
    vec_z = k.remote(s.v2, s.rvz.at[0], vec_sem + 6, k.zhi)
    vec_c = k.remote(s.v3, s.rvz.at[1], vec_sem + 7, k.mate)
    vec_l = k.remote(s.v4, s.rvz.at[2], vec_sem + 8, k.zlo)
    out_sem = k.locals(2 * CH)

    def lo_copy(b):
        return k.copy(s.lo.at[b], lo_out.at[ar2.mine(b)], out_sem + b)

    def gt_copy(b):
        return k.copy(s.gt.at[b], gt_out.at[ar4.mine(b)], out_sem + CH + b)

    s.vec[...] = jnp.zeros_like(s.vec)
    s.gacc[...] = jnp.zeros_like(s.gacc)

    def clear(b, c):
        for h in range(HEADS):
            s.dk[h, chunk(b), :] = jnp.zeros((BLK, 2 * HD), F32)
            s.dv[h, chunk(b), :] = jnp.zeros((BLK, 2 * HD), F32)
        return c

    lax.fori_loop(0, CH, clear, 0)
    s.gcol[0:W, :] = jnp.transpose(jnp.broadcast_to(qg_in[...].reshape(1, W), (128, W)))
    s.gcol[W:, :] = jnp.transpose(jnp.broadcast_to(kg_in[...].reshape(1, W), (128, W)))
    ag = ag_in[...].reshape(1, D)
    ash = as_in[...].reshape(1, D)
    mg = mg_in[...].reshape(1, D)
    msh = ms_in[...].reshape(1, D)
    limit = T - pad_in[0]

    load_x.wait()
    load_w.wait()

    def gain_col(c, h):
        col = s.gcol[c * W + h * HD : c * W + (h + 1) * HD, :]
        return jnp.concatenate([col, col], axis=1)

    lanes = lax.broadcasted_iota(jnp.int32, (1, BLK), 1)
    subs = lax.broadcasted_iota(jnp.int32, (HD, BLK), 0)

    def padded(b):
        return jnp.where(lanes + b * BLK >= limit, 1.0, 0.0)

    def project(b, c):
        def strip(i, c):
            rows = at(b * BLK + i * HALF, HALF, HALF)
            hat, _ = moments(s.x[rows, :].astype(F32))
            s.normed[rows, :] = (hat * ag + ash).astype(BF)
            return c

        lax.fori_loop(0, 2, strip, 0)
        raw = nt(s.wt[...], s.normed[chunk(b), :])
        for which in range(3):
            s.big0[0:W, which * BLK : (which + 1) * BLK] = raw[which * W : (which + 1) * W]
        same = jnp.where(subs == seg_in[:, chunk(b)], 1.0, 0.0)
        same_valid = same * (1.0 - padded(b))
        query_rows = jnp.where(subs == MINUS, -BIG, BIG * same)
        key_rows = jnp.where((subs >= LSE) & (subs <= MINUS), 1.0, same_valid)
        ones = jnp.where(subs < 2, 1.0, 0.0)
        for h in range(HEADS):
            rows = slice(h * HD, (h + 1) * HD)
            for which in range(2):
                value = s.big0[rows, which * BLK : (which + 1) * BLK]
                centre = value - jnp.mean(value, axis=0, keepdims=True)
                rstd = lax.rsqrt(jnp.mean(centre * centre, axis=0, keepdims=True) + EPS)
                hat = centre * rstd
                s.hat[which * W + h * HD : which * W + (h + 1) * HD, chunk(b)] = hat
                s.rstd[which * HEADS + h, :, chunk(b)] = rstd
                extra = (query_rows, key_rows)[which]
                value = hat * gain_col(which, h) * (1.0, SC)[which]
                both = jnp.concatenate([value, extra], axis=0)
                wide_ref, tall_ref = ((s.qta, s.qn), (s.kta, s.kn))[which]
                wide_ref[h, :, chunk(b)] = both.astype(BF)
                tall_ref[h, chunk(b), :] = jnp.transpose(both).astype(BF)
            value = s.big0[rows, 2 * BLK :]
            s.vt[rows, chunk(b)] = value.astype(BF)
            s.vn[h, chunk(b), :] = jnp.transpose(jnp.concatenate([value, ones], axis=0)).astype(BF)
        return c

    lax.fori_loop(0, CH, project, 0)

    def window(b):
        if isinstance(b, int):
            return range(max(b - 1, 0), min(b + 2, CH))
        return [b - 1, b, b + 1]

    def self_score(b, h):
        query = s.qta[h, 0:HD, chunk(b)].astype(F32)
        key = s.kta[h, 0:HD, chunk(b)].astype(F32)
        return query, key, jnp.sum(query * key, axis=0, keepdims=True)

    def attend(b):
        pad_row = padded(b)
        same = jnp.where(subs == MINUS, -BIG, jnp.where(subs == seg_in[:, chunk(b)], BIG, 0.0))
        for h in range(HEADS):
            rows = slice(h * HD, (h + 1) * HD)
            _, _, own = self_score(b, h)
            total = jnp.exp2(own) * pad_row
            out = s.vt[rows, chunk(b)].astype(F32) * total
            query = s.qta[h, :, chunk(b)]
            for i in window(b):
                weight = jnp.exp2(nn(s.kn[h, chunk(i), :], query))
                total = total + jnp.sum(weight, axis=0, keepdims=True)
                out = out + nn(s.vt[rows, chunk(i)], weight.astype(BF))
            out = out / total
            s.mixf[rows, chunk(b)] = out
            s.mixed[at(n * W + h * HD, HD, HD), chunk(b)] = out.astype(BF)
            lse = jnp.log(total) * -LOG2E
            for i in range(3):
                term = lse.astype(BF).astype(F32)
                same = jnp.where(subs == LSE + i, term, same)
                lse = lse - term
            s.qta[h, HD : 2 * HD, chunk(b)] = same.astype(BF)

    def send_mixed(b):
        mix_z(b).start()
        mix_mate(b).start()

    attend(0)
    pl.semaphore_wait(barrier, len(peers))
    load_wo.wait()
    for copy in wo_sends:
        copy.start()
    send_mixed(0)

    def attend_inner(b, c):
        attend(b)
        send_mixed(b)
        return c

    lax.fori_loop(1, CH - 1, attend_inner, 0)
    attend(CH - 1)
    send_mixed(CH - 1)

    load_dy.wait()
    load_dn.wait()
    s.gact[...] = nt(s.dy[...], s.dn[...])
    load_up.wait()
    for copy in wo_sends[1:]:
        copy.wait_recv()
    wo_pass.start()
    mix_z(0).wait_recv()
    mix_pass(0).start()
    wo_sends[0].wait_recv()
    wo_pass.wait_recv()

    def out_product(b):
        mix_mate(b).wait_recv()
        mix_pass(b).wait_recv()
        s.big0[...] = tn(s.mixed[:, chunk(b)], s.wo[...])

    def pass_mixed(b):
        mix_z(b).wait_recv()
        mix_pass(b).start()

    def second_norm(b):
        for i in range(2):
            rows = slice(b * BLK + i * HALF, b * BLK + (i + 1) * HALF)
            middle = s.x[rows, :].astype(F32) + s.big0[i * HALF : (i + 1) * HALF, :]
            s.mid[rows, :] = middle
            hat, _ = moments(middle)
            s.normed2[rows, :] = (hat * mg + msh).astype(BF)

    def gelu(b):
        for i in range(BLK // 32):
            out = slice(b * BLK + i * 32, b * BLK + (i + 1) * 32)
            pre = s.big1[i * 32 : (i + 1) * 32, :]
            square = pre * pre
            tanh = jnp.tanh(pre * (GELU_A + GELU_B * square))
            half = 0.5 + 0.5 * tanh
            slope = half + (0.5 * pre) * (1.0 - tanh * tanh) * (GELU_A + 3.0 * GELU_B * square)
            s.active[out, :] = (pre * half).astype(BF)
            s.gpre[out, :] = (s.gact[out, :] * slope).astype(BF)

    out_product(0)
    pass_mixed(1)
    second_norm(0)
    s.big1[...] = nn(s.normed2[0:BLK, :], s.up[...])
    for b in range(CH):
        rows = slice(b * BLK, (b + 1) * BLK)
        if b + 1 < CH:
            out_product(b + 1)
        gelu(b)
        if b + 2 < CH:
            pass_mixed(b + 2)
        s.p3[rows, :] = nt(s.gpre[rows, :], s.up[...]).astype(BF)
        s.p2[rows, :] = nn(s.active[rows, :], s.dn[...]).astype(BF)
        if b + 1 < CH:
            second_norm(b + 1)
        ar3.s1(b)
        ar2.s1(b)
        if b + 1 < CH:
            after = slice((b + 1) * BLK, (b + 2) * BLK)
            s.big1[...] = nn(s.normed2[after, :], s.up[...])
        ar3.s2(b)

    s.m1[...] = tn(s.active[...], s.dy[...]).astype(BF)
    wide_b.step1()
    s.m0[...] = tn(s.normed2[...], s.gpre[...]).astype(BF)
    wide_a.step1()

    def second_back(b):
        ar3.d2(b).wait_recv()
        total = ar3.total(b)
        hat, rstd = moments(s.mid[ar3.mine(b), :])
        s.vec[2:3, :] += 0.5 * jnp.sum(total * hat, axis=0, keepdims=True)
        s.vec[3:4, :] += 0.5 * jnp.sum(total, axis=0, keepdims=True)
        grad = s.dy[ar3.mine(b), :].astype(F32) + norm_back(total * mg, hat, rstd)
        s.gm[b] = grad
        s.gattn[ar3.mine(b), :] = grad.astype(BF)
        ar3.d3(b).start()

    def head_back(grad, which, h, b):
        rows = slice(which * W + h * HD, which * W + (h + 1) * HD)
        hat = s.hat[rows, chunk(b)]
        s.gacc[rows, :] += grad * hat
        grad = grad * gain_col(which, h)
        grad = (
            grad
            - jnp.mean(grad, axis=0, keepdims=True)
            - hat * jnp.mean(grad * hat, axis=0, keepdims=True)
        )
        s.gproj[rows, chunk(b)] = (grad * s.rstd[which * HEADS + h, :, chunk(b)]).astype(BF)

    def attend_back(b):
        ar3.d3(b).wait_recv()
        s.gmt[...] = nt(s.wo[at(n * W, W, W), :], s.gattn[chunk(b), :])
        pad_row = padded(b)
        for h in range(HEADS):
            rows = slice(h * HD, (h + 1) * HD)
            grad_out = s.gmt[rows, :].astype(BF).astype(F32)
            delta = jnp.sum(grad_out * s.mixf[rows, chunk(b)], axis=0, keepdims=True)
            high = delta.astype(BF).astype(F32)
            extra = jnp.where(subs == 0, -high, jnp.where(subs == 1, high - delta, 0.0))
            both = jnp.concatenate([grad_out, extra], axis=0)
            grad_wide = both.astype(BF)
            grad_tall = jnp.transpose(both).astype(BF)
            query = s.qta[h, :, chunk(b)]
            query_tall = s.qn[h, chunk(b), :]
            qf, kf, own = self_score(b, h)
            shift = jnp.sum(s.qta[h, HD + LSE : HD + MINUS, chunk(b)].astype(F32), axis=0, keepdims=True)
            own_prob = jnp.exp2(own + shift) * pad_row
            own_grad = jnp.sum(grad_out * s.vt[rows, chunk(b)].astype(F32), axis=0, keepdims=True)
            own_score = own_prob * (own_grad - delta)
            s.dkx[rows, chunk(b)] = qf * own_score
            s.dvx[rows, chunk(b)] = grad_out * own_prob
            grad_query = kf * own_score
            for i in window(b):
                prob = jnp.exp2(nn(s.kn[h, chunk(i), :], query))
                grad_score = (prob * nn(s.vn[h, chunk(i), :], grad_wide)).astype(BF)
                s.dv[h, chunk(i), :] += nn(prob.astype(BF), grad_tall)
                s.dk[h, chunk(i), :] += nn(grad_score, query_tall)
                grad_query = grad_query + nn(s.kta[h, 0:HD, chunk(i)], grad_score)
            head_back(grad_query * (0.125 / SC), 0, h, b)

    def first_part(b):
        for h in range(HEADS):
            rows = slice(h * HD, (h + 1) * HD)
            grad_key = jnp.transpose(s.dk[h, chunk(b), :])[0:HD, :] + s.dkx[rows, chunk(b)]
            head_back(grad_key * 0.125, 1, h, b)
            grad_value = jnp.transpose(s.dv[h, chunk(b), :])[0:HD, :] + s.dvx[rows, chunk(b)]
            s.gproj[2 * W + h * HD : 2 * W + (h + 1) * HD, chunk(b)] = grad_value.astype(BF)
        s.big0[...] = tn(s.gproj[:, chunk(b)], s.wt[...])

        def strip(i, c):
            rows = at(b * BLK + i * HALF, HALF, HALF)
            part = s.big0[at(i * HALF, HALF, HALF), :]
            s.p4[rows, :] = part.astype(BF)
            hat, _ = moments(s.x[rows, :].astype(F32))
            s.vec[0:1, :] += jnp.sum(part * hat, axis=0, keepdims=True)
            s.vec[1:2, :] += jnp.sum(part, axis=0, keepdims=True)
            return c

        lax.fori_loop(0, 2, strip, 0)
        ar4.s1(b)

    for b in range(CH):
        second_back(b)
        if b >= 1:
            ar2.s2(b - 1)
        if b >= 2:
            ar4.s2(b - 2)
        if b == 3:
            wide_a.step2()
            wide_b.step2()
        attend_back(b)
        if b >= 1:
            first_part(b - 1)
    first_part(CH - 1)
    s.m2[0 : 3 * W, :] = nn(s.gproj[...], s.normed[...]).astype(BF)
    s.m2[3 * W :, :] = nn(s.mixed[at(n * W, W, W), :], s.gattn[...]).astype(BF)
    wide_c.step1()
    wide_d.step1()
    for which in range(2):
        rows = slice(which * W, (which + 1) * W)
        both = s.gacc[rows, 0:128] + s.gacc[rows, 128:256]
        s.vec[4 + which : 5 + which, 0:W] = jnp.sum(jnp.transpose(both), axis=0, keepdims=True)
    s.vecs[...] = s.vec[...]
    s.rvx[k.x] = s.vec[...]
    for copy in vec_x:
        copy.start()

    def layer_out(b):
        ar2.d2(b).wait_recv()
        s.lo[b] = (s.mid[ar2.mine(b), :] + ar2.total(b)).astype(BF)
        ar2.d3(b).start()
        lo_copy(b).start()

    def grad_tokens(b):
        ar4.d2(b).wait_recv()
        hat, rstd = moments(s.x[ar4.mine(b), :].astype(F32))
        s.gt[b] = (s.gm[b] + norm_back(ar4.total(b) * ag, hat, rstd)).astype(BF)
        ar4.d3(b).start()
        gt_copy(b).start()

    wide_a.step3()
    wide_b.step3()
    ar4.s2(CH - 2)
    layer_out(0)
    layer_out(1)
    wide_a.step4()
    wide_b.step4()
    ar4.s2(CH - 1)
    layer_out(2)
    grad_tokens(0)
    wide_a.step5()
    wide_b.step5()
    wide_c.step2()
    wide_d.step2()
    for copy in vec_x:
        copy.wait_recv()
    s.v1[...] = (s.rvx[0] + s.rvx[1]) + (s.rvx[2] + s.rvx[3])
    s.rvy[k.y] = s.v1[...]
    for copy in vec_y:
        copy.start()
    grad_tokens(1)
    wide_c.step3()
    wide_d.step3()
    for copy in vec_y:
        copy.wait_recv()
    s.v2[...] = (s.rvy[0] + s.rvy[1]) + (s.rvy[2] + s.rvy[3])
    vec_z.start()
    ar2.s2(CH - 1)
    grad_tokens(2)
    wide_c.step4()
    wide_d.step4()
    vec_z.wait_recv()
    s.v3[...] = s.v2[...] + s.rvz[0]
    vec_c.start()
    grad_tokens(3)
    wide_c.step5()
    wide_d.step5()
    upper = lax.broadcasted_iota(jnp.int32, (8, D), 0) < 4
    vec_c.wait_recv()
    s.v4[...] = s.v3[...] + jnp.where(upper, s.rvz[1], 0.0)
    vec_l.start()
    layer_out(3)
    vec_l.wait_recv()
    vec_out[...] = s.v4[...] + jnp.where(upper, s.rvz[2], 0.0)

    for b in range(CH):
        ar2.d3(b).wait_recv()
        ar4.d3(b).wait_recv()
        lo_copy(b).wait()
        gt_copy(b).wait()
        mix_mate(b).wait_send()
        mix_z(b).wait_send()
        mix_pass(b).wait_send()
    for item in (ar2, ar3, ar4, wide_a, wide_b, wide_c, wide_d):
        item.finish()
    for copy in [*wo_sends, wo_pass, *vec_x, *vec_y, vec_z, vec_c, vec_l]:
        copy.wait_send()


PARTS = 4


def finish(lo, gt, gup, gdn, g2, vec, lo_o, gt_o, qkv_o, qg_o, kg_o, out_o, gup_o, gdn_o, ag_o, as_o, mg_o, ms_o, low, high, sem_in, sem_out):
    through = []
    for i, (src, dst) in enumerate(((lo, lo_o), (gt, gt_o))):
        for p in range(PARTS):
            rows = pl.ds(p * (T // PARTS), T // PARTS)
            through.append(pltpu.make_async_copy(src.at[rows], dst.at[rows], sem_out.at[3 + i, p]))
    size = D // PARTS
    loads = {}
    for i, src in enumerate((gup, gdn, g2)):
        for p in range(PARTS):
            rows = pl.ds(p * size, size)
            loads[i, p] = pltpu.make_async_copy(src.at[rows], low.at[i, rows], sem_in.at[i, p])
    for copy in loads.values():
        copy.start()
    for copy in through:
        copy.start()
    for ref, row, count in (
        (ag_o, 0, D),
        (as_o, 1, D),
        (mg_o, 2, D),
        (ms_o, 3, D),
        (qg_o, 4, W),
        (kg_o, 5, W),
    ):
        ref[...] = vec[row : row + 1, 0:count].reshape(count)
    for i in range(3):
        for p in range(PARTS):
            rows = pl.ds(p * size, size)
            loads[i, p].wait()
            high[i, rows, :] = low[i, rows, :].astype(F32)
            if i < 2:
                dst = (gup_o, gdn_o)[i].at[rows]
            else:
                dst = qkv_o.at[p] if p < 3 else out_o
            copy = pltpu.make_async_copy(high.at[i, rows], dst, sem_out.at[i, p])
            copy.start()
            through.append(copy)
    for copy in through:
        copy.wait()


def body(*args):
    any_spec = pl.BlockSpec(memory_space=pl.ANY)
    vmem = pl.BlockSpec(memory_space=pltpu.VMEM)
    smem = pl.BlockSpec(memory_space=pltpu.SMEM)
    args = list(args)
    args[4] = jnp.swapaxes(args[4], 1, 2).reshape(3 * W, D)
    out = pl.pallas_call(
        kernel,
        out_shape=(
            jax.ShapeDtypeStruct((T, D), BF),
            jax.ShapeDtypeStruct((T, D), BF),
            jax.ShapeDtypeStruct((D, F), BF),
            jax.ShapeDtypeStruct((F, D), BF),
            jax.ShapeDtypeStruct((4 * W, D), BF),
            jax.ShapeDtypeStruct((8, D), F32),
        ),
        in_specs=[any_spec, any_spec, vmem, smem, any_spec, vmem, vmem]
        + [any_spec] * 3
        + [vmem] * 4,
        out_specs=(any_spec, any_spec, any_spec, any_spec, any_spec, vmem),
        scratch_shapes=[pltpu.VMEM(shape, dtype) for shape, dtype in SCRATCH.values()]
        + [
            pltpu.SemaphoreType.DMA((NSEM,)),
            pltpu.SemaphoreType.DMA((NSEM,)),
            pltpu.SemaphoreType.DMA((NLOC,)),
        ],
        compiler_params=pltpu.CompilerParams(
            collective_id=0, has_side_effects=True, vmem_limit_bytes=60 * 1024 * 1024
        ),
        cost_estimate=pl.CostEstimate(
            flops=14 * 10**9, bytes_accessed=20 * 2**20, transcendentals=8 * 2**20
        ),
    )(*args)
    layer, tokens, qkv, *rest = pl.pallas_call(
        finish,
        out_shape=(
            jax.ShapeDtypeStruct((T, D), BF),
            jax.ShapeDtypeStruct((T, D), BF),
            jax.ShapeDtypeStruct((3, W, D), F32),
            jax.ShapeDtypeStruct((W,), F32),
            jax.ShapeDtypeStruct((W,), F32),
            jax.ShapeDtypeStruct((W, D), F32),
            jax.ShapeDtypeStruct((D, F), F32),
            jax.ShapeDtypeStruct((F, D), F32),
            jax.ShapeDtypeStruct((D,), F32),
            jax.ShapeDtypeStruct((D,), F32),
            jax.ShapeDtypeStruct((D,), F32),
            jax.ShapeDtypeStruct((D,), F32),
        ),
        in_specs=[any_spec] * 5 + [vmem],
        out_specs=(any_spec, any_spec, any_spec, vmem, vmem, any_spec, any_spec, any_spec)
        + (vmem,) * 4,
        scratch_shapes=[
            pltpu.VMEM((3, D, D), BF),
            pltpu.VMEM((3, D, D), F32),
            pltpu.SemaphoreType.DMA((3, PARTS)),
            pltpu.SemaphoreType.DMA((5, PARTS)),
        ],
        compiler_params=pltpu.CompilerParams(vmem_limit_bytes=32 * 1024 * 1024),
        cost_estimate=pl.CostEstimate(flops=0, bytes_accessed=17 * 2**20, transcendentals=0),
    )(*out)
    return (layer, tokens, jnp.swapaxes(qkv, 1, 2), *rest)


def solution(mesh):
    placed = (
        P("wide", None),
        P("wide", None),
        P("wide", None),
        P("wide"),
        P(None, None, "narrow"),
        P("narrow"),
        P("narrow"),
        P("narrow", None),
        P(None, "narrow"),
        P("narrow", None),
        P(),
        P(),
        P(),
        P(),
    )
    return jax.shard_map(
        body,
        mesh=mesh,
        in_specs=placed,
        out_specs=(
            P("wide", None),
            P("wide", None),
            P(None, None, "narrow"),
            P("narrow"),
            P("narrow"),
            P("narrow", None),
            P(None, "narrow"),
            P("narrow", None),
            P(),
            P(),
            P(),
            P(),
        ),
        check_vma=False,
    )
```

```python
import jax
import jax.numpy as jnp
from jax import lax
from jax.experimental import pallas as pl
from jax.experimental.pallas import tpu as pltpu
from jax.sharding import PartitionSpec as P

T = 1024
D = 768
HEADS = 3
HD = 64
W = HEADS * HD
F = 768
BLK = 256
CH = T // BLK
HALF = BLK // 2
BIG = 512.0
MINUS = 31
LOG2E = 1.4426950408889634
SC = 0.125 * LOG2E
EPS = 1e-06
GELU_A = 0.7978845608028654
GELU_B = 0.044715 * GELU_A

BF = jnp.bfloat16
F32 = jnp.float32
MESH = pl.DeviceIdType.MESH


def nn(a, b):
    return lax.dot_general(a, b, (((1,), (0,)), ((), ())), preferred_element_type=F32)


def nt(a, b):
    return lax.dot_general(a, b, (((1,), (1,)), ((), ())), preferred_element_type=F32)


def tn(a, b):
    return lax.dot_general(a, b, (((0,), (0,)), ((), ())), preferred_element_type=F32)


def at(start, size, unit):
    return pl.ds(pl.multiple_of(start, unit), size)


def chunk(b):
    return at(b * BLK, BLK, BLK)


def moments(values):
    centre = values - jnp.mean(values, axis=-1, keepdims=True)
    rstd = lax.rsqrt(jnp.mean(centre * centre, axis=-1, keepdims=True) + EPS)
    return centre * rstd, rstd


def norm_back(grad, hat, rstd):
    return rstd * (
        grad
        - jnp.mean(grad, axis=-1, keepdims=True)
        - hat * jnp.mean(grad * hat, axis=-1, keepdims=True)
    )


SCRATCH = dict(
    x=((T, D), BF),
    dy=((T, D), BF),
    wt=((3 * W, D), BF),
    wo=((4 * W, D), BF),
    up=((D, F), BF),
    dn=((F, D), BF),
    normed=((T, D), BF),
    hat1=((T, D), BF),
    qta=((HEADS, 2 * HD, T), BF),
    kta=((HEADS, 2 * HD, T), BF),
    vt=((W, T), BF),
    qn=((HEADS, T, 2 * HD), BF),
    kn=((HEADS, T, 2 * HD), BF),
    vn=((HEADS, T, 2 * HD), BF),
    hat=((2 * W, T), F32),
    rstd=((6, 1, T), F32),
    gcol=((2 * W, 128), F32),
    mixed=((4 * W, T), BF),
    mixf=((W, T), F32),
    mid=((CH, HALF, D), F32),
    wgt=((HEADS, 10, BLK, BLK), BF),
    inv=((HEADS, 1, T), F32),
    normed2=((T, D), BF),
    active=((T, F), BF),
    gpre=((T, F), BF),
    big0=((BLK, D), F32),
    gact=((T, F), F32),
    big1=((BLK, D), F32),
    p2=((T, D), BF),
    p3=((T, D), BF),
    p4=((T, D), BF),
    r12=((CH, HALF, D), BF),
    r13=((CH, HALF, D), BF),
    r14=((CH, HALF, D), BF),
    r22=((CH, HALF, D), BF),
    r23=((CH, HALF, D), BF),
    r24=((CH, HALF, D), BF),
    gm=((CH, HALF, D), F32),
    gattn=((T, D), BF),
    dkv=((HEADS, T, 2 * HD), F32),
    dkx=((W, T), F32),
    dvx=((W, T), F32),
    gproj=((3 * W, T), BF),
    gacc=((2 * W, BLK), F32),
    m0=((D, F), BF),
    m1=((F, D), BF),
    m2=((4 * W, D), BF),
    vec=((8, D), F32),
    vecs=((8, D), F32),
    rvx=((4, 8, D), F32),
    rvy=((4, 8, D), F32),
    rvz=((3, 8, D), F32),
    v1=((8, D), F32),
    v2=((8, D), F32),
    v3=((8, D), F32),
    v4=((8, D), F32),
)
RELAYED = "abcd"
for _s, _w in ((_c, D // 2) for _c in "abcdef"):
    SCRATCH["rs1" + _s] = ((3, 192, _w), BF)
    SCRATCH["s1" + _s] = ((192, _w), BF)
    SCRATCH["rs2" + _s] = ((3, 48, _w), BF)
    SCRATCH["s2" + _s] = ((48, _w), BF)
    SCRATCH["rz" + _s] = ((48, _w), BF)
    SCRATCH["rr" + _s] = ((192, _w), BF)
    if _s in RELAYED:
        SCRATCH["nb" + _s] = ((2, 192, _w), BF)

NSEM = 192
NLOC = 48


class Wide:
    def __init__(self, k, name, mat, cols, out, first, second):
        self.k, self.s, self.mat, self.cols, self.out = k, k.s, mat, cols, out
        self.name = name
        self.first, self.second = first, second
        self.u, self.t = k.coord(first), k.coord(second)
        self.base = k.sems(3 + 3 + 1 + 3 + 3 + 2)
        self.local = k.locals(3)
        self.relayed = name in RELAYED

    def ref(self, what):
        return getattr(self.s, what + self.name)

    def rs1(self, d):
        k = self.k
        q = lax.rem(self.u + d, 4)
        return k.remote(
            self.mat.at[at(q * 192, 192, 192), self.cols],
            self.ref("rs1").at[d - 1],
            self.base + d - 1,
            k.along(self.first, d),
        )

    def rs2(self, d):
        k = self.k
        q = lax.rem(self.t + d, 4)
        return k.remote(
            self.ref("s1").at[at(q * 48, 48, 48)],
            self.ref("rs2").at[d - 1],
            self.base + 3 + d - 1,
            k.along(self.second, d),
        )

    def zz(self):
        return self.k.remote(self.ref("s2"), self.ref("rz"), self.base + 6, self.k.zhi)

    def ag2(self, d):
        piece = self.ref("rr").at[at(self.t * 48, 48, 48)]
        return self.k.remote(piece, piece, self.base + 7 + d - 1, self.k.along(self.second, d))

    def rows_out(self, u, start=0, size=192):
        return self.out.at[at(lax.rem(u + 4, 4) * 192 + start, size, 96), self.cols]

    def ag1(self, d):
        if self.relayed:
            dst = self.ref("nb").at[0 if d == 1 else 1]
        else:
            dst = self.rows_out(self.u)
        return self.k.remote(self.ref("rr"), dst, self.base + 10 + d - 1, self.k.along(self.first, d))

    def forward(self, d):
        u, start = (self.u - 1, 0) if d == 1 else (self.u + 1, 96)
        src = self.ref("nb").at[0 if d == 1 else 1, pl.ds(start, 96)]
        return self.k.remote(
            src, self.rows_out(u, start, 96), self.base + 13 + d // 2, self.k.along(self.first, d)
        )

    def own(self, i=0):
        if i == 0:
            return self.k.copy(self.ref("rr"), self.rows_out(self.u), self.local)
        u = self.u - 1 if i == 1 else self.u + 1
        return self.k.copy(self.ref("nb").at[i - 1], self.rows_out(u), self.local + i)

    def step1(self, which=(2, 1, 3)):
        for d in which:
            self.rs1(d).start()

    def step2(self):
        for d in (1, 2, 3):
            self.rs1(d).wait_recv()
        rs1, s1 = self.ref("rs1"), self.ref("s1")

        def strip(i, c):
            rows = at(i * 48, 48, 48)
            total = self.mat[at(self.u * 192 + i * 48, 48, 48), self.cols].astype(F32)
            for d in range(3):
                total = total + rs1[d, rows, :].astype(F32)
            s1[rows, :] = total.astype(BF)
            return c

        lax.fori_loop(0, 4, strip, 0)
        for d in (2, 1, 3):
            self.rs2(d).start()

    def step3(self):
        for d in (1, 2, 3):
            self.rs2(d).wait_recv()
        total = self.ref("s1")[at(self.t * 48, 48, 48), :].astype(F32)
        for d in range(3):
            total = total + self.ref("rs2")[d].astype(F32)
        self.ref("s2")[...] = total.astype(BF)
        self.zz().start()

    def step4(self):
        self.zz().wait_recv()
        total = self.ref("s2")[...].astype(F32) + self.ref("rz")[...].astype(F32)
        self.ref("rr")[at(self.t * 48, 48, 48), :] = total.astype(BF)
        for d in (2, 1, 3):
            self.ag2(d).start()

    def step5(self):
        for d in (1, 2, 3):
            self.ag2(d).wait_recv()
        self.own().start()

    def step6(self, d):
        self.ag1(d).start()

    def step7(self):
        for d in (1, 3):
            self.ag1(d).wait_recv()
            self.forward(d).start()
        for i in (1, 2):
            self.own(i).start()

    def finish(self):
        self.own().wait()
        if self.relayed:
            for d in (1, 3):
                self.forward(d).wait_recv()
                self.forward(d).wait_send()
                self.ag1(d).wait_send()
                self.own(1 + d // 2).wait()
        else:
            for d in (1, 2, 3):
                self.ag1(d).wait_recv()
                self.ag1(d).wait_send()
        for d in (1, 2, 3):
            self.rs1(d).wait_send()
            self.rs2(d).wait_send()
            self.ag2(d).wait_send()
        self.zz().wait_send()


class Narrow:
    def __init__(self, k, part, r1, r2, result):
        self.k, self.part, self.r1, self.r2, self.result = k, part, r1, r2, result
        self.base = k.sems(3 * CH)

    def mine(self, b):
        return at(b * BLK + self.k.core * HALF, HALF, HALF)

    def theirs(self, b):
        return at(b * BLK + (1 - self.k.core) * HALF, HALF, HALF)

    def d1(self, b):
        return self.k.remote(
            self.part.at[self.theirs(b)], self.r1.at[b], self.base + b, self.k.mate
        )

    def d2(self, b):
        return self.k.remote(
            self.part.at[self.mine(b)], self.r2.at[b], self.base + CH + b, self.k.zlo
        )

    def d3(self, b):
        src, dst = self.result(b, self.mine(b))
        return self.k.remote(src, dst, self.base + 2 * CH + b, self.k.mate)

    def s1(self, b):
        self.d1(b).start()

    def s2(self, b):
        self.d1(b).wait_recv()
        total = self.part[self.mine(b), :].astype(F32) + self.r1[b].astype(F32)
        self.part[self.mine(b), :] = total.astype(BF)
        self.d2(b).start()

    def total(self, b):
        return self.part[self.mine(b), :].astype(F32) + self.r2[b].astype(F32)

    def finish(self, last=True):
        for b in range(CH):
            self.d1(b).wait_send()
            self.d2(b).wait_send()
            self.d3(b).wait_send()


class Names:
    pass


class Kernel:
    def __init__(self, s, send, recv, loc):
        self.s, self.send, self.recv, self.loc = s, send, recv, loc
        self.nsem = self.nloc = 0
        w = lax.axis_index("wide")
        n = lax.axis_index("narrow")
        self.w, self.n = w, n
        self.x = lax.rem(w, 4)
        self.y = lax.rem(lax.div(w, 4), 4)
        self.z = lax.div(w, 16)
        self.core = lax.rem(n, 2)
        self.n1 = n + 1 - 2 * self.core
        self.n2 = lax.rem(n + 2, 4)
        self.mate = (w, self.n1)
        self.zlo = (w, self.n2)
        self.zhi = (lax.rem(w + 16, 32), n)
        self.side = (lax.rem(w + 16, 32), self.n2)

    def coord(self, axis):
        return self.x if axis == "x" else self.y

    def along(self, axis, d):
        if axis == "x":
            return (self.w - self.x + lax.rem(self.x + d, 4), self.n)
        return (self.w - 4 * self.y + 4 * lax.rem(self.y + d, 4), self.n)

    def sems(self, count):
        self.nsem += count
        assert self.nsem <= NSEM
        return self.nsem - count

    def locals(self, count):
        self.nloc += count
        assert self.nloc <= NLOC
        return self.nloc - count

    def remote(self, src, dst, sem, device):
        return pltpu.make_async_remote_copy(
            src_ref=src,
            dst_ref=dst,
            send_sem=self.send.at[sem],
            recv_sem=self.recv.at[sem],
            device_id=device,
            device_id_type=MESH,
        )

    def copy(self, src, dst, sem):
        return pltpu.make_async_copy(src, dst, self.loc.at[sem])


def kernel(
    x_in,
    dy_in,
    seg_in,
    pad_in,
    wt_in,
    qg_in,
    kg_in,
    wo_in,
    up_in,
    dn_in,
    ag_in,
    as_in,
    mg_in,
    ms_in,
    lo_out,
    gt_out,
    gup_out,
    gdn_out,
    g2_out,
    vec_out,
    *scratch,
):
    s = Names()
    for name, ref in zip(SCRATCH, scratch):
        setattr(s, name, ref)
    k = Kernel(s, *scratch[len(SCRATCH) :])
    n, core = k.n, k.core

    own_wo = s.wo.at[at(n * W, W, W)]
    pieces = [pl.ds(b * BLK, BLK) for b in range(CH)]
    loads = [
        (x_in.at[pieces[0]], s.x.at[pieces[0]]),
        (wt_in, s.wt),
        (wo_in, own_wo),
        *[(x_in.at[rows], s.x.at[rows]) for rows in pieces[1:]],
        (up_in, s.up),
        (dn_in, s.dn),
        (dy_in, s.dy),
    ]
    load_sem = k.locals(len(loads))
    loads = [k.copy(src, dst, load_sem + i) for i, (src, dst) in enumerate(loads)]
    for load in loads[:6]:
        load.start()
    load_x, load_w, load_wo, *load_rest, load_up, load_dn, load_dy = loads

    barrier = pltpu.get_barrier_semaphore()
    peers = [k.mate, k.zlo, k.zhi, k.side]
    peers += [k.along(axis, d) for axis in "xy" for d in (1, 2, 3)]
    for peer in peers:
        pl.semaphore_signal(barrier, inc=1, device_id=peer, device_id_type=MESH)

    sem = k.sems(4)
    own_low = s.wo.at[at(n * W, W // 3, W // 3)]
    own_high = s.wo.at[at(n * W + W // 3, 2 * W // 3, W // 3)]
    other_wo = s.wo.at[at(k.n2 * W, W, W)]
    wo_sends = [
        k.remote(own_wo, own_wo, sem, k.mate),
        k.remote(own_low, own_low, sem + 1, k.zlo),
        k.remote(own_high, own_high, sem + 2, k.side),
    ]
    wo_pass = k.remote(other_wo, other_wo, sem + 3, k.mate)
    mix_sem = k.sems(3 * CH)

    def mix_mate(b):
        ref = s.mixed.at[at(n * W, W, W), chunk(b)]
        return k.remote(ref, ref, mix_sem + b, k.mate)

    def mix_z(b):
        ref = s.mixed.at[at(n * W, W, W), chunk(b)]
        return k.remote(ref, ref, mix_sem + CH + b, k.zlo)

    def mix_pass(b):
        ref = s.mixed.at[at(k.n2 * W, W, W), chunk(b)]
        return k.remote(ref, ref, mix_sem + 2 * CH + b, k.mate)

    ar2 = Narrow(k, s.p2, s.r12, s.r22, lambda b, rows: (s.r22.at[b], lo_out.at[rows]))
    ar3 = Narrow(k, s.p3, s.r13, s.r23, lambda b, rows: (s.gattn.at[rows], s.gattn.at[rows]))
    ar4 = Narrow(k, s.p4, s.r14, s.r24, lambda b, rows: (s.r24.at[b], gt_out.at[rows]))
    low_cols, high_cols = pl.ds(0, D // 2), pl.ds(D // 2, D // 2)
    wide_1 = Wide(k, "a", s.m1, low_cols, gdn_out, "x", "y"), Wide(k, "b", s.m1, high_cols, gdn_out, "y", "x")
    wide_2 = Wide(k, "c", s.m0, low_cols, gup_out, "x", "y"), Wide(k, "d", s.m0, high_cols, gup_out, "y", "x")
    wide_3 = Wide(k, "e", s.m2, low_cols, g2_out, "x", "y"), Wide(k, "f", s.m2, high_cols, g2_out, "y", "x")

    def wide(pair, step, *args):
        for item in pair:
            getattr(item, step)(*args)

    vec_sem = k.sems(3 + 3 + 3)
    vec_c = k.remote(s.vecs, s.rvz.at[0], vec_sem, k.mate)
    vec_x = [k.remote(s.v1, s.rvx.at[k.x], vec_sem + d, k.along("x", d)) for d in (1, 2, 3)]
    vec_y = [k.remote(s.v2, s.rvy.at[k.y], vec_sem + 3 + d, k.along("y", d)) for d in (1, 2, 3)]
    vec_z = k.remote(s.v3, s.rvz.at[1], vec_sem + 7, k.zhi)
    vec_l = k.remote(s.v4, s.rvz.at[2], vec_sem + 8, k.zlo)
    out_sem = k.locals(2 * CH)

    def lo_copy(b):
        return k.copy(s.r22.at[b], lo_out.at[ar2.mine(b)], out_sem + b)

    def gt_copy(b):
        return k.copy(s.r24.at[b], gt_out.at[ar4.mine(b)], out_sem + CH + b)


    ag = ag_in[...].reshape(1, D)
    ash = as_in[...].reshape(1, D)
    mg = mg_in[...].reshape(1, D)
    msh = ms_in[...].reshape(1, D)
    limit = T - pad_in[0]

    load_x.wait()

    def gain_col(c, h):
        col = s.gcol[c * W + h * HD : c * W + (h + 1) * HD, :]
        return jnp.concatenate([col, col], axis=1)

    lanes = lax.broadcasted_iota(jnp.int32, (1, BLK), 1)
    subs = lax.broadcasted_iota(jnp.int32, (HD, BLK), 0)

    def padded(b):
        return jnp.where(lanes + b * BLK >= limit, 1.0, 0.0)

    def first_norm(b):
        for i in range(2):
            rows = slice(b * BLK + i * HALF, b * BLK + (i + 1) * HALF)
            hat, _ = moments(s.x[rows, :].astype(F32))
            s.hat1[rows, :] = hat.astype(BF)
            s.normed[rows, :] = (hat * ag + ash).astype(BF)

    def project(b):
        raw = nt(s.wt[...], s.normed[chunk(b), :])
        if b + 1 < CH:
            first_norm(b + 1)
        same = jnp.where(subs == seg_in[:, chunk(b)], 1.0, 0.0)
        same_valid = same * (1.0 - padded(b))
        query_rows = jnp.where(subs == MINUS, -BIG, BIG * same)
        key_rows = jnp.where(subs == MINUS, 1.0, same_valid)
        ones = jnp.where(subs < 2, 1.0, 0.0)
        for h in range(HEADS):
            for which in range(2):
                rows = slice(which * W + h * HD, which * W + (h + 1) * HD)
                value = raw[rows]
                centre = value - jnp.mean(value, axis=0, keepdims=True)
                rstd = lax.rsqrt(jnp.mean(centre * centre, axis=0, keepdims=True) + EPS)
                hat = centre * rstd
                s.hat[rows, chunk(b)] = hat
                s.rstd[which * HEADS + h, :, chunk(b)] = rstd
                value = hat * gain_col(which, h) * (1.0, SC)[which]
                both = jnp.concatenate([value, (query_rows, key_rows)[which]], axis=0)
                if which == 0:
                    s.qta[h, :, chunk(b)] = both.astype(BF)
                    tall = jnp.concatenate([value, jnp.zeros_like(value)], axis=0)
                    s.qn[h, chunk(b), :] = jnp.transpose(tall).astype(BF)
                else:
                    s.kta[h, :, chunk(b)] = both.astype(BF)
                    s.kn[h, chunk(b), :] = jnp.transpose(both).astype(BF)
            value = raw[2 * W + h * HD : 2 * W + (h + 1) * HD]
            s.vt[h * HD : (h + 1) * HD, chunk(b)] = value.astype(BF)
            s.vn[h, chunk(b), :] = jnp.transpose(jnp.concatenate([value, ones], axis=0)).astype(BF)

    first_norm(0)
    s.vec[...] = jnp.zeros_like(s.vec)
    s.gacc[...] = jnp.zeros_like(s.gacc)
    s.gcol[0:W, :] = jnp.transpose(jnp.broadcast_to(qg_in[...].reshape(1, W), (128, W)))
    s.gcol[W:, :] = jnp.transpose(jnp.broadcast_to(kg_in[...].reshape(1, W), (128, W)))
    load_w.wait()
    load_wo.wait()
    for load in loads[3:6]:
        load.wait()
    for load in loads[6:]:
        load.start()
    pl.semaphore_wait(barrier, len(peers))
    for copy in wo_sends:
        copy.start()
    for b in range(CH):
        project(b)

    def window(b):
        return range(max(b - 1, 0), min(b + 2, CH))

    def self_score(b, h):
        query = s.qta[h, 0:HD, chunk(b)].astype(F32)
        key = s.kta[h, 0:HD, chunk(b)].astype(F32)
        return query, key, jnp.sum(query * key, axis=0, keepdims=True)

    units = [(b, i) for b in range(CH) for i in window(b)]

    def attend(b):
        pad_row = padded(b)
        pairs = [(h, i) for h in range(HEADS) for i in window(b)]
        scores = [nn(s.kn[h, chunk(i), :], s.qta[h, :, chunk(b)]) for h, i in pairs]
        totals, outs = [], []
        for h in range(HEADS):
            own = jnp.exp2(self_score(b, h)[2]) * pad_row
            totals.append(own)
            outs.append(s.vt[h * HD : (h + 1) * HD, chunk(b)].astype(F32) * own)
        for (h, i), score in zip(pairs, scores):
            weight = jnp.exp2(score)
            totals[h] = totals[h] + jnp.sum(weight, axis=0, keepdims=True)
            weight = weight.astype(BF)
            s.wgt[h, units.index((b, i))] = weight
            outs[h] = outs[h] + nn(s.vt[h * HD : (h + 1) * HD, chunk(i)], weight)
        for h in range(HEADS):
            inv = 1.0 / totals[h]
            s.inv[h, :, chunk(b)] = inv
            out = outs[h] * inv
            s.mixf[h * HD : (h + 1) * HD, chunk(b)] = out
            s.mixed[at(n * W + h * HD, HD, HD), chunk(b)] = out.astype(BF)

    def send_mixed(b):
        mix_z(b).start()
        mix_mate(b).start()

    for b in range(CH):
        attend(b)
        send_mixed(b)

    load_dy.wait()
    load_dn.wait()
    s.gact[0 : T // 2, :] = nt(s.dy[0 : T // 2, :], s.dn[...])
    for copy in wo_sends[1:]:
        copy.wait_recv()
    wo_pass.start()
    s.gact[T // 2 :, :] = nt(s.dy[T // 2 :, :], s.dn[...])
    load_up.wait()
    mix_z(0).wait_recv()
    mix_pass(0).start()
    wo_sends[0].wait_recv()
    wo_pass.wait_recv()

    def wait_mixed(b):
        mix_mate(b).wait_recv()
        mix_pass(b).wait_recv()

    def out_product(b):
        s.big0[...] = tn(s.mixed[:, chunk(b)], s.wo[...])

    def pass_mixed(b):
        mix_z(b).wait_recv()
        mix_pass(b).start()

    def second_norm(b):
        for i in range(2):
            rows = slice(b * BLK + i * HALF, b * BLK + (i + 1) * HALF)
            hat, _ = moments(s.x[rows, :].astype(F32) + s.big0[i * HALF : (i + 1) * HALF, :])
            s.normed2[rows, :] = (hat * mg + msh).astype(BF)
        own = s.x[ar3.mine(b), :].astype(F32)
        s.mid[b] = own + s.big0[at(core * HALF, HALF, HALF), :]

    def gelu(b):
        for i in range(BLK // 8):
            out = slice(b * BLK + i * 8, b * BLK + (i + 1) * 8)
            pre = s.big1[i * 8 : (i + 1) * 8, :]
            square = pre * pre
            tanh = jnp.tanh(pre * (GELU_A + GELU_B * square))
            half = 0.5 + 0.5 * tanh
            slope = half + (0.5 * pre) * (1.0 - tanh * tanh) * (GELU_A + 3.0 * GELU_B * square)
            s.active[out, :] = (pre * half).astype(BF)
            s.gpre[out, :] = (s.gact[out, :] * slope).astype(BF)

    def mlp_part(b):
        rows = slice(b * BLK, (b + 1) * BLK)
        s.p2[rows, :] = nn(s.active[rows, :], s.dn[...]).astype(BF)

    wait_mixed(0)
    out_product(0)
    pass_mixed(1)
    second_norm(0)
    s.big1[...] = nn(s.normed2[0:BLK, :], s.up[...])
    for b in range(CH):
        rows = slice(b * BLK, (b + 1) * BLK)
        if b + 1 < CH:
            wait_mixed(b + 1)
        gelu(b)
        if b + 1 < CH:
            out_product(b + 1)
        if b >= 1:
            ar3.s2(b - 1)
            ar2.s1(b - 1)
        if b + 2 < CH:
            pass_mixed(b + 2)
        s.p3[rows, :] = nt(s.gpre[rows, :], s.up[...]).astype(BF)
        if b + 1 < CH:
            second_norm(b + 1)
        ar3.s1(b)
        if b + 1 < CH:
            after = slice((b + 1) * BLK, (b + 2) * BLK)
            s.big1[...] = nn(s.normed2[after, :], s.up[...])
            mlp_part(b)

    left, right = slice(0, D // 2), slice(D // 2, D)
    s.m1[:, left] = tn(s.active[...], s.dy[:, left]).astype(BF)
    ar3.s2(CH - 1)
    wide(wide_1[:1], "step1")
    s.m1[:, right] = tn(s.active[...], s.dy[:, right]).astype(BF)
    wide(wide_1[1:], "step1")

    def second_back(b):
        ar3.d2(b).wait_recv()
        total = ar3.total(b)
        hat, rstd = moments(s.mid[b])
        s.vec[2:3, :] += 0.5 * jnp.sum(total * hat, axis=0, keepdims=True)
        s.vec[3:4, :] += 0.5 * jnp.sum(total, axis=0, keepdims=True)
        grad = s.dy[ar3.mine(b), :].astype(F32) + norm_back(total * mg, hat, rstd)
        s.gm[b] = grad
        s.gattn[ar3.mine(b), :] = grad.astype(BF)
        ar3.d3(b).start()

    def head_back(grad, which, h, b):
        rows = slice(which * W + h * HD, which * W + (h + 1) * HD)
        hat = s.hat[rows, chunk(b)]
        s.gacc[rows, :] += grad * hat
        grad = grad * gain_col(which, h)
        grad = (
            grad
            - jnp.mean(grad, axis=0, keepdims=True)
            - hat * jnp.mean(grad * hat, axis=0, keepdims=True)
        )
        s.gproj[rows, chunk(b)] = (grad * s.rstd[which * HEADS + h, :, chunk(b)]).astype(BF)

    def attend_back(b):
        ar3.d3(b).wait_recv()
        grad_mixed = nt(s.wo[at(n * W, W, W), :], s.gattn[chunk(b), :])
        if b == CH - 1:
            s.m2[3 * W :, :] = nn(s.mixed[at(n * W, W, W), :], s.gattn[...]).astype(BF)
        pad_row = padded(b)
        wides, pairs, grad_queries = [], [], []
        for h in range(HEADS):
            rows = slice(h * HD, (h + 1) * HD)
            grad_out = grad_mixed[rows].astype(BF).astype(F32)
            inv = s.inv[h, :, chunk(b)]
            delta = jnp.sum(grad_out * s.mixf[rows, chunk(b)], axis=0, keepdims=True)
            scaled = grad_out * inv
            low = delta * inv
            high = low.astype(BF).astype(F32)
            extra = jnp.where(subs == 0, -high, jnp.where(subs == 1, high - low, 0.0))
            wides.append(jnp.concatenate([scaled, extra], axis=0).astype(BF))
            tall = jnp.concatenate([jnp.zeros_like(scaled), scaled], axis=0)
            tall = jnp.transpose(tall).astype(BF)
            pairs.append(jnp.concatenate([s.qn[h, chunk(b), :], tall], axis=0))
            qf, kf, own = self_score(b, h)
            own_prob = jnp.exp2(own) * inv * pad_row
            own_grad = jnp.sum(grad_out * s.vt[rows, chunk(b)].astype(F32), axis=0, keepdims=True)
            own_score = own_prob * (own_grad - delta)
            s.dkx[rows, chunk(b)] = qf * own_score
            s.dvx[rows, chunk(b)] = grad_out * own_prob
            grad_queries.append(kf * own_score)
        tasks = [(h, i) for h in range(HEADS) for i in window(b)]
        products, ahead = {}, 3
        grad_scores = [[] for _ in range(HEADS)]
        for t in range(len(tasks) + ahead):
            if t < len(tasks):
                h, i = tasks[t]
                products[t] = nn(s.vn[h, chunk(i), :], wides[h])
            if t < ahead:
                continue
            h, i = tasks[t - ahead]
            weight = s.wgt[h, units.index((b, i))]
            grad_score = (weight.astype(F32) * products.pop(t - ahead)).astype(BF)
            grad_scores[h].append(grad_score)
            both = nn(jnp.concatenate([grad_score, weight], axis=1), pairs[h])
            if b == max(i - 1, 0):
                s.dkv[h, chunk(i), :] = both
            else:
                s.dkv[h, chunk(i), :] += both
            if i == window(b)[-1]:
                keys = s.kta[h, 0:HD, window(b)[0] * BLK : (i + 1) * BLK]
                grad_queries[h] = grad_queries[h] + nn(
                    keys, jnp.concatenate(grad_scores[h], axis=0)
                )
        for h in range(HEADS):
            head_back(grad_queries[h] * (0.125 / SC), 0, h, b)

    def keys_back(b):
        for h in range(HEADS):
            rows = slice(h * HD, (h + 1) * HD)
            both = jnp.transpose(s.dkv[h, chunk(b), :])
            head_back((both[0:HD] + s.dkx[rows, chunk(b)]) * 0.125, 1, h, b)
            grad_value = both[HD:] + s.dvx[rows, chunk(b)]
            s.gproj[2 * W + h * HD : 2 * W + (h + 1) * HD, chunk(b)] = grad_value.astype(BF)

    def first_part(b):
        s.big0[...] = tn(s.gproj[:, chunk(b)], s.wt[...])
        for i in range(2):
            rows = slice(b * BLK + i * HALF, b * BLK + (i + 1) * HALF)
            part = s.big0[i * HALF : (i + 1) * HALF, :]
            s.p4[rows, :] = part.astype(BF)
            s.vec[0:1, :] += jnp.sum(part * s.hat1[rows, :].astype(F32), axis=0, keepdims=True)
            s.vec[1:2, :] += jnp.sum(part, axis=0, keepdims=True)
        ar4.s1(b)

    second_back(0)
    s.m0[...] = tn(s.normed2[...], s.gpre[...]).astype(BF)
    wide(wide_2, "step1", (2,))
    attend_back(0)
    second_back(1)
    mlp_part(CH - 1)
    ar2.s1(CH - 1)
    ar2.s2(0)
    attend_back(1)
    keys_back(0)
    second_back(2)
    first_part(0)
    wide(wide_1, "step2")
    wide(wide_2, "step1", (1, 3))
    attend_back(2)
    keys_back(1)
    second_back(3)
    first_part(1)
    wide(wide_1, "step3")
    ar2.s2(1)
    attend_back(3)
    keys_back(2)
    keys_back(3)
    wide(wide_2, "step2")
    s.m2[0 : 3 * W, left] = nn(s.gproj[...], s.normed[:, left]).astype(BF)
    wide(wide_3[:1], "step1")
    s.m2[0 : 3 * W, right] = nn(s.gproj[...], s.normed[:, right]).astype(BF)
    wide(wide_3[1:], "step1")
    ar4.s2(0)
    wide(wide_1, "step4")
    first_part(2)
    first_part(3)
    for which in range(2):
        rows = slice(which * W, (which + 1) * W)
        both = s.gacc[rows, 0:128] + s.gacc[rows, 128:256]
        s.vec[4 + which : 5 + which, 0:W] = jnp.sum(jnp.transpose(both), axis=0, keepdims=True)
    s.vecs[...] = s.vec[...]
    vec_c.start()

    def layer_out(b):
        ar2.d2(b).wait_recv()
        s.r22[b] = (s.mid[b] + ar2.total(b)).astype(BF)
        ar2.d3(b).start()
        lo_copy(b).start()

    def grad_tokens(b):
        ar4.d2(b).wait_recv()
        hat, rstd = moments(s.x[ar4.mine(b), :].astype(F32))
        s.r24[b] = (s.gm[b] + norm_back(ar4.total(b) * ag, hat, rstd)).astype(BF)
        ar4.d3(b).start()
        gt_copy(b).start()

    wide(wide_2, "step3")
    ar2.s2(2)
    ar4.s2(1)
    upper = lax.broadcasted_iota(jnp.int32, (8, D), 0) < 4
    vec_c.wait_recv()
    s.v1[...] = s.vec[...] + jnp.where(upper, s.rvz[0], 0.0)
    s.rvx[k.x] = s.v1[...]
    for copy in vec_x:
        copy.start()
    layer_out(0)
    wide(wide_3, "step2")
    wide(wide_2, "step4")
    wide(wide_1, "step5")
    for d in (1, 3):
        wide(wide_1, "step6", d)
    for copy in vec_x:
        copy.wait_recv()
    s.v2[...] = (s.rvx[0] + s.rvx[1]) + (s.rvx[2] + s.rvx[3])
    s.rvy[k.y] = s.v2[...]
    for copy in vec_y:
        copy.start()
    layer_out(1)
    wide(wide_3, "step3")
    ar4.s2(2)
    wide(wide_2, "step5")
    for copy in vec_y:
        copy.wait_recv()
    s.v3[...] = (s.rvy[0] + s.rvy[1]) + (s.rvy[2] + s.rvy[3])
    vec_z.start()
    ar2.s2(3)
    grad_tokens(0)
    wide(wide_3, "step4")
    wide(wide_1, "step7")
    for d in (1, 3):
        wide(wide_2, "step6", d)
    vec_z.wait_recv()
    s.v4[...] = s.v3[...] + s.rvz[1]
    vec_l.start()
    ar4.s2(3)
    layer_out(2)
    grad_tokens(1)
    wide(wide_3, "step5")
    for d in (2, 1, 3):
        wide(wide_3, "step6", d)
    wide(wide_2, "step7")
    vec_l.wait_recv()
    vec_out[...] = s.v4[...] + jnp.where(upper, s.rvz[2], 0.0)
    grad_tokens(2)
    layer_out(3)
    grad_tokens(3)

    for b in range(CH):
        ar2.d3(b).wait_recv()
        ar4.d3(b).wait_recv()
        lo_copy(b).wait()
        gt_copy(b).wait()
        mix_mate(b).wait_send()
        mix_z(b).wait_send()
        mix_pass(b).wait_send()
    for item in (ar2, ar3, ar4, *wide_1, *wide_2, *wide_3):
        item.finish()
    for copy in [*wo_sends, wo_pass, *vec_x, *vec_y, vec_z, vec_c, vec_l]:
        copy.wait_send()


PARTS = 4


def finish(lo, gt, gup, gdn, g2, vec, lo_o, gt_o, qkv_o, qg_o, kg_o, out_o, gup_o, gdn_o, ag_o, as_o, mg_o, ms_o, low, high, same, sem_in, sem_out):
    size = D // PARTS
    pieces = []
    for i, (src, dst) in enumerate(((gup, gup_o), (gdn, gdn_o), (g2, None))):
        for p in range(PARTS):
            rows = pl.ds(p * size, size)
            if dst is None:
                to = qkv_o.at[p] if p < 3 else out_o
            else:
                to = dst.at[rows]
            load = pltpu.make_async_copy(src.at[rows], low.at[i, rows], sem_in.at[i, p])
            pieces.append((load, (i, rows), pltpu.make_async_copy(high.at[i, rows], to, sem_out.at[i, p])))
    size = T // PARTS
    for i, (src, dst) in enumerate(((lo, lo_o), (gt, gt_o))):
        for p in range(PARTS):
            rows = pl.ds(p * size, size)
            load = pltpu.make_async_copy(src.at[rows], same.at[i, rows], sem_in.at[3 + i, p])
            pieces.append((load, None, pltpu.make_async_copy(same.at[i, rows], dst.at[rows], sem_out.at[3 + i, p])))
    for load, _, _ in pieces:
        load.start()
    for ref, row, count in (
        (ag_o, 0, D),
        (as_o, 1, D),
        (mg_o, 2, D),
        (ms_o, 3, D),
        (qg_o, 4, W),
        (kg_o, 5, W),
    ):
        ref[...] = vec[row : row + 1, 0:count].reshape(count)
    for load, cast, store in pieces:
        load.wait()
        if cast is not None:
            high[cast] = low[cast].astype(F32)
        store.start()
    for _, _, store in pieces:
        store.wait()


def body(*args):
    any_spec = pl.BlockSpec(memory_space=pl.ANY)
    vmem = pl.BlockSpec(memory_space=pltpu.VMEM)
    smem = pl.BlockSpec(memory_space=pltpu.SMEM)
    args = list(args)
    args[4] = jnp.swapaxes(args[4], 1, 2).reshape(3 * W, D)
    out = pl.pallas_call(
        kernel,
        out_shape=(
            jax.ShapeDtypeStruct((T, D), BF),
            jax.ShapeDtypeStruct((T, D), BF),
            jax.ShapeDtypeStruct((D, F), BF),
            jax.ShapeDtypeStruct((F, D), BF),
            jax.ShapeDtypeStruct((4 * W, D), BF),
            jax.ShapeDtypeStruct((8, D), F32),
        ),
        in_specs=[any_spec, any_spec, vmem, smem, any_spec, vmem, vmem]
        + [any_spec] * 3
        + [vmem] * 4,
        out_specs=(any_spec, any_spec, any_spec, any_spec, any_spec, vmem),
        scratch_shapes=[pltpu.VMEM(shape, dtype) for shape, dtype in SCRATCH.values()]
        + [
            pltpu.SemaphoreType.DMA((NSEM,)),
            pltpu.SemaphoreType.DMA((NSEM,)),
            pltpu.SemaphoreType.DMA((NLOC,)),
        ],
        compiler_params=pltpu.CompilerParams(
            collective_id=0, has_side_effects=True, vmem_limit_bytes=60 * 1024 * 1024
        ),
        cost_estimate=pl.CostEstimate(
            flops=14 * 10**9, bytes_accessed=20 * 2**20, transcendentals=8 * 2**20
        ),
    )(*args)
    layer, tokens, qkv, *rest = pl.pallas_call(
        finish,
        out_shape=(
            jax.ShapeDtypeStruct((T, D), BF),
            jax.ShapeDtypeStruct((T, D), BF),
            jax.ShapeDtypeStruct((3, W, D), F32),
            jax.ShapeDtypeStruct((W,), F32),
            jax.ShapeDtypeStruct((W,), F32),
            jax.ShapeDtypeStruct((W, D), F32),
            jax.ShapeDtypeStruct((D, F), F32),
            jax.ShapeDtypeStruct((F, D), F32),
            jax.ShapeDtypeStruct((D,), F32),
            jax.ShapeDtypeStruct((D,), F32),
            jax.ShapeDtypeStruct((D,), F32),
            jax.ShapeDtypeStruct((D,), F32),
        ),
        in_specs=[any_spec] * 5 + [vmem],
        out_specs=(any_spec, any_spec, any_spec, vmem, vmem, any_spec, any_spec, any_spec)
        + (vmem,) * 4,
        scratch_shapes=[
            pltpu.VMEM((3, D, D), BF),
            pltpu.VMEM((3, D, D), F32),
            pltpu.VMEM((2, T, D), BF),
            pltpu.SemaphoreType.DMA((5, PARTS)),
            pltpu.SemaphoreType.DMA((5, PARTS)),
        ],
        compiler_params=pltpu.CompilerParams(vmem_limit_bytes=60 * 1024 * 1024),
        cost_estimate=pl.CostEstimate(flops=0, bytes_accessed=17 * 2**20, transcendentals=0),
    )(*out)
    return (layer, tokens, jnp.swapaxes(qkv, 1, 2), *rest)


def solution(mesh):
    placed = (
        P("wide", None),
        P("wide", None),
        P("wide", None),
        P("wide"),
        P(None, None, "narrow"),
        P("narrow"),
        P("narrow"),
        P("narrow", None),
        P(None, "narrow"),
        P("narrow", None),
        P(),
        P(),
        P(),
        P(),
    )
    return jax.shard_map(
        body,
        mesh=mesh,
        in_specs=placed,
        out_specs=(
            P("wide", None),
            P("wide", None),
            P(None, None, "narrow"),
            P("narrow"),
            P("narrow"),
            P("narrow", None),
            P(None, "narrow"),
            P("narrow", None),
            P(),
            P(),
            P(),
            P(),
        ),
        check_vma=False,
    )
```

```python
import jax
import jax.numpy as jnp
from jax import lax
from jax.experimental import pallas as pl
from jax.experimental.pallas import tpu as pltpu
from jax.sharding import PartitionSpec as P

T = 1024
D = 768
HEADS = 3
HD = 64
W = HEADS * HD
F = 768
BLK = 256
CH = T // BLK
HALF = BLK // 2
BIG = 512.0
MINUS = 31
LOG2E = 1.4426950408889634
SC = 0.125 * LOG2E
EPS = 1e-06
GELU_A = 0.7978845608028654
GELU_B = 0.044715 * GELU_A

BF = jnp.bfloat16
F32 = jnp.float32
MESH = pl.DeviceIdType.MESH


def nn(a, b):
    return lax.dot_general(a, b, (((1,), (0,)), ((), ())), preferred_element_type=F32)


def nt(a, b):
    return lax.dot_general(a, b, (((1,), (1,)), ((), ())), preferred_element_type=F32)


def tn(a, b):
    return lax.dot_general(a, b, (((0,), (0,)), ((), ())), preferred_element_type=F32)


def at(start, size, unit):
    return pl.ds(pl.multiple_of(start, unit), size)


def chunk(b):
    return at(b * BLK, BLK, BLK)


def moments(values):
    centre = values - jnp.mean(values, axis=-1, keepdims=True)
    rstd = lax.rsqrt(jnp.mean(centre * centre, axis=-1, keepdims=True) + EPS)
    return centre * rstd, rstd


def norm_back(grad, hat, rstd):
    return rstd * (
        grad
        - jnp.mean(grad, axis=-1, keepdims=True)
        - hat * jnp.mean(grad * hat, axis=-1, keepdims=True)
    )


SCRATCH = dict(
    seg=((1, T), jnp.int32),
    qg=((W,), F32),
    kg=((W,), F32),
    ag=((D,), F32),
    ash=((D,), F32),
    mg=((D,), F32),
    msh=((D,), F32),
    x=((T, D), BF),
    dy=((T, D), BF),
    wt=((3 * W, D), BF),
    wo=((4 * W, D), BF),
    up=((D, F), BF),
    dn=((F, D), BF),
    normed=((T, D), BF),
    hat1=((T, D), BF),
    qta=((HEADS, 2 * HD, T), BF),
    kta=((HEADS, 2 * HD, T), BF),
    vt=((W, T), BF),
    qn=((HEADS, T, 2 * HD), BF),
    kn=((HEADS, T, 2 * HD), BF),
    vn=((HEADS, T, 2 * HD), BF),
    hat=((2 * W, T), F32),
    rstd=((6, 1, T), F32),
    gcol=((2 * W, 128), F32),
    mixed=((4 * W, T), BF),
    mixf=((W, T), F32),
    mid=((CH, HALF, D), F32),
    wgt=((HEADS, 10, BLK, BLK), BF),
    inv=((HEADS, 1, T), F32),
    normed2=((T, D), BF),
    active=((T, F), BF),
    gpre=((T, F), BF),
    big0=((BLK, D), F32),
    gact=((T, F), F32),
    big1=((BLK, D), F32),
    p2=((T, D), BF),
    p3=((T, D), BF),
    p4=((T, D), BF),
    r12=((CH, HALF, D), BF),
    r13=((CH, HALF, D), BF),
    r14=((CH, HALF, D), BF),
    r22=((CH, HALF, D), BF),
    r23=((CH, HALF, D), BF),
    r24=((CH, HALF, D), BF),
    gm=((CH, HALF, D), F32),
    gattn=((T, D), BF),
    dkv=((HEADS, T, 2 * HD), F32),
    dkx=((W, T), F32),
    dvx=((W, T), F32),
    gproj=((3 * W, T), BF),
    gacc=((2 * W, BLK), F32),
    m0=((D, F), BF),
    m1=((F, D), BF),
    m2=((4 * W, D), BF),
    vec=((8, D), F32),
    vecs=((8, D), F32),
    rvx=((4, 8, D), F32),
    rvy=((4, 8, D), F32),
    rvz=((3, 8, D), F32),
    v1=((8, D), F32),
    v2=((8, D), F32),
    v3=((8, D), F32),
    v4=((8, D), F32),
)
RELAYED = "abcd"
for _s, _w in ((_c, D // 2) for _c in "abcdef"):
    SCRATCH["rs1" + _s] = ((3, 192, _w), BF)
    SCRATCH["s1" + _s] = ((192, _w), BF)
    SCRATCH["rs2" + _s] = ((3, 48, _w), BF)
    SCRATCH["s2" + _s] = ((48, _w), BF)
    SCRATCH["rz" + _s] = ((48, _w), BF)
    SCRATCH["rr" + _s] = ((192, _w), BF)
    if _s in RELAYED:
        SCRATCH["nb" + _s] = ((2, 192, _w), BF)

NSEM = 224
NLOC = 56


class Wide:
    def __init__(self, k, name, mat, cols, out, first, second):
        self.k, self.s, self.mat, self.cols, self.out = k, k.s, mat, cols, out
        self.name = name
        self.first, self.second = first, second
        self.u, self.t = k.coord(first), k.coord(second)
        self.base = k.sems(3 + 3 + 1 + 3 + 12)
        self.local = k.locals(3)
        self.relayed = name in RELAYED

    def ref(self, what):
        return getattr(self.s, what + self.name)

    def rs1(self, d):
        k = self.k
        q = lax.rem(self.u + d, 4)
        return k.remote(
            self.mat.at[at(q * 192, 192, 192), self.cols],
            self.ref("rs1").at[d - 1],
            self.base + d - 1,
            k.along(self.first, d),
        )

    def rs2(self, d):
        k = self.k
        q = lax.rem(self.t + d, 4)
        return k.remote(
            self.ref("s1").at[at(q * 48, 48, 48)],
            self.ref("rs2").at[d - 1],
            self.base + 3 + d - 1,
            k.along(self.second, d),
        )

    def zz(self):
        return self.k.remote(self.ref("s2"), self.ref("rz"), self.base + 6, self.k.zhi)

    def ag2(self, d):
        piece = self.ref("rr").at[at(self.t * 48, 48, 48)]
        return self.k.remote(piece, piece, self.base + 7 + d - 1, self.k.along(self.second, d))

    def rows_out(self, u, start=0, size=192):
        return self.out.at[at(lax.rem(u + 4, 4) * 192 + start, size, 96), self.cols]

    def ag1(self, d):
        dst = self.ref("nb").at[0 if d == 1 else 1]
        return self.k.remote(self.ref("rr"), dst, self.base + 10 + d - 1, self.k.along(self.first, d))

    def piece(self, d, e):
        start = lax.rem(self.t + 4 - e, 4) * 48
        return self.k.remote(
            self.ref("rr").at[at(start, 48, 48)],
            self.out.at[at(self.u * 192 + start, 48, 48), self.cols],
            self.base + 10 + 3 * e + d - 1,
            self.k.along(self.first, d),
        )

    def forward(self, d):
        u, start = (self.u - 1, 0) if d == 1 else (self.u + 1, 96)
        src = self.ref("nb").at[0 if d == 1 else 1, pl.ds(start, 96)]
        return self.k.remote(
            src, self.rows_out(u, start, 96), self.base + 13 + d // 2, self.k.along(self.first, d)
        )

    def own(self, i=0):
        if i == 0:
            return self.k.copy(self.ref("rr"), self.rows_out(self.u), self.local)
        u = self.u - 1 if i == 1 else self.u + 1
        return self.k.copy(self.ref("nb").at[i - 1], self.rows_out(u), self.local + i)

    def step1(self, which=(2, 1, 3)):
        for d in which:
            self.rs1(d).start()

    def step2(self):
        for d in (1, 2, 3):
            self.rs1(d).wait_recv()
        rs1, s1 = self.ref("rs1"), self.ref("s1")

        def strip(i, c):
            rows = at(i * 48, 48, 48)
            total = self.mat[at(self.u * 192 + i * 48, 48, 48), self.cols].astype(F32)
            for d in range(3):
                total = total + rs1[d, rows, :].astype(F32)
            s1[rows, :] = total.astype(BF)
            return c

        lax.fori_loop(0, 4, strip, 0)
        for d in (2, 1, 3):
            self.rs2(d).start()

    def step3(self):
        for d in (1, 2, 3):
            self.rs2(d).wait_recv()
        total = self.ref("s1")[at(self.t * 48, 48, 48), :].astype(F32)
        for d in range(3):
            total = total + self.ref("rs2")[d].astype(F32)
        self.ref("s2")[...] = total.astype(BF)
        self.zz().start()

    def step4(self):
        self.zz().wait_recv()
        total = self.ref("s2")[...].astype(F32) + self.ref("rz")[...].astype(F32)
        self.ref("rr")[at(self.t * 48, 48, 48), :] = total.astype(BF)
        for d in (2, 1, 3):
            self.ag2(d).start()
        if not self.relayed:
            for d in (2, 1, 3):
                self.piece(d, 0).start()

    def step5(self):
        for e in (1, 3, 2):
            self.ag2(e).wait_recv()
            if not self.relayed:
                for d in (2, 1, 3):
                    self.piece(d, e).start()
        self.own().start()

    def step6(self, d):
        self.ag1(d).start()

    def step7(self):
        for d in (1, 3):
            self.ag1(d).wait_recv()
            self.forward(d).start()
        for i in (1, 2):
            self.own(i).start()

    def finish(self):
        self.own().wait()
        if self.relayed:
            for d in (1, 3):
                self.forward(d).wait_recv()
                self.forward(d).wait_send()
                self.ag1(d).wait_send()
                self.own(1 + d // 2).wait()
        else:
            for d in (1, 2, 3):
                for e in range(4):
                    self.piece(d, e).wait_recv()
                    self.piece(d, e).wait_send()
        for d in (1, 2, 3):
            self.rs1(d).wait_send()
            self.rs2(d).wait_send()
            self.ag2(d).wait_send()
        self.zz().wait_send()


class Narrow:
    def __init__(self, k, part, r1, r2, result):
        self.k, self.part, self.r1, self.r2, self.result = k, part, r1, r2, result
        self.base = k.sems(3 * CH)

    def mine(self, b):
        return at(b * BLK + self.k.core * HALF, HALF, HALF)

    def theirs(self, b):
        return at(b * BLK + (1 - self.k.core) * HALF, HALF, HALF)

    def d1(self, b):
        return self.k.remote(
            self.part.at[self.theirs(b)], self.r1.at[b], self.base + b, self.k.mate
        )

    def d2(self, b):
        return self.k.remote(
            self.part.at[self.mine(b)], self.r2.at[b], self.base + CH + b, self.k.zlo
        )

    def d3(self, b):
        src, dst = self.result(b, self.mine(b))
        return self.k.remote(src, dst, self.base + 2 * CH + b, self.k.mate)

    def s1(self, b):
        self.d1(b).start()

    def s2(self, b):
        self.d1(b).wait_recv()
        total = self.part[self.mine(b), :].astype(F32) + self.r1[b].astype(F32)
        self.part[self.mine(b), :] = total.astype(BF)
        self.d2(b).start()

    def total(self, b):
        return self.part[self.mine(b), :].astype(F32) + self.r2[b].astype(F32)

    def finish(self, last=True):
        for b in range(CH):
            self.d1(b).wait_send()
            self.d2(b).wait_send()
            self.d3(b).wait_send()


class Names:
    pass


class Kernel:
    def __init__(self, s, send, recv, loc):
        self.s, self.send, self.recv, self.loc = s, send, recv, loc
        self.nsem = self.nloc = 0
        w = lax.axis_index("wide")
        n = lax.axis_index("narrow")
        self.w, self.n = w, n
        self.x = lax.rem(w, 4)
        self.y = lax.rem(lax.div(w, 4), 4)
        self.z = lax.div(w, 16)
        self.core = lax.rem(n, 2)
        self.n1 = n + 1 - 2 * self.core
        self.n2 = lax.rem(n + 2, 4)
        self.mate = (w, self.n1)
        self.zlo = (w, self.n2)
        self.zhi = (lax.rem(w + 16, 32), n)
        self.side = (lax.rem(w + 16, 32), self.n2)

    def coord(self, axis):
        return self.x if axis == "x" else self.y

    def along(self, axis, d):
        if axis == "x":
            return (self.w - self.x + lax.rem(self.x + d, 4), self.n)
        return (self.w - 4 * self.y + 4 * lax.rem(self.y + d, 4), self.n)

    def sems(self, count):
        self.nsem += count
        assert self.nsem <= NSEM
        return self.nsem - count

    def locals(self, count):
        self.nloc += count
        assert self.nloc <= NLOC
        return self.nloc - count

    def remote(self, src, dst, sem, device):
        return pltpu.make_async_remote_copy(
            src_ref=src,
            dst_ref=dst,
            send_sem=self.send.at[sem],
            recv_sem=self.recv.at[sem],
            device_id=device,
            device_id_type=MESH,
        )

    def copy(self, src, dst, sem):
        return pltpu.make_async_copy(src, dst, self.loc.at[sem])


def kernel(
    x_in,
    dy_in,
    seg_in,
    pad_in,
    wt_in,
    qg_in,
    kg_in,
    wo_in,
    up_in,
    dn_in,
    ag_in,
    as_in,
    mg_in,
    ms_in,
    lo_out,
    gt_out,
    gup_out,
    gdn_out,
    g2_out,
    vec_out,
    *scratch,
):
    s = Names()
    for name, ref in zip(SCRATCH, scratch):
        setattr(s, name, ref)
    k = Kernel(s, *scratch[len(SCRATCH) :])
    n, core = k.n, k.core

    own_wo = s.wo.at[at(n * W, W, W)]
    pieces = [pl.ds(b * BLK, BLK) for b in range(CH)]
    loads = [
        (x_in.at[pieces[0]], s.x.at[pieces[0]]),
        (wt_in, s.wt),
        (wo_in, own_wo),
        *[(x_in.at[rows], s.x.at[rows]) for rows in pieces[1:]],
        (up_in, s.up),
        (dn_in, s.dn),
        (dy_in, s.dy),
    ]
    load_sem = k.locals(len(loads))
    loads = [k.copy(src, dst, load_sem + i) for i, (src, dst) in enumerate(loads)]
    smalls = [
        (ag_in, s.ag),
        (as_in, s.ash),
        (qg_in, s.qg),
        (kg_in, s.kg),
        (seg_in, s.seg),
        (mg_in, s.mg),
        (ms_in, s.msh),
    ]
    small_sem = k.locals(len(smalls))
    smalls = [k.copy(src, dst, small_sem + i) for i, (src, dst) in enumerate(smalls)]
    loads[0].start()
    for load in smalls + loads[1:6]:
        load.start()
    load_x, load_w, load_wo, *load_rest, load_up, load_dn, load_dy = loads

    barrier = pltpu.get_barrier_semaphore()
    peers = [k.mate, k.zlo, k.zhi, k.side]
    peers += [k.along(axis, d) for axis in "xy" for d in (1, 2, 3)]
    for peer in peers:
        pl.semaphore_signal(barrier, inc=1, device_id=peer, device_id_type=MESH)

    sem = k.sems(4)
    own_low = s.wo.at[at(n * W, W // 3, W // 3)]
    own_high = s.wo.at[at(n * W + W // 3, 2 * W // 3, W // 3)]
    other_wo = s.wo.at[at(k.n2 * W, W, W)]
    wo_sends = [
        k.remote(own_wo, own_wo, sem, k.mate),
        k.remote(own_low, own_low, sem + 1, k.zlo),
        k.remote(own_high, own_high, sem + 2, k.side),
    ]
    wo_pass = k.remote(other_wo, other_wo, sem + 3, k.mate)
    mix_sem = k.sems(3 * CH)

    def mix_mate(b):
        ref = s.mixed.at[at(n * W, W, W), chunk(b)]
        return k.remote(ref, ref, mix_sem + b, k.mate)

    def mix_z(b):
        ref = s.mixed.at[at(n * W, W, W), chunk(b)]
        return k.remote(ref, ref, mix_sem + CH + b, k.zlo)

    def mix_pass(b):
        ref = s.mixed.at[at(k.n2 * W, W, W), chunk(b)]
        return k.remote(ref, ref, mix_sem + 2 * CH + b, k.mate)

    ar2 = Narrow(k, s.p2, s.r12, s.r22, lambda b, rows: (s.r22.at[b], lo_out.at[rows]))
    ar3 = Narrow(k, s.p3, s.r13, s.r23, lambda b, rows: (s.gattn.at[rows], s.gattn.at[rows]))
    ar4 = Narrow(k, s.p4, s.r14, s.r24, lambda b, rows: (s.r24.at[b], gt_out.at[rows]))
    low_cols, high_cols = pl.ds(0, D // 2), pl.ds(D // 2, D // 2)
    wide_1 = Wide(k, "a", s.m1, low_cols, gdn_out, "x", "y"), Wide(k, "b", s.m1, high_cols, gdn_out, "y", "x")
    wide_2 = Wide(k, "c", s.m0, low_cols, gup_out, "x", "y"), Wide(k, "d", s.m0, high_cols, gup_out, "y", "x")
    wide_3 = Wide(k, "e", s.m2, low_cols, g2_out, "x", "y"), Wide(k, "f", s.m2, high_cols, g2_out, "y", "x")

    def wide(pair, step, *args):
        for item in pair:
            getattr(item, step)(*args)

    vec_sem = k.sems(3 + 3 + 3)
    vec_c = k.remote(s.vecs, s.rvz.at[0], vec_sem, k.mate)
    vec_x = [k.remote(s.v1, s.rvx.at[k.x], vec_sem + d, k.along("x", d)) for d in (1, 2, 3)]
    vec_y = [k.remote(s.v2, s.rvy.at[k.y], vec_sem + 3 + d, k.along("y", d)) for d in (1, 2, 3)]
    vec_z = k.remote(s.v3, s.rvz.at[1], vec_sem + 7, k.zhi)
    vec_l = k.remote(s.v4, s.rvz.at[2], vec_sem + 8, k.zlo)
    out_sem = k.locals(2 * CH)

    def lo_copy(b):
        return k.copy(s.r22.at[b], lo_out.at[ar2.mine(b)], out_sem + b)

    def gt_copy(b):
        return k.copy(s.r24.at[b], gt_out.at[ar4.mine(b)], out_sem + CH + b)


    limit = T - pad_in[0]

    for load in smalls:
        load.wait()
    load_x.wait()

    ag = s.ag[...].reshape(1, D)
    ash = s.ash[...].reshape(1, D)
    mg = s.mg[...].reshape(1, D)
    msh = s.msh[...].reshape(1, D)

    def gain_col(c, h):
        col = s.gcol[c * W + h * HD : c * W + (h + 1) * HD, :]
        return jnp.concatenate([col, col], axis=1)

    lanes = lax.broadcasted_iota(jnp.int32, (1, BLK), 1)
    subs = lax.broadcasted_iota(jnp.int32, (HD, BLK), 0)

    def padded(b):
        return jnp.where(lanes + b * BLK >= limit, 1.0, 0.0)

    def first_norm(b):
        for i in range(2):
            rows = slice(b * BLK + i * HALF, b * BLK + (i + 1) * HALF)
            hat, _ = moments(s.x[rows, :].astype(F32))
            s.hat1[rows, :] = hat.astype(BF)
            s.normed[rows, :] = (hat * ag + ash).astype(BF)

    def project(b):
        raw = nt(s.wt[...], s.normed[chunk(b), :])
        if b + 1 < CH:
            first_norm(b + 1)
        same = jnp.where(subs == s.seg[:, chunk(b)], 1.0, 0.0)
        same_valid = same * (1.0 - padded(b))
        query_rows = jnp.where(subs == MINUS, -BIG, BIG * same)
        key_rows = jnp.where(subs == MINUS, 1.0, same_valid)
        ones = jnp.where(subs < 2, 1.0, 0.0)
        for h in range(HEADS):
            for which in range(2):
                rows = slice(which * W + h * HD, which * W + (h + 1) * HD)
                value = raw[rows]
                centre = value - jnp.mean(value, axis=0, keepdims=True)
                rstd = lax.rsqrt(jnp.mean(centre * centre, axis=0, keepdims=True) + EPS)
                hat = centre * rstd
                s.hat[rows, chunk(b)] = hat
                s.rstd[which * HEADS + h, :, chunk(b)] = rstd
                value = hat * gain_col(which, h) * (1.0, SC)[which]
                both = jnp.concatenate([value, (query_rows, key_rows)[which]], axis=0)
                if which == 0:
                    s.qta[h, :, chunk(b)] = both.astype(BF)
                    tall = jnp.concatenate([value, jnp.zeros_like(value)], axis=0)
                    s.qn[h, chunk(b), :] = jnp.transpose(tall).astype(BF)
                else:
                    s.kta[h, :, chunk(b)] = both.astype(BF)
                    s.kn[h, chunk(b), :] = jnp.transpose(both).astype(BF)
            value = raw[2 * W + h * HD : 2 * W + (h + 1) * HD]
            s.vt[h * HD : (h + 1) * HD, chunk(b)] = value.astype(BF)
            s.vn[h, chunk(b), :] = jnp.transpose(jnp.concatenate([value, ones], axis=0)).astype(BF)

    first_norm(0)
    load_wo.wait()
    pl.semaphore_wait(barrier, len(peers))
    for copy in wo_sends:
        copy.start()
    s.vec[...] = jnp.zeros_like(s.vec)
    s.gacc[...] = jnp.zeros_like(s.gacc)
    s.gcol[0:W, :] = jnp.transpose(jnp.broadcast_to(s.qg[...].reshape(1, W), (128, W)))
    s.gcol[W:, :] = jnp.transpose(jnp.broadcast_to(s.kg[...].reshape(1, W), (128, W)))
    def window(b):
        return range(max(b - 1, 0), min(b + 2, CH))

    def self_score(b, h):
        query = s.qta[h, 0:HD, chunk(b)].astype(F32)
        key = s.kta[h, 0:HD, chunk(b)].astype(F32)
        return query, key, jnp.sum(query * key, axis=0, keepdims=True)

    units = [(b, i) for b in range(CH) for i in window(b)]

    def attend(b):
        pad_row = padded(b)
        pairs = [(h, i) for h in range(HEADS) for i in window(b)]
        scores = [nn(s.kn[h, chunk(i), :], s.qta[h, :, chunk(b)]) for h, i in pairs]
        totals, outs = [], []
        for h in range(HEADS):
            own = jnp.exp2(self_score(b, h)[2]) * pad_row
            totals.append(own)
            outs.append(s.vt[h * HD : (h + 1) * HD, chunk(b)].astype(F32) * own)
        for (h, i), score in zip(pairs, scores):
            weight = jnp.exp2(score)
            totals[h] = totals[h] + jnp.sum(weight, axis=0, keepdims=True)
            weight = weight.astype(BF)
            s.wgt[h, units.index((b, i))] = weight
            outs[h] = outs[h] + nn(s.vt[h * HD : (h + 1) * HD, chunk(i)], weight)
        for h in range(HEADS):
            inv = 1.0 / totals[h]
            s.inv[h, :, chunk(b)] = inv
            out = outs[h] * inv
            s.mixf[h * HD : (h + 1) * HD, chunk(b)] = out
            s.mixed[at(n * W + h * HD, HD, HD), chunk(b)] = out.astype(BF)

    def send_mixed(b):
        mix_z(b).start()
        mix_mate(b).start()

    load_w.wait()
    for load in load_rest:
        load.wait()
    for load in loads[6:]:
        load.start()
    for b in range(CH):
        project(b)
    for b in range(CH):
        attend(b)
        send_mixed(b)

    load_dy.wait()
    load_dn.wait()
    s.gact[0 : T // 2, :] = nt(s.dy[0 : T // 2, :], s.dn[...])
    for copy in wo_sends[1:]:
        copy.wait_recv()
    wo_pass.start()
    s.gact[T // 2 :, :] = nt(s.dy[T // 2 :, :], s.dn[...])
    load_up.wait()
    mix_z(0).wait_recv()
    mix_pass(0).start()
    wo_sends[0].wait_recv()
    wo_pass.wait_recv()

    def wait_mixed(b):
        mix_mate(b).wait_recv()
        mix_pass(b).wait_recv()

    def out_product(b):
        s.big0[...] = tn(s.mixed[:, chunk(b)], s.wo[...])

    def pass_mixed(b):
        mix_z(b).wait_recv()
        mix_pass(b).start()

    def second_norm(b):
        for i in range(2):
            rows = slice(b * BLK + i * HALF, b * BLK + (i + 1) * HALF)
            hat, _ = moments(s.x[rows, :].astype(F32) + s.big0[i * HALF : (i + 1) * HALF, :])
            s.normed2[rows, :] = (hat * mg + msh).astype(BF)
        own = s.x[ar3.mine(b), :].astype(F32)
        s.mid[b] = own + s.big0[at(core * HALF, HALF, HALF), :]

    def gelu(b):
        for i in range(BLK // 8):
            out = slice(b * BLK + i * 8, b * BLK + (i + 1) * 8)
            pre = s.big1[i * 8 : (i + 1) * 8, :]
            square = pre * pre
            tanh = jnp.tanh(pre * (GELU_A + GELU_B * square))
            half = 0.5 + 0.5 * tanh
            slope = half + (0.5 * pre) * (1.0 - tanh * tanh) * (GELU_A + 3.0 * GELU_B * square)
            s.active[out, :] = (pre * half).astype(BF)
            s.gpre[out, :] = (s.gact[out, :] * slope).astype(BF)

    def mlp_part(b):
        rows = slice(b * BLK, (b + 1) * BLK)
        s.p2[rows, :] = nn(s.active[rows, :], s.dn[...]).astype(BF)

    def up_product(b):
        s.big1[...] = nn(s.normed2[b * BLK : (b + 1) * BLK, :], s.up[...])

    wait_mixed(0)
    out_product(0)
    pass_mixed(1)
    second_norm(0)
    up_product(0)
    for b in range(CH):
        rows = slice(b * BLK, (b + 1) * BLK)
        gelu(b)
        if b >= 1:
            ar2.s1(b - 1)
        s.p3[rows, :] = nt(s.gpre[rows, :], s.up[...]).astype(BF)
        if b >= 1 and b + 1 < CH:
            second_norm(b + 1)
        ar3.s1(b)
        if b == 0:
            wait_mixed(1)
            out_product(1)
            second_norm(1)
            pass_mixed(2)
            ar3.s2(0)
        if b + 2 < CH:
            wait_mixed(b + 2)
        if b + 3 < CH:
            pass_mixed(b + 3)
        if b + 1 < CH:
            up_product(b + 1)
            mlp_part(b)
        if 1 <= b < CH - 1:
            ar3.s2(b)
        if b + 2 < CH:
            out_product(b + 2)

    left, right = slice(0, D // 2), slice(D // 2, D)
    s.m1[:, left] = tn(s.active[...], s.dy[:, left]).astype(BF)
    ar3.s2(CH - 1)
    wide(wide_1[:1], "step1")
    s.m1[:, right] = tn(s.active[...], s.dy[:, right]).astype(BF)
    wide(wide_1[1:], "step1")

    def second_back(b):
        ar3.d2(b).wait_recv()
        total = ar3.total(b)
        hat, rstd = moments(s.mid[b])
        s.vec[2:3, :] += 0.5 * jnp.sum(total * hat, axis=0, keepdims=True)
        s.vec[3:4, :] += 0.5 * jnp.sum(total, axis=0, keepdims=True)
        grad = s.dy[ar3.mine(b), :].astype(F32) + norm_back(total * mg, hat, rstd)
        s.gm[b] = grad
        s.gattn[ar3.mine(b), :] = grad.astype(BF)
        ar3.d3(b).start()

    def head_back(grad, which, h, b):
        rows = slice(which * W + h * HD, which * W + (h + 1) * HD)
        hat = s.hat[rows, chunk(b)]
        s.gacc[rows, :] += grad * hat
        grad = grad * gain_col(which, h)
        grad = (
            grad
            - jnp.mean(grad, axis=0, keepdims=True)
            - hat * jnp.mean(grad * hat, axis=0, keepdims=True)
        )
        s.gproj[rows, chunk(b)] = (grad * s.rstd[which * HEADS + h, :, chunk(b)]).astype(BF)

    def attend_back(b):
        ar3.d3(b).wait_recv()
        grad_mixed = nt(s.wo[at(n * W, W, W), :], s.gattn[chunk(b), :])
        if b == CH - 1:
            s.m2[3 * W :, :] = nn(s.mixed[at(n * W, W, W), :], s.gattn[...]).astype(BF)
        pad_row = padded(b)
        wides, pairs, grad_queries = [], [], []
        for h in range(HEADS):
            rows = slice(h * HD, (h + 1) * HD)
            grad_out = grad_mixed[rows].astype(BF).astype(F32)
            inv = s.inv[h, :, chunk(b)]
            delta = jnp.sum(grad_out * s.mixf[rows, chunk(b)], axis=0, keepdims=True)
            scaled = grad_out * inv
            low = delta * inv
            high = low.astype(BF).astype(F32)
            extra = jnp.where(subs == 0, -high, jnp.where(subs == 1, high - low, 0.0))
            wides.append(jnp.concatenate([scaled, extra], axis=0).astype(BF))
            tall = jnp.concatenate([jnp.zeros_like(scaled), scaled], axis=0)
            tall = jnp.transpose(tall).astype(BF)
            pairs.append(jnp.concatenate([s.qn[h, chunk(b), :], tall], axis=0))
            qf, kf, own = self_score(b, h)
            own_prob = jnp.exp2(own) * inv * pad_row
            own_grad = jnp.sum(grad_out * s.vt[rows, chunk(b)].astype(F32), axis=0, keepdims=True)
            own_score = own_prob * (own_grad - delta)
            s.dkx[rows, chunk(b)] = qf * own_score
            s.dvx[rows, chunk(b)] = grad_out * own_prob
            grad_queries.append(kf * own_score)
        tasks = [(h, i) for h in range(HEADS) for i in window(b)]
        products, ahead = {}, 3
        grad_scores = [[] for _ in range(HEADS)]
        for t in range(len(tasks) + ahead):
            if t < len(tasks):
                h, i = tasks[t]
                products[t] = nn(s.vn[h, chunk(i), :], wides[h])
            if t < ahead:
                continue
            h, i = tasks[t - ahead]
            weight = s.wgt[h, units.index((b, i))]
            grad_score = (weight.astype(F32) * products.pop(t - ahead)).astype(BF)
            grad_scores[h].append(grad_score)
            both = nn(jnp.concatenate([grad_score, weight], axis=1), pairs[h])
            if b == max(i - 1, 0):
                s.dkv[h, chunk(i), :] = both
            else:
                s.dkv[h, chunk(i), :] += both
            if i == window(b)[-1]:
                keys = s.kta[h, 0:HD, window(b)[0] * BLK : (i + 1) * BLK]
                grad_queries[h] = grad_queries[h] + nn(
                    keys, jnp.concatenate(grad_scores[h], axis=0)
                )
        for h in range(HEADS):
            head_back(grad_queries[h] * (0.125 / SC), 0, h, b)

    def keys_back(b):
        for h in range(HEADS):
            rows = slice(h * HD, (h + 1) * HD)
            both = jnp.transpose(s.dkv[h, chunk(b), :])
            head_back((both[0:HD] + s.dkx[rows, chunk(b)]) * 0.125, 1, h, b)
            grad_value = both[HD:] + s.dvx[rows, chunk(b)]
            s.gproj[2 * W + h * HD : 2 * W + (h + 1) * HD, chunk(b)] = grad_value.astype(BF)

    def first_part(b):
        s.big0[...] = tn(s.gproj[:, chunk(b)], s.wt[...])
        for i in range(2):
            rows = slice(b * BLK + i * HALF, b * BLK + (i + 1) * HALF)
            part = s.big0[i * HALF : (i + 1) * HALF, :]
            s.p4[rows, :] = part.astype(BF)
            s.vec[0:1, :] += jnp.sum(part * s.hat1[rows, :].astype(F32), axis=0, keepdims=True)
            s.vec[1:2, :] += jnp.sum(part, axis=0, keepdims=True)
        ar4.s1(b)

    second_back(0)
    s.m0[:, left] = tn(s.normed2[...], s.gpre[:, left]).astype(BF)
    wide(wide_2[:1], "step1")
    attend_back(0)
    second_back(1)
    s.m0[:, right] = tn(s.normed2[...], s.gpre[:, right]).astype(BF)
    wide(wide_2[1:], "step1")
    ar2.s2(0)
    attend_back(1)
    keys_back(0)
    second_back(2)
    first_part(0)
    ar2.s2(1)
    attend_back(2)
    keys_back(1)
    wide(wide_1, "step2")
    second_back(3)
    first_part(1)
    attend_back(3)
    keys_back(2)
    keys_back(3)
    ar4.s2(0)
    wide(wide_2, "step2")
    s.m2[0 : 3 * W, left] = nn(s.gproj[...], s.normed[:, left]).astype(BF)
    wide(wide_3[:1], "step1")
    s.m2[0 : 3 * W, right] = nn(s.gproj[...], s.normed[:, right]).astype(BF)
    wide(wide_3[1:], "step1")
    wide(wide_1, "step3")
    first_part(2)
    first_part(3)
    for which in range(2):
        rows = slice(which * W, (which + 1) * W)
        both = s.gacc[rows, 0:128] + s.gacc[rows, 128:256]
        s.vec[4 + which : 5 + which, 0:W] = jnp.sum(jnp.transpose(both), axis=0, keepdims=True)
    s.vecs[...] = s.vec[...]
    vec_c.start()
    wide(wide_2, "step3")
    ar4.s2(1)
    mlp_part(CH - 1)
    ar2.s1(CH - 1)

    def layer_out(b):
        ar2.d2(b).wait_recv()
        s.r22[b] = (s.mid[b] + ar2.total(b)).astype(BF)
        ar2.d3(b).start()
        lo_copy(b).start()

    def grad_tokens(b):
        ar4.d2(b).wait_recv()
        hat, rstd = moments(s.x[ar4.mine(b), :].astype(F32))
        s.r24[b] = (s.gm[b] + norm_back(ar4.total(b) * ag, hat, rstd)).astype(BF)
        ar4.d3(b).start()
        gt_copy(b).start()

    upper = lax.broadcasted_iota(jnp.int32, (8, D), 0) < 4
    vec_c.wait_recv()
    s.v1[...] = s.vec[...] + jnp.where(upper, s.rvz[0], 0.0)
    s.rvx[k.x] = s.v1[...]
    for copy in vec_x:
        copy.start()
    layer_out(0)
    wide(wide_1, "step4")
    wide(wide_2, "step4")
    layer_out(1)
    ar2.s2(2)
    wide(wide_3, "step2")
    for copy in vec_x:
        copy.wait_recv()
    s.v2[...] = (s.rvx[0] + s.rvx[1]) + (s.rvx[2] + s.rvx[3])
    s.rvy[k.y] = s.v2[...]
    for copy in vec_y:
        copy.start()
    wide(wide_1, "step5")
    for d in (1, 3):
        wide(wide_1, "step6", d)
    wide(wide_2, "step5")
    for d in (1, 3):
        wide(wide_2, "step6", d)
    wide(wide_3, "step3")
    for copy in vec_y:
        copy.wait_recv()
    s.v3[...] = (s.rvy[0] + s.rvy[1]) + (s.rvy[2] + s.rvy[3])
    vec_z.start()
    ar4.s2(2)
    ar2.s2(3)
    grad_tokens(0)
    wide(wide_3, "step4")
    wide(wide_1, "step7")
    wide(wide_2, "step7")
    vec_z.wait_recv()
    s.v4[...] = s.v3[...] + s.rvz[1]
    vec_l.start()
    ar4.s2(3)
    grad_tokens(1)
    layer_out(2)
    wide(wide_3, "step5")
    vec_l.wait_recv()
    vec_out[...] = s.v4[...] + jnp.where(upper, s.rvz[2], 0.0)
    grad_tokens(2)
    layer_out(3)
    grad_tokens(3)

    for b in range(CH):
        ar2.d3(b).wait_recv()
        ar4.d3(b).wait_recv()
        lo_copy(b).wait()
        gt_copy(b).wait()
        mix_mate(b).wait_send()
        mix_z(b).wait_send()
        mix_pass(b).wait_send()
    for item in (ar2, ar3, ar4, *wide_1, *wide_2, *wide_3):
        item.finish()
    for copy in [*wo_sends, wo_pass, *vec_x, *vec_y, vec_z, vec_c, vec_l]:
        copy.wait_send()


PARTS = 4


def finish(lo, gt, gup, gdn, g2, vec, lo_o, gt_o, qkv_o, qg_o, kg_o, out_o, gup_o, gdn_o, ag_o, as_o, mg_o, ms_o, low, high, same, sem_in, sem_out):
    size = D // PARTS
    pieces = []
    for i, (src, dst) in enumerate(((gup, gup_o), (gdn, gdn_o), (g2, None))):
        for p in range(PARTS):
            rows = pl.ds(p * size, size)
            if dst is None:
                to = qkv_o.at[p] if p < 3 else out_o
            else:
                to = dst.at[rows]
            load = pltpu.make_async_copy(src.at[rows], low.at[i, rows], sem_in.at[i, p])
            pieces.append((load, (i, rows), pltpu.make_async_copy(high.at[i, rows], to, sem_out.at[i, p])))
    for i, (src, dst) in enumerate(((gt, gt_o), (lo, lo_o))):
        load = pltpu.make_async_copy(src, same.at[i], sem_in.at[3 + i, 0])
        store = pltpu.make_async_copy(same.at[i], dst, sem_out.at[3 + i, 0])
        pieces.insert(0, (load, None, store))
    for load, _, _ in pieces:
        load.start()
    for ref, row, count in (
        (ag_o, 0, D),
        (as_o, 1, D),
        (mg_o, 2, D),
        (ms_o, 3, D),
        (qg_o, 4, W),
        (kg_o, 5, W),
    ):
        ref[...] = vec[row : row + 1, 0:count].reshape(count)
    for load, cast, store in pieces:
        load.wait()
        if cast is not None:
            high[cast] = low[cast].astype(F32)
        store.start()
    for _, _, store in pieces:
        store.wait()


def body(*args):
    any_spec = pl.BlockSpec(memory_space=pl.ANY)
    vmem = pl.BlockSpec(memory_space=pltpu.VMEM)
    smem = pl.BlockSpec(memory_space=pltpu.SMEM)
    args = list(args)
    args[4] = jnp.swapaxes(args[4], 1, 2).reshape(3 * W, D)
    out = pl.pallas_call(
        kernel,
        out_shape=(
            jax.ShapeDtypeStruct((T, D), BF),
            jax.ShapeDtypeStruct((T, D), BF),
            jax.ShapeDtypeStruct((D, F), BF),
            jax.ShapeDtypeStruct((F, D), BF),
            jax.ShapeDtypeStruct((4 * W, D), BF),
            jax.ShapeDtypeStruct((8, D), F32),
        ),
        in_specs=[any_spec] * 3 + [smem] + [any_spec] * 10,
        out_specs=(any_spec, any_spec, any_spec, any_spec, any_spec, vmem),
        scratch_shapes=[pltpu.VMEM(shape, dtype) for shape, dtype in SCRATCH.values()]
        + [
            pltpu.SemaphoreType.DMA((NSEM,)),
            pltpu.SemaphoreType.DMA((NSEM,)),
            pltpu.SemaphoreType.DMA((NLOC,)),
        ],
        compiler_params=pltpu.CompilerParams(
            collective_id=0, has_side_effects=True, vmem_limit_bytes=60 * 1024 * 1024
        ),
        cost_estimate=pl.CostEstimate(
            flops=14 * 10**9, bytes_accessed=20 * 2**20, transcendentals=8 * 2**20
        ),
    )(*args)
    layer, tokens, qkv, *rest = pl.pallas_call(
        finish,
        out_shape=(
            jax.ShapeDtypeStruct((T, D), BF),
            jax.ShapeDtypeStruct((T, D), BF),
            jax.ShapeDtypeStruct((3, W, D), F32),
            jax.ShapeDtypeStruct((W,), F32),
            jax.ShapeDtypeStruct((W,), F32),
            jax.ShapeDtypeStruct((W, D), F32),
            jax.ShapeDtypeStruct((D, F), F32),
            jax.ShapeDtypeStruct((F, D), F32),
            jax.ShapeDtypeStruct((D,), F32),
            jax.ShapeDtypeStruct((D,), F32),
            jax.ShapeDtypeStruct((D,), F32),
            jax.ShapeDtypeStruct((D,), F32),
        ),
        in_specs=[any_spec] * 5 + [vmem],
        out_specs=(any_spec, any_spec, any_spec, vmem, vmem, any_spec, any_spec, any_spec)
        + (vmem,) * 4,
        scratch_shapes=[
            pltpu.VMEM((3, D, D), BF),
            pltpu.VMEM((3, D, D), F32),
            pltpu.VMEM((2, T, D), BF),
            pltpu.SemaphoreType.DMA((5, PARTS)),
            pltpu.SemaphoreType.DMA((5, PARTS)),
        ],
        compiler_params=pltpu.CompilerParams(vmem_limit_bytes=60 * 1024 * 1024),
        cost_estimate=pl.CostEstimate(flops=0, bytes_accessed=17 * 2**20, transcendentals=0),
    )(*out)
    return (layer, tokens, jnp.swapaxes(qkv, 1, 2), *rest)


def solution(mesh):
    placed = (
        P("wide", None),
        P("wide", None),
        P("wide", None),
        P("wide"),
        P(None, None, "narrow"),
        P("narrow"),
        P("narrow"),
        P("narrow", None),
        P(None, "narrow"),
        P("narrow", None),
        P(),
        P(),
        P(),
        P(),
    )
    return jax.shard_map(
        body,
        mesh=mesh,
        in_specs=placed,
        out_specs=(
            P("wide", None),
            P("wide", None),
            P(None, None, "narrow"),
            P("narrow"),
            P("narrow"),
            P("narrow", None),
            P(None, "narrow"),
            P("narrow", None),
            P(),
            P(),
            P(),
            P(),
        ),
        check_vma=False,
    )
```

```python
import jax
import jax.numpy as jnp
from jax import lax
from jax.experimental import pallas as pl
from jax.experimental.pallas import tpu as pltpu
from jax.sharding import PartitionSpec as P

T = 1024
D = 768
HEADS = 3
HD = 64
W = HEADS * HD
F = 768
BLK = 256
CH = T // BLK
HALF = BLK // 2
BIG = 512.0
MINUS = 31
LOG2E = 1.4426950408889634
SC = 0.125 * LOG2E
EPS = 1e-06
GELU_A = 0.7978845608028654
GELU_B = 0.044715 * GELU_A

BF = jnp.bfloat16
F32 = jnp.float32
MESH = pl.DeviceIdType.MESH


def nn(a, b):
    return lax.dot_general(a, b, (((1,), (0,)), ((), ())), preferred_element_type=F32)


def nt(a, b):
    return lax.dot_general(a, b, (((1,), (1,)), ((), ())), preferred_element_type=F32)


def tn(a, b):
    return lax.dot_general(a, b, (((0,), (0,)), ((), ())), preferred_element_type=F32)


def at(start, size, unit):
    return pl.ds(pl.multiple_of(start, unit), size)


def chunk(b):
    return at(b * BLK, BLK, BLK)


def moments(values):
    centre = values - jnp.mean(values, axis=-1, keepdims=True)
    rstd = lax.rsqrt(jnp.mean(centre * centre, axis=-1, keepdims=True) + EPS)
    return centre * rstd, rstd


def norm_back(grad, hat, rstd):
    return rstd * (
        grad
        - jnp.mean(grad, axis=-1, keepdims=True)
        - hat * jnp.mean(grad * hat, axis=-1, keepdims=True)
    )


SCRATCH = dict(
    seg=((1, T), jnp.int32),
    qg=((W,), F32),
    kg=((W,), F32),
    ag=((D,), F32),
    ash=((D,), F32),
    mg=((D,), F32),
    msh=((D,), F32),
    x=((T, D), BF),
    dy=((T, D), BF),
    wt=((3 * W, D), BF),
    wo=((4 * W, D), BF),
    up=((D, F), BF),
    dn=((F, D), BF),
    normed=((T, D), BF),
    hat1=((T, D), BF),
    qta=((HEADS, 2 * HD, T), BF),
    kta=((HEADS, 2 * HD, T), BF),
    vt=((W, T), BF),
    qn=((HEADS, T, 2 * HD), BF),
    kn=((HEADS, T, 2 * HD), BF),
    vn=((HEADS, T, 2 * HD), BF),
    hat=((2 * W, T), F32),
    rstd=((6, 1, T), F32),
    gcol=((2 * W, 128), F32),
    mixed=((4 * W, T), BF),
    mixf=((W, T), F32),
    mid=((CH, HALF, D), F32),
    wgt=((HEADS, 10, BLK, BLK), BF),
    inv=((HEADS, 1, T), F32),
    normed2=((T, D), BF),
    active=((T, F), BF),
    gpre=((T, F), BF),
    big0=((BLK, D), F32),
    gact=((T, F), F32),
    n2s=((T, D), BF),
    r12s=((CH, HALF, D), BF),
    big1=((BLK, D), F32),
    p2=((T, D), BF),
    p3=((T, D), BF),
    p4=((T, D), BF),
    r12=((CH, HALF, D), BF),
    r13=((CH, HALF, D), BF),
    r14=((CH, HALF, D), BF),
    r22=((CH, HALF, D), BF),
    r23=((CH, HALF, D), BF),
    r24=((CH, HALF, D), BF),
    gattn=((T, D), BF),
    dkx=((W, T), F32),
    dvx=((W, T), F32),
    gproj=((3 * W, T), BF),
    gacc=((2 * W, BLK), F32),
    m0=((D, F), BF),
    m1=((F, D), BF),
    m2=((4 * W, D), BF),
    vec=((8, D), F32),
    vecs=((8, D), F32),
    rvx=((4, 8, D), F32),
    rvy=((4, 8, D), F32),
    rvz=((3, 8, D), F32),
    v1=((8, D), F32),
    v2=((8, D), F32),
    v3=((8, D), F32),
    v4=((8, D), F32),
)
SIDE = 2
RELAYED = "abcd"
for _s, _w in ((_c, D // 2) for _c in "abcdef"):
    SCRATCH["rs1" + _s] = ((4, 96, _w), BF)
    SCRATCH["ra" + _s] = ((2, 96, _w), BF)
    SCRATCH["rb" + _s] = ((2, 96, _w), BF)
    SCRATCH["s1" + _s] = ((192, _w), BF)
    SCRATCH["rs2" + _s] = ((3, 48, _w), BF)
    SCRATCH["s2" + _s] = ((48, _w), BF)
    SCRATCH["rz" + _s] = ((48, _w), BF)
    SCRATCH["rr" + _s] = ((192, _w), BF)
    if _s in RELAYED:
        SCRATCH["nb" + _s] = ((2, 192, _w), BF)

NSEND, NRECV, NLOC = 29, 101, 24


class Wide:
    def __init__(self, k, name, mat, cols, out, first, second):
        self.k, self.s, self.mat, self.cols, self.out = k, k.s, mat, cols, out
        self.name = name
        self.first, self.second = first, second
        self.u, self.t = k.coord(first), k.coord(second)
        self.relayed = name in RELAYED
        self.send = k.sends(3)
        self.recv = k.recvs(7 if self.relayed else 8)
        self.local = k.locals(1)

    def ref(self, what):
        return getattr(self.s, what + self.name)

    def half(self, q, i):
        return at(lax.rem(self.u + q + 4, 4) * 192 + i * 96, 96, 96)

    def rs1(self, i):
        k = self.k
        if i < 4:
            q, part = ((2, 0), (2, 1), (1, 1), (-1, 0))[i]
            src = self.mat.at[self.half(q, part), self.cols]
        else:
            src = self.ref("rb").at[i - 4]
        dst = self.ref("ra").at[i] if i < 2 else self.ref("rs1").at[i - 2]
        return k.remote(
            src,
            dst,
            self.send,
            self.recv + (0 if i < 2 else 1),
            k.along(self.first, 1 if i % 2 == 0 else 3),
        )

    def rs2(self, d):
        k = self.k
        q = lax.rem(self.t + d, 4)
        return k.remote(
            self.ref("s1").at[at(q * 48, 48, 48)],
            self.ref("rs2").at[d - 1],
            self.send + 1,
            self.recv + 2,
            k.along(self.second, d),
        )

    def zz(self):
        return self.k.remote(self.ref("s2"), self.ref("rz"), self.send + 1, self.recv + 3, self.k.zhi)

    def ag2(self, d):
        piece = self.ref("rr").at[at(self.t * 48, 48, 48)]
        recv = self.recv + 4 + (0 if self.relayed else d - 1)
        return self.k.remote(piece, piece, self.send + 1, recv, self.k.along(self.second, d))

    def rows_out(self, u, start=0, size=192):
        return self.out.at[at(lax.rem(u + 4, 4) * 192 + start, size, 96), self.cols]

    def ag1(self, d):
        dst = self.ref("nb").at[0 if d == 1 else 1]
        return self.k.remote(
            self.ref("rr"), dst, self.send + 2, self.recv + 5, self.k.along(self.first, d)
        )

    def piece(self, d, e):
        start = lax.rem(self.t + 4 - e, 4) * 48
        return self.k.remote(
            self.ref("rr").at[at(start, 48, 48)],
            self.out.at[at(self.u * 192 + start, 48, 48), self.cols],
            self.send + 2,
            self.recv + 7,
            self.k.along(self.first, d),
        )

    def forward(self, d):
        u, start = (self.u - 1, 0) if d == 1 else (self.u + 1, 96)
        src = self.ref("nb").at[0 if d == 1 else 1, pl.ds(start, 96)]
        return self.k.remote(
            src,
            self.rows_out(u, start, 96),
            self.send + 2,
            self.recv + 6,
            self.k.along(self.first, d),
        )

    def own(self, i=0):
        if i == 0:
            return self.k.copy(self.ref("rr"), self.rows_out(self.u), self.local)
        u = self.u - 1 if i == 1 else self.u + 1
        return self.k.copy(self.ref("nb").at[i - 1], self.rows_out(u), self.local)

    def step1(self):
        for i in range(4):
            self.rs1(i).start()

    def step1b(self):
        self.k.await_recvs(self.ref("ra"), self.recv)
        for i, (q, part) in enumerate(((1, 0), (-1, 1))):
            own = self.mat[self.half(q, part), self.cols].astype(F32)
            self.ref("rb")[i] = (own + self.ref("ra")[i].astype(F32)).astype(BF)
            self.rs1(4 + i).start()

    def step2(self):
        self.k.await_recvs(self.ref("rs1"), self.recv + 1)
        rs1, s1 = self.ref("rs1"), self.ref("s1")
        for i, (one, two) in enumerate(((1, 2), (0, 3))):
            total = self.mat[self.half(0, i), self.cols].astype(F32)
            total = total + (rs1[one].astype(F32) + rs1[two].astype(F32))
            s1[i * 96 : (i + 1) * 96, :] = total.astype(BF)
        for d in (2, 1, 3):
            self.rs2(d).start()

    def step3(self):
        self.k.await_recvs(self.ref("rs2"), self.recv + 2)
        total = self.ref("s1")[at(self.t * 48, 48, 48), :].astype(F32)
        for d in range(3):
            total = total + self.ref("rs2")[d].astype(F32)
        self.ref("s2")[...] = total.astype(BF)
        self.zz().start()

    def step4(self):
        self.zz().wait_recv()
        total = self.ref("s2")[...].astype(F32) + self.ref("rz")[...].astype(F32)
        self.ref("rr")[at(self.t * 48, 48, 48), :] = total.astype(BF)
        for d in (2, 1, 3):
            self.ag2(d).start()
        if not self.relayed:
            for d in (2, 1, 3):
                self.piece(d, 0).start()

    def step5(self):
        if self.relayed:
            self.k.await_recvs(self.ref("rr").at[pl.ds(0, 144)], self.recv + 4)
        else:
            for e in (1, 3, 2):
                self.ag2(e).wait_recv()
                for d in (2, 1, 3):
                    self.piece(d, e).start()
        self.own().start()

    def step6(self, d):
        self.ag1(d).start()

    def step7(self):
        self.k.await_recvs(self.ref("nb"), self.recv + 5)
        for d in (1, 3):
            self.forward(d).start()
        for i in (1, 2):
            self.own(i).start()

    def finish(self):
        k = self.k
        some, most = (pl.ds(0, 336), self.cols), (pl.ds(0, 576), self.cols)
        if self.relayed:
            k.await_recvs(self.out.at[pl.ds(0, 192), self.cols], self.recv + 6)
            k.copy(self.mat.at[most], self.out.at[most], self.local).wait()
        else:
            k.await_recvs(self.out.at[most], self.recv + 7)
            self.own().wait()
        k.await_sends(self.mat.at[most], self.send)
        k.await_sends(self.mat.at[some], self.send + 1)
        k.await_sends(self.mat.at[most], self.send + 2)


class Narrow:
    def __init__(self, k, part, r1, r2, result, joint=True, side=None):
        self.k, self.part, self.r1, self.r2, self.result = k, part, r1, r2, result
        self.side = side
        self.joint = joint
        self.send = k.sends(2 if side is None else 3)
        self.recv = k.recvs((2 * CH + 1 if joint else 3 * CH) + (0 if side is None else CH - SIDE))

    def mine(self, b):
        return at(b * BLK + self.k.core * HALF, HALF, HALF)

    def theirs(self, b):
        return at(b * BLK + (1 - self.k.core) * HALF, HALF, HALF)

    def d1(self, b):
        return self.k.remote(
            self.part.at[self.theirs(b)], self.r1.at[b], self.send, self.recv + b, self.k.mate
        )

    def d2(self, b):
        if self.side is None or b < SIDE:
            src, device = self.part, self.k.zlo
        else:
            src, device = self.side[0], self.k.side
        return self.k.remote(
            src.at[self.mine(b)], self.r2.at[b], self.send, self.recv + CH + b, device
        )

    def d3(self, b):
        src, dst = self.result(b, self.mine(b))
        recv = self.recv + 2 * CH + (0 if self.joint else b)
        return self.k.remote(src, dst, self.send + 1, recv, self.k.mate)

    def s1(self, b):
        self.d1(b).start()

    def s2(self, b):
        self.d1(b).wait_recv()
        total = self.part[self.mine(b), :].astype(F32) + self.r1[b].astype(F32)
        self.part[self.mine(b), :] = total.astype(BF)
        if self.side is None or b < SIDE:
            self.d2(b).start()

    def d1_side(self, b):
        part, r1 = self.side
        return self.k.remote(
            part.at[self.theirs(b)],
            r1.at[b],
            self.send + 2,
            self.recv + 2 * CH + 1 + b - SIDE,
            self.k.mate,
        )

    def s2_side(self, b):
        part, r1 = self.side
        self.d1_side(b).wait_recv()
        total = part[self.mine(b), :].astype(F32) + r1[b].astype(F32)
        part[self.mine(b), :] = total.astype(BF)
        self.d2(b).start()

    def total(self, b):
        return self.part[self.mine(b), :].astype(F32) + self.r2[b].astype(F32)

    def finish(self):
        k, half = self.k, self.part.at[pl.ds(0, T // 2)]
        if self.joint:
            k.await_recvs(half, self.recv + 2 * CH)
        k.await_sends(self.part, self.send)
        k.await_sends(half, self.send + 1)
        if self.side is not None:
            k.await_sends(self.part.at[pl.ds(0, (CH - SIDE) * HALF)], self.send + 2)


class Names:
    pass


class Kernel:
    def __init__(self, s, send, recv, loc):
        self.s, self.send, self.recv, self.loc = s, send, recv, loc
        self.taken = {}
        w = lax.axis_index("wide")
        n = lax.axis_index("narrow")
        self.w, self.n = w, n
        self.x = lax.rem(w, 4)
        self.y = lax.rem(lax.div(w, 4), 4)
        self.z = lax.div(w, 16)
        self.core = lax.rem(n, 2)
        self.n1 = n + 1 - 2 * self.core
        self.n2 = lax.rem(n + 2, 4)
        self.mate = (w, self.n1)
        self.zlo = (w, self.n2)
        self.zhi = (lax.rem(w + 16, 32), n)
        self.side = (lax.rem(w + 16, 32), self.n2)

    def coord(self, axis):
        return self.x if axis == "x" else self.y

    def along(self, axis, d):
        if axis == "x":
            return (self.w - self.x + lax.rem(self.x + d, 4), self.n)
        return (self.w - 4 * self.y + 4 * lax.rem(self.y + d, 4), self.n)

    def take(self, kind, count, most):
        start = self.taken.get(kind, 0)
        self.taken[kind] = start + count
        assert start + count <= most, (kind, start + count, most)
        return start

    def sends(self, count):
        return self.take("send", count, NSEND)

    def recvs(self, count):
        return self.take("recv", count, NRECV)

    def locals(self, count):
        return self.take("local", count, NLOC)

    def remote(self, src, dst, send, recv, device):
        return pltpu.make_async_remote_copy(
            src_ref=src,
            dst_ref=dst,
            send_sem=self.send.at[send],
            recv_sem=self.recv.at[recv],
            device_id=device,
            device_id_type=MESH,
        )

    def await_sends(self, ref, send):
        self.remote(ref, ref, send, 0, self.mate).wait_send()

    def await_recvs(self, ref, recv):
        self.remote(ref, ref, 0, recv, self.mate).wait_recv()

    def copy(self, src, dst, sem):
        return pltpu.make_async_copy(src, dst, self.loc.at[sem])


def kernel(
    x_in,
    dy_in,
    seg_in,
    pad_in,
    wt_in,
    qg_in,
    kg_in,
    wo_in,
    up_in,
    dn_in,
    ag_in,
    as_in,
    mg_in,
    ms_in,
    lo_out,
    gt_out,
    gup_out,
    gdn_out,
    g2_out,
    vec_out,
    *scratch,
):
    s = Names()
    for name, ref in zip(SCRATCH, scratch):
        setattr(s, name, ref)
    k = Kernel(s, *scratch[len(SCRATCH) :])
    n, core = k.n, k.core

    own_wo = s.wo.at[at(n * W, W, W)]
    pieces = [pl.ds(b * BLK, BLK) for b in range(CH)]
    loads = [
        (x_in.at[pieces[0]], s.x.at[pieces[0]]),
        (wt_in, s.wt),
        (wo_in, own_wo),
        *[(x_in.at[rows], s.x.at[rows]) for rows in pieces[1:]],
        (up_in, s.up),
        (dn_in, s.dn),
        (dy_in, s.dy),
    ]
    load_sem = k.locals(len(loads))
    loads = [k.copy(src, dst, load_sem + i) for i, (src, dst) in enumerate(loads)]
    smalls = [
        (ag_in, s.ag),
        (as_in, s.ash),
        (qg_in, s.qg),
        (kg_in, s.kg),
        (seg_in, s.seg),
        (mg_in, s.mg),
        (ms_in, s.msh),
    ]
    small_sem = k.locals(len(smalls))
    smalls = [k.copy(src, dst, small_sem + i) for i, (src, dst) in enumerate(smalls)]
    loads[0].start()
    for load in smalls + loads[1:6]:
        load.start()
    load_x, load_w, load_wo, *load_rest, load_up, load_dn, load_dy = loads

    barrier = pltpu.get_barrier_semaphore()
    peers = [k.mate, k.zlo, k.zhi, k.side]
    peers += [k.along(axis, d) for axis in "xy" for d in (1, 2, 3)]
    for peer in peers:
        pl.semaphore_signal(barrier, inc=1, device_id=peer, device_id_type=MESH)

    wo_send, wo_recv = k.sends(1), k.recvs(4)
    own_low = s.wo.at[at(n * W, W // 3, W // 3)]
    own_high = s.wo.at[at(n * W + W // 3, 2 * W // 3, W // 3)]
    other_wo = s.wo.at[at(k.n2 * W, W, W)]
    wo_sends = [
        k.remote(own_wo, own_wo, wo_send, wo_recv, k.mate),
        k.remote(own_low, own_low, wo_send, wo_recv + 1, k.zlo),
        k.remote(own_high, own_high, wo_send, wo_recv + 2, k.side),
    ]
    wo_pass = k.remote(other_wo, other_wo, wo_send, wo_recv + 3, k.mate)
    mix_send, mix_sem = k.sends(1), k.recvs(3 * CH)

    def mix_mate(b):
        ref = s.mixed.at[at(n * W, W, W), chunk(b)]
        return k.remote(ref, ref, mix_send, mix_sem + b, k.mate)

    def mix_z(b):
        ref = s.mixed.at[at(n * W, W, W), chunk(b)]
        return k.remote(ref, ref, mix_send, mix_sem + CH + b, k.zlo)

    def mix_pass(b):
        ref = s.mixed.at[at(k.n2 * W, W, W), chunk(b)]
        return k.remote(ref, ref, mix_send, mix_sem + 2 * CH + b, k.mate)

    ar2 = Narrow(k, s.p2, s.r12, s.r22, lambda b, rows: (s.r22.at[b], lo_out.at[rows]), side=(s.gpre, s.r12s))
    ar3 = Narrow(k, s.p3, s.r13, s.r23, lambda b, rows: (s.gattn.at[rows], s.gattn.at[rows]), joint=False)
    ar4 = Narrow(k, s.p4, s.r14, s.r24, lambda b, rows: (s.r24.at[b], gt_out.at[rows]))
    low_cols, high_cols = pl.ds(0, D // 2), pl.ds(D // 2, D // 2)
    wide_1 = Wide(k, "a", s.m1, low_cols, gdn_out, "x", "y"), Wide(k, "b", s.m1, high_cols, gdn_out, "y", "x")
    wide_2 = Wide(k, "c", s.m0, low_cols, gup_out, "x", "y"), Wide(k, "d", s.m0, high_cols, gup_out, "y", "x")
    wide_3 = Wide(k, "e", s.m2, low_cols, g2_out, "x", "y"), Wide(k, "f", s.m2, high_cols, g2_out, "y", "x")

    def wide(pair, step, *args):
        for item in pair:
            getattr(item, step)(*args)

    vec_send, vec_sem = k.sends(1), k.recvs(5)
    vec_c = k.remote(s.vecs, s.rvz.at[0], vec_send, vec_sem, k.mate)
    vec_x = [
        k.remote(s.v1, s.rvx.at[k.x], vec_send, vec_sem + 1, k.along("x", d)) for d in (1, 2, 3)
    ]
    vec_y = [
        k.remote(s.v2, s.rvy.at[k.y], vec_send, vec_sem + 2, k.along("y", d)) for d in (1, 2, 3)
    ]
    vec_z = k.remote(s.v3, s.rvz.at[1], vec_send, vec_sem + 3, k.zhi)
    vec_l = k.remote(s.v4, s.rvz.at[2], vec_send, vec_sem + 4, k.zlo)
    out_sem = k.locals(2)

    side_send, side_sem = k.sends(1), k.recvs(2 * (CH - SIDE))

    def side_norm(b):
        rows = ar2.mine(b)
        return k.remote(s.normed2.at[rows], s.n2s.at[rows], side_send, side_sem + b - SIDE, k.side)

    def side_pass(b):
        rows = ar2.mine(b)
        return k.remote(s.n2s.at[rows], s.n2s.at[rows], side_send, side_sem + CH - SIDE + b - SIDE, k.mate)

    def lo_copy(b):
        return k.copy(s.r22.at[b], lo_out.at[ar2.mine(b)], out_sem)

    def gt_copy(b):
        return k.copy(s.r24.at[b], gt_out.at[ar4.mine(b)], out_sem + 1)


    limit = T - pad_in[0]

    for load in smalls:
        load.wait()
    load_x.wait()

    ag = s.ag[...].reshape(1, D)
    ash = s.ash[...].reshape(1, D)
    mg = s.mg[...].reshape(1, D)
    msh = s.msh[...].reshape(1, D)

    def gain_col(c, h):
        col = s.gcol[c * W + h * HD : c * W + (h + 1) * HD, :]
        return jnp.concatenate([col, col], axis=1)

    lanes = lax.broadcasted_iota(jnp.int32, (1, BLK), 1)
    subs = lax.broadcasted_iota(jnp.int32, (HD, BLK), 0)

    def padded(b):
        return jnp.where(lanes + b * BLK >= limit, 1.0, 0.0)

    def first_norm(b):
        for i in range(2):
            rows = slice(b * BLK + i * HALF, b * BLK + (i + 1) * HALF)
            hat, _ = moments(s.x[rows, :].astype(F32))
            s.hat1[rows, :] = hat.astype(BF)
            s.normed[rows, :] = (hat * ag + ash).astype(BF)

    def project(b):
        raw = nt(s.wt[...], s.normed[chunk(b), :])
        if b + 1 < CH:
            first_norm(b + 1)
        same = jnp.where(subs == s.seg[:, chunk(b)], 1.0, 0.0)
        same_valid = same * (1.0 - padded(b))
        query_rows = jnp.where(subs == MINUS, -BIG, BIG * same)
        key_rows = jnp.where(subs == MINUS, 1.0, same_valid)
        ones = jnp.where(subs < 2, 1.0, 0.0)
        for h in range(HEADS):
            for which in range(2):
                rows = slice(which * W + h * HD, which * W + (h + 1) * HD)
                value = raw[rows]
                centre = value - jnp.mean(value, axis=0, keepdims=True)
                rstd = lax.rsqrt(jnp.mean(centre * centre, axis=0, keepdims=True) + EPS)
                hat = centre * rstd
                s.hat[rows, chunk(b)] = hat
                s.rstd[which * HEADS + h, :, chunk(b)] = rstd
                value = hat * gain_col(which, h) * (1.0, SC)[which]
                both = jnp.concatenate([value, (query_rows, key_rows)[which]], axis=0)
                if which == 0:
                    s.qta[h, :, chunk(b)] = both.astype(BF)
                    tall = jnp.concatenate([value, jnp.zeros_like(value)], axis=0)
                    s.qn[h, chunk(b), :] = jnp.transpose(tall).astype(BF)
                else:
                    s.kta[h, :, chunk(b)] = both.astype(BF)
                    s.kn[h, chunk(b), :] = jnp.transpose(both).astype(BF)
            value = raw[2 * W + h * HD : 2 * W + (h + 1) * HD]
            s.vt[h * HD : (h + 1) * HD, chunk(b)] = value.astype(BF)
            s.vn[h, chunk(b), :] = jnp.transpose(jnp.concatenate([value, ones], axis=0)).astype(BF)

    first_norm(0)
    load_wo.wait()
    pl.semaphore_wait(barrier, len(peers))
    for copy in wo_sends:
        copy.start()
    s.vec[...] = jnp.zeros_like(s.vec)
    s.gacc[...] = jnp.zeros_like(s.gacc)
    s.gcol[0:W, :] = jnp.transpose(jnp.broadcast_to(s.qg[...].reshape(1, W), (128, W)))
    s.gcol[W:, :] = jnp.transpose(jnp.broadcast_to(s.kg[...].reshape(1, W), (128, W)))
    def window(b):
        return range(max(b - 1, 0), min(b + 2, CH))

    def self_score(b, h):
        query = s.qta[h, 0:HD, chunk(b)].astype(F32)
        key = s.kta[h, 0:HD, chunk(b)].astype(F32)
        return query, key, jnp.sum(query * key, axis=0, keepdims=True)

    units = [(b, i) for b in range(CH) for i in window(b)]

    def attend(b):
        pad_row = padded(b)
        pairs = [(h, i) for h in range(HEADS) for i in window(b)]
        scores = [nn(s.kn[h, chunk(i), :], s.qta[h, :, chunk(b)]) for h, i in pairs]
        totals, outs = [], []
        for h in range(HEADS):
            own = jnp.exp2(self_score(b, h)[2]) * pad_row
            totals.append(own)
            outs.append(s.vt[h * HD : (h + 1) * HD, chunk(b)].astype(F32) * own)
        for (h, i), score in zip(pairs, scores):
            weight = jnp.exp2(score)
            totals[h] = totals[h] + jnp.sum(weight, axis=0, keepdims=True)
            weight = weight.astype(BF)
            s.wgt[h, units.index((b, i))] = weight
            outs[h] = outs[h] + nn(s.vt[h * HD : (h + 1) * HD, chunk(i)], weight)
        for h in range(HEADS):
            inv = 1.0 / totals[h]
            s.inv[h, :, chunk(b)] = inv
            out = outs[h] * inv
            s.mixf[h * HD : (h + 1) * HD, chunk(b)] = out
            s.mixed[at(n * W + h * HD, HD, HD), chunk(b)] = out.astype(BF)

    def send_mixed(b):
        mix_z(b).start()
        mix_mate(b).start()

    load_w.wait()
    for load in load_rest:
        load.wait()
    for load in loads[6:]:
        load.start()
    for b in range(CH):
        project(b)
    for b in range(CH):
        attend(b)
        send_mixed(b)

    load_dy.wait()
    load_dn.wait()
    s.gact[0 : T // 2, :] = nt(s.dy[0 : T // 2, :], s.dn[...])
    for copy in wo_sends[1:]:
        copy.wait_recv()
    wo_pass.start()
    s.gact[T // 2 :, :] = nt(s.dy[T // 2 :, :], s.dn[...])
    load_up.wait()
    mix_z(0).wait_recv()
    mix_pass(0).start()
    wo_sends[0].wait_recv()
    wo_pass.wait_recv()

    def wait_mixed(b):
        mix_mate(b).wait_recv()
        mix_pass(b).wait_recv()

    def out_product(b):
        s.big0[...] = tn(s.mixed[:, chunk(b)], s.wo[...])

    def pass_mixed(b):
        mix_z(b).wait_recv()
        mix_pass(b).start()

    def second_norm(b):
        for i in range(2):
            rows = slice(b * BLK + i * HALF, b * BLK + (i + 1) * HALF)
            hat, _ = moments(s.x[rows, :].astype(F32) + s.big0[i * HALF : (i + 1) * HALF, :])
            s.normed2[rows, :] = (hat * mg + msh).astype(BF)
        own = s.x[ar3.mine(b), :].astype(F32)
        s.mid[b] = own + s.big0[at(core * HALF, HALF, HALF), :]

    def gelu(b):
        for i in range(BLK // 8):
            out = slice(b * BLK + i * 8, b * BLK + (i + 1) * 8)
            pre = s.big1[i * 8 : (i + 1) * 8, :]
            square = pre * pre
            tanh = jnp.tanh(pre * (GELU_A + GELU_B * square))
            half = 0.5 + 0.5 * tanh
            slope = half + (0.5 * pre) * (1.0 - tanh * tanh) * (GELU_A + 3.0 * GELU_B * square)
            s.active[out, :] = (pre * half).astype(BF)
            s.gpre[out, :] = (s.gact[out, :] * slope).astype(BF)

    def mlp_part(b):
        rows = slice(b * BLK, (b + 1) * BLK)
        s.p2[rows, :] = nn(s.active[rows, :], s.dn[...]).astype(BF)

    def up_product(b):
        s.big1[...] = nn(s.normed2[b * BLK : (b + 1) * BLK, :], s.up[...])

    wait_mixed(0)
    out_product(0)
    pass_mixed(1)
    second_norm(0)
    up_product(0)
    for b in range(CH):
        rows = slice(b * BLK, (b + 1) * BLK)
        gelu(b)
        if b >= 1:
            ar2.s1(b - 1)
        if b == 3:
            ar3.s2(2)
        s.p3[rows, :] = nt(s.gpre[rows, :], s.up[...]).astype(BF)
        if b >= 1 and b + 1 < CH:
            second_norm(b + 1)
            if b + 1 >= SIDE:
                side_norm(b + 1).start()
        ar3.s1(b)
        if b == 0:
            wait_mixed(1)
            out_product(1)
            second_norm(1)
            pass_mixed(2)
            ar3.s2(0)
        if b + 1 < CH:
            up_product(b + 1)
            mlp_part(b)
        if b + 2 < CH:
            wait_mixed(b + 2)
            out_product(b + 2)
        if b + 3 < CH:
            pass_mixed(b + 3)
        if b == 1:
            ar3.s2(1)

    left, right = slice(0, D // 2), slice(D // 2, D)
    s.m1[:, left] = tn(s.active[...], s.dy[:, left]).astype(BF)
    ar3.s2(CH - 1)
    wide(wide_1[:1], "step1")
    s.m1[:, right] = tn(s.active[...], s.dy[:, right]).astype(BF)
    wide(wide_1[1:], "step1")

    def second_back(b):
        ar3.d2(b).wait_recv()
        total = ar3.total(b)
        hat, rstd = moments(s.mid[b])
        s.vec[2:3, :] += 0.5 * jnp.sum(total * hat, axis=0, keepdims=True)
        s.vec[3:4, :] += 0.5 * jnp.sum(total, axis=0, keepdims=True)
        grad = s.dy[ar3.mine(b), :].astype(F32) + norm_back(total * mg, hat, rstd)
        s.gact[b * HALF : (b + 1) * HALF, :] = grad
        s.gattn[ar3.mine(b), :] = grad.astype(BF)
        ar3.d3(b).start()

    def key_sums(h, b):
        col = (b // 2 * HEADS + h) * 2 * HD
        return slice(T // 2 + b % 2 * BLK, T // 2 + (b % 2 + 1) * BLK), slice(col, col + 2 * HD)

    def head_back(grad, which, h, b):
        rows = slice(which * W + h * HD, which * W + (h + 1) * HD)
        hat = s.hat[rows, chunk(b)]
        s.gacc[rows, :] += grad * hat
        grad = grad * gain_col(which, h)
        grad = (
            grad
            - jnp.mean(grad, axis=0, keepdims=True)
            - hat * jnp.mean(grad * hat, axis=0, keepdims=True)
        )
        s.gproj[rows, chunk(b)] = (grad * s.rstd[which * HEADS + h, :, chunk(b)]).astype(BF)

    def attend_back(b):
        ar3.d3(b).wait_recv()
        grad_mixed = nt(s.wo[at(n * W, W, W), :], s.gattn[chunk(b), :])
        if b == CH - 1:
            s.m2[3 * W :, :] = nn(s.mixed[at(n * W, W, W), :], s.gattn[...]).astype(BF)
        pad_row = padded(b)
        wides, pairs, grad_queries = [], [], []
        for h in range(HEADS):
            rows = slice(h * HD, (h + 1) * HD)
            grad_out = grad_mixed[rows].astype(BF).astype(F32)
            inv = s.inv[h, :, chunk(b)]
            delta = jnp.sum(grad_out * s.mixf[rows, chunk(b)], axis=0, keepdims=True)
            scaled = grad_out * inv
            low = delta * inv
            high = low.astype(BF).astype(F32)
            extra = jnp.where(subs == 0, -high, jnp.where(subs == 1, high - low, 0.0))
            wides.append(jnp.concatenate([scaled, extra], axis=0).astype(BF))
            tall = jnp.concatenate([jnp.zeros_like(scaled), scaled], axis=0)
            tall = jnp.transpose(tall).astype(BF)
            pairs.append(jnp.concatenate([s.qn[h, chunk(b), :], tall], axis=0))
            qf, kf, own = self_score(b, h)
            own_prob = jnp.exp2(own) * inv * pad_row
            own_grad = jnp.sum(grad_out * s.vt[rows, chunk(b)].astype(F32), axis=0, keepdims=True)
            own_score = own_prob * (own_grad - delta)
            s.dkx[rows, chunk(b)] = qf * own_score
            s.dvx[rows, chunk(b)] = grad_out * own_prob
            grad_queries.append(kf * own_score)
        tasks = [(h, i) for h in range(HEADS) for i in window(b)]
        products, ahead = {}, 3
        grad_scores = [[] for _ in range(HEADS)]
        for t in range(len(tasks) + ahead):
            if t < len(tasks):
                h, i = tasks[t]
                products[t] = nn(s.vn[h, chunk(i), :], wides[h])
            if t < ahead:
                continue
            h, i = tasks[t - ahead]
            weight = s.wgt[h, units.index((b, i))]
            grad_score = (weight.astype(F32) * products.pop(t - ahead)).astype(BF)
            grad_scores[h].append(grad_score)
            both = nn(jnp.concatenate([grad_score, weight], axis=1), pairs[h])
            if b == max(i - 1, 0):
                s.gact[key_sums(h, i)] = both
            else:
                s.gact[key_sums(h, i)] += both
            if i == window(b)[-1]:
                keys = s.kta[h, 0:HD, window(b)[0] * BLK : (i + 1) * BLK]
                grad_queries[h] = grad_queries[h] + nn(
                    keys, jnp.concatenate(grad_scores[h], axis=0)
                )
        for h in range(HEADS):
            head_back(grad_queries[h] * (0.125 / SC), 0, h, b)

    def keys_back(b):
        for h in range(HEADS):
            rows = slice(h * HD, (h + 1) * HD)
            both = jnp.transpose(s.gact[key_sums(h, b)])
            head_back((both[0:HD] + s.dkx[rows, chunk(b)]) * 0.125, 1, h, b)
            grad_value = both[HD:] + s.dvx[rows, chunk(b)]
            s.gproj[2 * W + h * HD : 2 * W + (h + 1) * HD, chunk(b)] = grad_value.astype(BF)

    def first_part(b):
        s.big0[...] = tn(s.gproj[:, chunk(b)], s.wt[...])
        for i in range(2):
            rows = slice(b * BLK + i * HALF, b * BLK + (i + 1) * HALF)
            part = s.big0[i * HALF : (i + 1) * HALF, :]
            s.p4[rows, :] = part.astype(BF)
            s.vec[0:1, :] += jnp.sum(part * s.hat1[rows, :].astype(F32), axis=0, keepdims=True)
            s.vec[1:2, :] += jnp.sum(part, axis=0, keepdims=True)
        ar4.s1(b)

    def side_mlp(b):
        side_pass(b).wait_recv()
        rows = slice(b * BLK, (b + 1) * BLK)
        s.big0[...] = nn(s.n2s[rows, :], s.up[...])
        for i in range(BLK // 8):
            out = slice(b * BLK + i * 8, b * BLK + (i + 1) * 8)
            pre = s.big0[i * 8 : (i + 1) * 8, :]
            half = 0.5 + 0.5 * jnp.tanh(pre * (GELU_A + GELU_B * (pre * pre)))
            s.active[out, :] = (pre * half).astype(BF)
        s.gpre[rows, :] = nn(s.active[rows, :], s.dn[...]).astype(BF)
        ar2.d1_side(b).start()

    def pass_side(b):
        side_norm(b).wait_recv()
        side_pass(b).start()

    second_back(0)
    s.m0[:, left] = tn(s.normed2[...], s.gpre[:, left]).astype(BF)
    wide(wide_2[:1], "step1")
    attend_back(0)
    second_back(1)
    s.m0[:, right] = tn(s.normed2[...], s.gpre[:, right]).astype(BF)
    wide(wide_1, "step1b")
    wide(wide_2[1:], "step1")
    ar2.s2(0)
    attend_back(1)
    keys_back(0)
    second_back(2)
    first_part(0)
    ar2.s2(1)
    attend_back(2)
    keys_back(1)
    second_back(3)
    wide(wide_2, "step1b")
    wide(wide_1, "step2")
    first_part(1)
    attend_back(3)
    keys_back(2)
    keys_back(3)
    ar4.s2(0)
    s.m2[0 : 3 * W, left] = nn(s.gproj[...], s.normed[:, left]).astype(BF)
    wide(wide_3[:1], "step1")
    wide(wide_2, "step2")
    s.m2[0 : 3 * W, right] = nn(s.gproj[...], s.normed[:, right]).astype(BF)
    wide(wide_3[1:], "step1")
    wide(wide_1, "step3")
    first_part(2)
    first_part(3)
    for which in range(2):
        rows = slice(which * W, (which + 1) * W)
        both = s.gacc[rows, 0:128] + s.gacc[rows, 128:256]
        s.vec[4 + which : 5 + which, 0:W] = jnp.sum(jnp.transpose(both), axis=0, keepdims=True)
    s.vecs[...] = s.vec[...]
    vec_c.start()
    wide(wide_2, "step3")
    ar4.s2(1)
    wide(wide_3, "step1b")
    mlp_part(CH - 1)
    ar2.s1(CH - 1)
    for b in range(SIDE, CH):
        pass_side(b)

    def layer_out(b):
        ar2.d2(b).wait_recv()
        s.r22[b] = (s.mid[b] + ar2.total(b)).astype(BF)
        ar2.d3(b).start()
        lo_copy(b).start()

    def grad_tokens(b):
        ar4.d2(b).wait_recv()
        hat, rstd = moments(s.x[ar4.mine(b), :].astype(F32))
        s.r24[b] = (s.gact[b * HALF : (b + 1) * HALF, :] + norm_back(ar4.total(b) * ag, hat, rstd)).astype(BF)
        ar4.d3(b).start()
        gt_copy(b).start()

    upper = lax.broadcasted_iota(jnp.int32, (8, D), 0) < 4
    vec_c.wait_recv()
    s.v1[...] = s.vec[...] + jnp.where(upper, s.rvz[0], 0.0)
    s.rvx[k.x] = s.v1[...]
    for copy in vec_x:
        copy.start()
    ar4.s2(2)
    wide(wide_1, "step4")
    side_mlp(2)
    wide(wide_2, "step4")
    side_mlp(3)
    ar2.s2_side(2)
    wide(wide_3, "step2")
    k.await_recvs(s.rvx.at[pl.ds(0, 3)], vec_sem + 1)
    s.v2[...] = (s.rvx[0] + s.rvx[1]) + (s.rvx[2] + s.rvx[3])
    s.rvy[k.y] = s.v2[...]
    for copy in vec_y:
        copy.start()
    wide(wide_1, "step5")
    for d in (1, 3):
        wide(wide_1, "step6", d)
    ar2.s2_side(3)
    ar2.s2(2)
    ar2.s2(3)
    layer_out(0)
    wide(wide_2, "step5")
    for d in (1, 3):
        wide(wide_2, "step6", d)
    layer_out(1)
    wide(wide_3, "step3")
    k.await_recvs(s.rvy.at[pl.ds(0, 3)], vec_sem + 2)
    s.v3[...] = (s.rvy[0] + s.rvy[1]) + (s.rvy[2] + s.rvy[3])
    vec_z.start()
    ar4.s2(3)
    grad_tokens(0)
    wide(wide_1, "step7")
    wide(wide_3, "step4")
    wide(wide_2, "step7")
    vec_z.wait_recv()
    s.v4[...] = s.v3[...] + s.rvz[1]
    vec_l.start()
    grad_tokens(1)
    wide(wide_3, "step5")
    layer_out(2)
    grad_tokens(2)
    layer_out(3)
    vec_l.wait_recv()
    vec_out[...] = s.v4[...] + jnp.where(upper, s.rvz[2], 0.0)
    grad_tokens(3)

    half = pl.ds(0, T // 2)
    k.copy(s.p2.at[half], lo_out.at[half], out_sem).wait()
    k.copy(s.p4.at[half], gt_out.at[half], out_sem + 1).wait()
    for item in (ar2, ar3, ar4, *wide_1, *wide_2, *wide_3):
        item.finish()
    k.await_sends(s.wo.at[pl.ds(0, 3 * W)], wo_send)
    k.await_sends(s.mixed.at[pl.ds(0, 3 * W)], mix_send)
    k.await_sends(s.n2s.at[pl.ds(0, (CH - SIDE) * BLK)], side_send)
    k.await_sends(s.big0.at[pl.ds(0, 72)], vec_send)


PARTS = 4


def finish(lo, gt, gup, gdn, g2, vec, lo_o, gt_o, qkv_o, qg_o, kg_o, out_o, gup_o, gdn_o, ag_o, as_o, mg_o, ms_o, low, high, same, sem_in, sem_out):
    size = D // PARTS
    pieces = []
    for i, (src, dst) in enumerate(((gup, gup_o), (gdn, gdn_o), (g2, None))):
        for p in range(PARTS):
            rows = pl.ds(p * size, size)
            if dst is None:
                to = qkv_o.at[p] if p < 3 else out_o
            else:
                to = dst.at[rows]
            load = pltpu.make_async_copy(src.at[rows], low.at[i, rows], sem_in.at[i, p])
            pieces.append((load, (i, rows), pltpu.make_async_copy(high.at[i, rows], to, sem_out.at[i, p])))
    for i, (src, dst) in enumerate(((gt, gt_o), (lo, lo_o))):
        load = pltpu.make_async_copy(src, same.at[i], sem_in.at[3 + i, 0])
        store = pltpu.make_async_copy(same.at[i], dst, sem_out.at[3 + i, 0])
        pieces.insert(0, (load, None, store))
    for load, _, _ in pieces:
        load.start()
    for ref, row, count in (
        (ag_o, 0, D),
        (as_o, 1, D),
        (mg_o, 2, D),
        (ms_o, 3, D),
        (qg_o, 4, W),
        (kg_o, 5, W),
    ):
        ref[...] = vec[row : row + 1, 0:count].reshape(count)
    for load, cast, store in pieces:
        load.wait()
        if cast is not None:
            high[cast] = low[cast].astype(F32)
        store.start()
    for _, _, store in pieces:
        store.wait()


def body(*args):
    any_spec = pl.BlockSpec(memory_space=pl.ANY)
    vmem = pl.BlockSpec(memory_space=pltpu.VMEM)
    smem = pl.BlockSpec(memory_space=pltpu.SMEM)
    args = list(args)
    args[4] = jnp.swapaxes(args[4], 1, 2).reshape(3 * W, D)
    out = pl.pallas_call(
        kernel,
        out_shape=(
            jax.ShapeDtypeStruct((T, D), BF),
            jax.ShapeDtypeStruct((T, D), BF),
            jax.ShapeDtypeStruct((D, F), BF),
            jax.ShapeDtypeStruct((F, D), BF),
            jax.ShapeDtypeStruct((4 * W, D), BF),
            jax.ShapeDtypeStruct((8, D), F32),
        ),
        in_specs=[any_spec] * 3 + [smem] + [any_spec] * 10,
        out_specs=(any_spec, any_spec, any_spec, any_spec, any_spec, vmem),
        scratch_shapes=[pltpu.VMEM(shape, dtype) for shape, dtype in SCRATCH.values()]
        + [
            pltpu.SemaphoreType.DMA((NSEND,)),
            pltpu.SemaphoreType.DMA((NRECV,)),
            pltpu.SemaphoreType.DMA((NLOC,)),
        ],
        compiler_params=pltpu.CompilerParams(
            collective_id=0, has_side_effects=True, vmem_limit_bytes=60 * 1024 * 1024
        ),
        cost_estimate=pl.CostEstimate(
            flops=14 * 10**9, bytes_accessed=20 * 2**20, transcendentals=8 * 2**20
        ),
    )(*args)
    layer, tokens, qkv, *rest = pl.pallas_call(
        finish,
        out_shape=(
            jax.ShapeDtypeStruct((T, D), BF),
            jax.ShapeDtypeStruct((T, D), BF),
            jax.ShapeDtypeStruct((3, W, D), F32),
            jax.ShapeDtypeStruct((W,), F32),
            jax.ShapeDtypeStruct((W,), F32),
            jax.ShapeDtypeStruct((W, D), F32),
            jax.ShapeDtypeStruct((D, F), F32),
            jax.ShapeDtypeStruct((F, D), F32),
            jax.ShapeDtypeStruct((D,), F32),
            jax.ShapeDtypeStruct((D,), F32),
            jax.ShapeDtypeStruct((D,), F32),
            jax.ShapeDtypeStruct((D,), F32),
        ),
        in_specs=[any_spec] * 5 + [vmem],
        out_specs=(any_spec, any_spec, any_spec, vmem, vmem, any_spec, any_spec, any_spec)
        + (vmem,) * 4,
        scratch_shapes=[
            pltpu.VMEM((3, D, D), BF),
            pltpu.VMEM((3, D, D), F32),
            pltpu.VMEM((2, T, D), BF),
            pltpu.SemaphoreType.DMA((5, PARTS)),
            pltpu.SemaphoreType.DMA((5, PARTS)),
        ],
        compiler_params=pltpu.CompilerParams(vmem_limit_bytes=60 * 1024 * 1024),
        cost_estimate=pl.CostEstimate(flops=0, bytes_accessed=17 * 2**20, transcendentals=0),
    )(*out)
    return (layer, tokens, jnp.swapaxes(qkv, 1, 2), *rest)


def solution(mesh):
    placed = (
        P("wide", None),
        P("wide", None),
        P("wide", None),
        P("wide"),
        P(None, None, "narrow"),
        P("narrow"),
        P("narrow"),
        P("narrow", None),
        P(None, "narrow"),
        P("narrow", None),
        P(),
        P(),
        P(),
        P(),
    )
    return jax.shard_map(
        body,
        mesh=mesh,
        in_specs=placed,
        out_specs=(
            P("wide", None),
            P("wide", None),
            P(None, None, "narrow"),
            P("narrow"),
            P("narrow"),
            P("narrow", None),
            P(None, "narrow"),
            P("narrow", None),
            P(),
            P(),
            P(),
            P(),
        ),
        check_vma=False,
    )
```

```python
import jax
import jax.numpy as jnp
from jax import lax
from jax.experimental import pallas as pl
from jax.experimental.pallas import tpu as pltpu
from jax.sharding import PartitionSpec as P

T = 1024
D = 768
HEADS = 3
HD = 64
W = HEADS * HD
F = 768
BLK = 256
CH = T // BLK
HALF = BLK // 2
BIG = 512.0
MINUS = 31
LOG2E = 1.4426950408889634
SC = 0.125 * LOG2E
EPS = 1e-06
GELU_A = 0.7978845608028654
GELU_B = 0.044715 * GELU_A

BF = jnp.bfloat16
F32 = jnp.float32
MESH = pl.DeviceIdType.MESH


def nn(a, b):
    return lax.dot_general(a, b, (((1,), (0,)), ((), ())), preferred_element_type=F32)


def nt(a, b):
    return lax.dot_general(a, b, (((1,), (1,)), ((), ())), preferred_element_type=F32)


def tn(a, b):
    return lax.dot_general(a, b, (((0,), (0,)), ((), ())), preferred_element_type=F32)


def at(start, size, unit):
    return pl.ds(pl.multiple_of(start, unit), size)


def chunk(b):
    return at(b * BLK, BLK, BLK)


def moments(values):
    centre = values - jnp.mean(values, axis=-1, keepdims=True)
    rstd = lax.rsqrt(jnp.mean(centre * centre, axis=-1, keepdims=True) + EPS)
    return centre * rstd, rstd


def norm_back(grad, hat, rstd):
    return rstd * (
        grad
        - jnp.mean(grad, axis=-1, keepdims=True)
        - hat * jnp.mean(grad * hat, axis=-1, keepdims=True)
    )


SCRATCH = dict(
    seg=((1, T), jnp.int32),
    qg=((W,), F32),
    kg=((W,), F32),
    ag=((D,), F32),
    ash=((D,), F32),
    mg=((D,), F32),
    msh=((D,), F32),
    x=((T, D), BF),
    dy=((T, D), BF),
    wt=((3 * W, D), BF),
    wo=((4 * W, D), BF),
    up=((D, F), BF),
    dn=((F, D), BF),
    normed=((T, D), BF),
    hat1=((T, D), BF),
    qta=((HEADS, 2 * HD, T), BF),
    kta=((HEADS, 2 * HD, T), BF),
    vt=((W, T), BF),
    qn=((HEADS, T, 2 * HD), BF),
    kn=((HEADS, T, 2 * HD), BF),
    vn=((HEADS, T, 2 * HD), BF),
    hat=((2 * W, T), F32),
    rstd=((6, 1, T), F32),
    gcol=((2 * W, 128), F32),
    mixed=((4 * W, T), BF),
    mixf=((W, T), F32),
    mid=((CH, HALF, D), F32),
    wgt=((HEADS, 10, BLK, BLK), BF),
    inv=((HEADS, 1, T), F32),
    normed2=((T, D), BF),
    active=((T, F), BF),
    gpre=((T, F), BF),
    big0=((BLK, D), F32),
    gact=((T, F), F32),
    n2s=((T, D), BF),
    r12s=((CH, HALF, D), BF),
    big1=((BLK, D), F32),
    p2=((T, D), BF),
    p3=((T, D), BF),
    p4=((T, D), BF),
    r12=((CH, HALF, D), BF),
    r13=((CH, HALF, D), BF),
    r14=((CH, HALF, D), BF),
    r22=((CH, HALF, D), BF),
    r23=((CH, HALF, D), BF),
    r24=((CH, HALF, D), BF),
    gattn=((T, D), BF),
    dkx=((W, T), F32),
    dvx=((W, T), F32),
    gproj=((3 * W, T), BF),
    gacc=((2 * W, BLK), F32),
    m0=((D, F), BF),
    m1=((F, D), BF),
    m2=((4 * W, D), BF),
    vec=((8, D), F32),
    vecs=((8, D), F32),
    rvx=((4, 8, D), F32),
    rvy=((4, 8, D), F32),
    rvz=((3, 8, D), F32),
    v1=((8, D), F32),
    v2=((8, D), F32),
    v3=((8, D), F32),
    v4=((8, D), F32),
)
SIDE = 2
RELAYED = "abcd"
for _s, _w in ((_c, D // 2) for _c in "abcdef"):
    SCRATCH["rs1" + _s] = ((4, 96, _w), BF)
    SCRATCH["ra" + _s] = ((2, 96, _w), BF)
    SCRATCH["rb" + _s] = ((2, 96, _w), BF)
    SCRATCH["s1" + _s] = ((192, _w), BF)
    SCRATCH["rs2" + _s] = ((3, 48, _w), BF)
    SCRATCH["s2" + _s] = ((48, _w), BF)
    SCRATCH["rz" + _s] = ((48, _w), BF)
    SCRATCH["rr" + _s] = ((192, _w), BF)
    if _s in RELAYED:
        SCRATCH["nb" + _s] = ((2, 192, _w), BF)

NSEND, NRECV, NLOC = 20, 95, 25


class Wide:
    def __init__(self, k, send, name, mat, cols, out, first, second):
        self.k, self.s, self.mat, self.cols, self.out = k, k.s, mat, cols, out
        self.name = name
        self.first, self.second = first, second
        self.u, self.t = k.coord(first), k.coord(second)
        self.relayed = name in RELAYED
        self.send = send
        self.recv = k.recvs(7 if self.relayed else 8)
        self.local = k.locals(1)

    def ref(self, what):
        return getattr(self.s, what + self.name)

    def half(self, q, i):
        return at(lax.rem(self.u + q + 4, 4) * 192 + i * 96, 96, 96)

    def rs1(self, i):
        k = self.k
        if i < 4:
            q, part = ((2, 0), (2, 1), (1, 1), (-1, 0))[i]
            src = self.mat.at[self.half(q, part), self.cols]
        else:
            src = self.ref("rb").at[i - 4]
        dst = self.ref("ra").at[i] if i < 2 else self.ref("rs1").at[i - 2]
        return k.remote(
            src,
            dst,
            self.send,
            self.recv + (0 if i < 2 else 1),
            k.along(self.first, 1 if i % 2 == 0 else 3),
        )

    def rs2(self, d):
        k = self.k
        q = lax.rem(self.t + d, 4)
        return k.remote(
            self.ref("s1").at[at(q * 48, 48, 48)],
            self.ref("rs2").at[d - 1],
            self.send + 1,
            self.recv + 2,
            k.along(self.second, d),
        )

    def zz(self):
        return self.k.remote(self.ref("s2"), self.ref("rz"), self.send + 1, self.recv + 3, self.k.zhi)

    def ag2(self, d):
        piece = self.ref("rr").at[at(self.t * 48, 48, 48)]
        recv = self.recv + 4 + (0 if self.relayed else d - 1)
        return self.k.remote(piece, piece, self.send + 1, recv, self.k.along(self.second, d))

    def rows_out(self, u, start=0, size=192):
        return self.out.at[at(lax.rem(u + 4, 4) * 192 + start, size, 96), self.cols]

    def ag1(self, d):
        dst = self.ref("nb").at[0 if d == 1 else 1]
        return self.k.remote(
            self.ref("rr"), dst, self.send + 2, self.recv + 5, self.k.along(self.first, d)
        )

    def piece(self, d, e):
        start = lax.rem(self.t + 4 - e, 4) * 48
        return self.k.remote(
            self.ref("rr").at[at(start, 48, 48)],
            self.out.at[at(self.u * 192 + start, 48, 48), self.cols],
            self.send + 2,
            self.recv + 7,
            self.k.along(self.first, d),
        )

    def forward(self, d):
        u, start = (self.u - 1, 0) if d == 1 else (self.u + 1, 96)
        src = self.ref("nb").at[0 if d == 1 else 1, pl.ds(start, 96)]
        return self.k.remote(
            src,
            self.rows_out(u, start, 96),
            self.send + 2,
            self.recv + 6,
            self.k.along(self.first, d),
        )

    def own(self, i=0):
        if i == 0:
            return self.k.copy(self.ref("rr"), self.rows_out(self.u), self.local)
        u = self.u - 1 if i == 1 else self.u + 1
        return self.k.copy(self.ref("nb").at[i - 1], self.rows_out(u), self.local)

    def step1(self):
        for i in range(4):
            self.rs1(i).start()

    def step1b(self):
        self.k.await_recvs(self.ref("ra"), self.recv)
        for i, (q, part) in enumerate(((1, 0), (-1, 1))):
            own = self.mat[self.half(q, part), self.cols].astype(F32)
            self.ref("rb")[i] = (own + self.ref("ra")[i].astype(F32)).astype(BF)
            self.rs1(4 + i).start()

    def step2(self):
        self.k.await_recvs(self.ref("rs1"), self.recv + 1)
        rs1, s1 = self.ref("rs1"), self.ref("s1")
        for i, (one, two) in enumerate(((1, 2), (0, 3))):
            total = self.mat[self.half(0, i), self.cols].astype(F32)
            total = total + (rs1[one].astype(F32) + rs1[two].astype(F32))
            s1[i * 96 : (i + 1) * 96, :] = total.astype(BF)
        for d in (2, 1, 3):
            self.rs2(d).start()

    def step3(self):
        self.k.await_recvs(self.ref("rs2"), self.recv + 2)
        total = self.ref("s1")[at(self.t * 48, 48, 48), :].astype(F32)
        for d in range(3):
            total = total + self.ref("rs2")[d].astype(F32)
        self.ref("s2")[...] = total.astype(BF)
        self.zz().start()

    def step4(self):
        self.zz().wait_recv()
        total = self.ref("s2")[...].astype(F32) + self.ref("rz")[...].astype(F32)
        self.ref("rr")[at(self.t * 48, 48, 48), :] = total.astype(BF)
        for d in (2, 1, 3):
            self.ag2(d).start()
        if not self.relayed:
            for d in (2, 1, 3):
                self.piece(d, 0).start()

    def step5(self):
        if self.relayed:
            self.k.await_recvs(self.ref("rr").at[pl.ds(0, 144)], self.recv + 4)
        else:
            for e in (1, 3, 2):
                self.ag2(e).wait_recv()
                for d in (2, 1, 3):
                    self.piece(d, e).start()
        self.own().start()

    def step6(self, d):
        self.ag1(d).start()

    def step7(self):
        self.k.await_recvs(self.ref("nb"), self.recv + 5)
        for d in (1, 3):
            self.forward(d).start()
        for i in (1, 2):
            self.own(i).start()

    def finish(self):
        k = self.k
        most = (pl.ds(0, 576), self.cols)
        if self.relayed:
            k.await_recvs(self.out.at[pl.ds(0, 192), self.cols], self.recv + 6)
            k.copy(self.mat.at[most], self.out.at[most], self.local).wait()
        else:
            k.await_recvs(self.out.at[most], self.recv + 7)
            self.own().wait()
        if self.first == "x":
            k.await_sends(self.mat.at[pl.ds(0, 576)], self.send)
            k.await_sends(self.mat.at[pl.ds(0, 336)], self.send + 1)
            k.await_sends(self.mat.at[pl.ds(0, 576)], self.send + 2)


class Narrow:
    def __init__(self, k, part, r1, r2, result, joint=True, side=None):
        self.k, self.part, self.r1, self.r2, self.result = k, part, r1, r2, result
        self.side = side
        self.joint = joint
        self.send = k.sends(2 if side is None else 3)
        self.recv = k.recvs((2 * CH + 1 if joint else 3 * CH) + (0 if side is None else CH - SIDE))

    def mine(self, b):
        return at(b * BLK + self.k.core * HALF, HALF, HALF)

    def theirs(self, b):
        return at(b * BLK + (1 - self.k.core) * HALF, HALF, HALF)

    def d1(self, b):
        return self.k.remote(
            self.part.at[self.theirs(b)], self.r1.at[b], self.send, self.recv + b, self.k.mate
        )

    def d2(self, b):
        if self.side is None or b < SIDE:
            src, device = self.part, self.k.zlo
        else:
            src, device = self.side[0], self.k.side
        return self.k.remote(
            src.at[self.mine(b)], self.r2.at[b], self.send, self.recv + CH + b, device
        )

    def d3(self, b):
        src, dst = self.result(b, self.mine(b))
        recv = self.recv + 2 * CH + (0 if self.joint else b)
        return self.k.remote(src, dst, self.send + 1, recv, self.k.mate)

    def s1(self, b):
        self.d1(b).start()

    def s2(self, b):
        self.d1(b).wait_recv()
        total = self.part[self.mine(b), :].astype(F32) + self.r1[b].astype(F32)
        self.part[self.mine(b), :] = total.astype(BF)
        if self.side is None or b < SIDE:
            self.d2(b).start()

    def d1_side(self, b):
        part, r1 = self.side
        return self.k.remote(
            part.at[self.theirs(b)],
            r1.at[b],
            self.send + 2,
            self.recv + 2 * CH + 1 + b - SIDE,
            self.k.mate,
        )

    def s2_side(self, b):
        part, r1 = self.side
        self.d1_side(b).wait_recv()
        total = part[self.mine(b), :].astype(F32) + r1[b].astype(F32)
        part[self.mine(b), :] = total.astype(BF)
        self.d2(b).start()

    def total(self, b):
        return self.part[self.mine(b), :].astype(F32) + self.r2[b].astype(F32)

    def finish(self):
        k, half = self.k, self.part.at[pl.ds(0, T // 2)]
        if self.joint:
            k.await_recvs(half, self.recv + 2 * CH)
        k.await_sends(self.part, self.send)
        k.await_sends(half, self.send + 1)
        if self.side is not None:
            k.await_sends(self.part.at[pl.ds(0, (CH - SIDE) * HALF)], self.send + 2)


class Names:
    pass


class Kernel:
    def __init__(self, s, send, recv, loc):
        self.s, self.send, self.recv, self.loc = s, send, recv, loc
        self.taken = {}
        w = lax.axis_index("wide")
        n = lax.axis_index("narrow")
        self.w, self.n = w, n
        self.x = lax.rem(w, 4)
        self.y = lax.rem(lax.div(w, 4), 4)
        self.z = lax.div(w, 16)
        self.core = lax.rem(n, 2)
        self.n1 = n + 1 - 2 * self.core
        self.n2 = lax.rem(n + 2, 4)
        self.mate = (w, self.n1)
        self.zlo = (w, self.n2)
        self.zhi = (lax.rem(w + 16, 32), n)
        self.side = (lax.rem(w + 16, 32), self.n2)

    def coord(self, axis):
        return self.x if axis == "x" else self.y

    def along(self, axis, d):
        if axis == "x":
            return (self.w - self.x + lax.rem(self.x + d, 4), self.n)
        return (self.w - 4 * self.y + 4 * lax.rem(self.y + d, 4), self.n)

    def take(self, kind, count, most):
        start = self.taken.get(kind, 0)
        self.taken[kind] = start + count
        assert start + count <= most, (kind, start + count, most)
        return start

    def sends(self, count):
        return self.take("send", count, NSEND)

    def recvs(self, count):
        return self.take("recv", count, NRECV)

    def locals(self, count):
        return self.take("local", count, NLOC)

    def remote(self, src, dst, send, recv, device):
        return pltpu.make_async_remote_copy(
            src_ref=src,
            dst_ref=dst,
            send_sem=self.send.at[send],
            recv_sem=self.recv.at[recv],
            device_id=device,
            device_id_type=MESH,
        )

    def await_sends(self, ref, send):
        self.remote(ref, ref, send, 0, self.mate).wait_send()

    def await_recvs(self, ref, recv):
        self.remote(ref, ref, 0, recv, self.mate).wait_recv()

    def copy(self, src, dst, sem):
        return pltpu.make_async_copy(src, dst, self.loc.at[sem])


def kernel(
    x_in,
    dy_in,
    seg_in,
    pad_in,
    wt_in,
    qg_in,
    kg_in,
    wo_in,
    up_in,
    dn_in,
    ag_in,
    as_in,
    mg_in,
    ms_in,
    lo_out,
    gt_out,
    gup_out,
    gdn_out,
    g2_out,
    vec_out,
    *scratch,
):
    s = Names()
    for name, ref in zip(SCRATCH, scratch):
        setattr(s, name, ref)
    pad_smem, *semaphores = scratch[len(SCRATCH) :]
    k = Kernel(s, *semaphores)
    n, core = k.n, k.core

    own_wo = s.wo.at[at(n * W, W, W)]
    pieces = [pl.ds(b * BLK, BLK) for b in range(CH)]
    loads = [
        (x_in.at[pieces[0]], s.x.at[pieces[0]]),
        (wt_in, s.wt),
        (wo_in, own_wo),
        *[(x_in.at[rows], s.x.at[rows]) for rows in pieces[1:]],
        (up_in, s.up),
        (dn_in, s.dn),
        (dy_in, s.dy),
    ]
    load_sem = k.locals(len(loads))
    loads = [k.copy(src, dst, load_sem + i) for i, (src, dst) in enumerate(loads)]
    smalls = [
        (ag_in, s.ag),
        (as_in, s.ash),
        (qg_in, s.qg),
        (kg_in, s.kg),
        (seg_in, s.seg),
        (pad_in, pad_smem),
        (mg_in, s.mg),
        (ms_in, s.msh),
    ]
    small_sem = k.locals(len(smalls))
    smalls = [k.copy(src, dst, small_sem + i) for i, (src, dst) in enumerate(smalls)]
    loads[0].start()
    for load in smalls + loads[1:6]:
        load.start()
    load_x, load_w, load_wo, *load_rest, load_up, load_dn, load_dy = loads

    barrier = pltpu.get_barrier_semaphore()
    peers = [k.mate, k.zlo, k.zhi, k.side]
    peers += [k.along(axis, d) for axis in "xy" for d in (1, 2, 3)]
    for peer in peers:
        pl.semaphore_signal(barrier, inc=1, device_id=peer, device_id_type=MESH)

    wo_send, wo_recv = k.sends(1), k.recvs(2)
    own_low = s.wo.at[at(n * W, W // 3, W // 3)]
    own_high = s.wo.at[at(n * W + W // 3, 2 * W // 3, W // 3)]
    other_wo = s.wo.at[at(k.n2 * W, W, W)]
    wo_sends = [
        k.remote(own_wo, own_wo, wo_send, wo_recv, k.mate),
        k.remote(own_low, own_low, wo_send, wo_recv + 1, k.zlo),
        k.remote(own_high, own_high, wo_send, wo_recv + 1, k.side),
    ]
    wo_pass = k.remote(other_wo, other_wo, wo_send, wo_recv, k.mate)
    mix_send, mix_sem = k.sends(1), k.recvs(2 * CH)

    def mix_mate(b):
        ref = s.mixed.at[at(n * W, W, W), chunk(b)]
        return k.remote(ref, ref, mix_send, mix_sem + b, k.mate)

    def mix_z(b):
        ref = s.mixed.at[at(n * W, W, W), chunk(b)]
        return k.remote(ref, ref, mix_send, mix_sem + CH + b, k.zlo)

    def mix_pass(b):
        ref = s.mixed.at[at(k.n2 * W, W, W), chunk(b)]
        return k.remote(ref, ref, mix_send, mix_sem + b, k.mate)

    ar2 = Narrow(k, s.p2, s.r12, s.r22, lambda b, rows: (s.r22.at[b], lo_out.at[rows]), side=(s.gpre, s.r12s))
    ar3 = Narrow(k, s.p3, s.r13, s.r23, lambda b, rows: (s.gattn.at[rows], s.gattn.at[rows]), joint=False)
    ar4 = Narrow(k, s.p4, s.r14, s.r24, lambda b, rows: (s.r24.at[b], gt_out.at[rows]))
    low_cols, high_cols = pl.ds(0, D // 2), pl.ds(D // 2, D // 2)
    wide_sends = [k.sends(3) for _ in range(3)]
    wide_1 = Wide(k, wide_sends[0], "a", s.m1, low_cols, gdn_out, "x", "y"), Wide(k, wide_sends[0], "b", s.m1, high_cols, gdn_out, "y", "x")
    wide_2 = Wide(k, wide_sends[1], "c", s.m0, low_cols, gup_out, "x", "y"), Wide(k, wide_sends[1], "d", s.m0, high_cols, gup_out, "y", "x")
    wide_3 = Wide(k, wide_sends[2], "e", s.m2, low_cols, g2_out, "x", "y"), Wide(k, wide_sends[2], "f", s.m2, high_cols, g2_out, "y", "x")

    def wide(pair, step, *args):
        for item in pair:
            getattr(item, step)(*args)

    vec_send, vec_sem = k.sends(1), k.recvs(5)
    vec_c = k.remote(s.vecs, s.rvz.at[0], vec_send, vec_sem, k.mate)
    vec_x = [
        k.remote(s.v1, s.rvx.at[k.x], vec_send, vec_sem + 1, k.along("x", d)) for d in (1, 2, 3)
    ]
    vec_y = [
        k.remote(s.v2, s.rvy.at[k.y], vec_send, vec_sem + 2, k.along("y", d)) for d in (1, 2, 3)
    ]
    vec_z = k.remote(s.v3, s.rvz.at[1], vec_send, vec_sem + 3, k.zhi)
    vec_l = k.remote(s.v4, s.rvz.at[2], vec_send, vec_sem + 4, k.zlo)
    out_sem = k.locals(2)

    side_send, side_sem = k.sends(1), k.recvs(2 * (CH - SIDE))

    def side_norm(b):
        rows = ar2.mine(b)
        return k.remote(s.normed2.at[rows], s.n2s.at[rows], side_send, side_sem + b - SIDE, k.side)

    def side_pass(b):
        rows = ar2.mine(b)
        return k.remote(s.n2s.at[rows], s.n2s.at[rows], side_send, side_sem + CH - SIDE + b - SIDE, k.mate)

    def lo_copy(b):
        return k.copy(s.r22.at[b], lo_out.at[ar2.mine(b)], out_sem)

    def gt_copy(b):
        return k.copy(s.r24.at[b], gt_out.at[ar4.mine(b)], out_sem + 1)


    for load in smalls:
        load.wait()
    load_x.wait()

    ag = s.ag[...].reshape(1, D)
    ash = s.ash[...].reshape(1, D)
    mg = s.mg[...].reshape(1, D)
    msh = s.msh[...].reshape(1, D)

    def gain_col(c, h):
        col = s.gcol[c * W + h * HD : c * W + (h + 1) * HD, :]
        return jnp.concatenate([col, col], axis=1)

    lanes = lax.broadcasted_iota(jnp.int32, (1, BLK), 1)
    subs = lax.broadcasted_iota(jnp.int32, (HD, BLK), 0)

    limit = T - pad_smem[0]

    def padded(b):
        return jnp.where(lanes + b * BLK >= limit, 1.0, 0.0)

    def first_norm(b):
        for i in range(2):
            rows = slice(b * BLK + i * HALF, b * BLK + (i + 1) * HALF)
            hat, _ = moments(s.x[rows, :].astype(F32))
            s.hat1[rows, :] = hat.astype(BF)
            s.normed[rows, :] = (hat * ag + ash).astype(BF)

    def project(b):
        raw = nt(s.wt[...], s.normed[chunk(b), :])
        if b + 1 < CH:
            first_norm(b + 1)
        same = jnp.where(subs == s.seg[:, chunk(b)], 1.0, 0.0)
        same_valid = same * (1.0 - padded(b))
        query_rows = jnp.where(subs == MINUS, -BIG, BIG * same)
        key_rows = jnp.where(subs == MINUS, 1.0, same_valid)
        ones = jnp.where(subs < 2, 1.0, 0.0)
        for h in range(HEADS):
            for which in range(2):
                rows = slice(which * W + h * HD, which * W + (h + 1) * HD)
                value = raw[rows]
                centre = value - jnp.mean(value, axis=0, keepdims=True)
                rstd = lax.rsqrt(jnp.mean(centre * centre, axis=0, keepdims=True) + EPS)
                hat = centre * rstd
                s.hat[rows, chunk(b)] = hat
                s.rstd[which * HEADS + h, :, chunk(b)] = rstd
                value = hat * gain_col(which, h) * (1.0, SC)[which]
                both = jnp.concatenate([value, (query_rows, key_rows)[which]], axis=0)
                if which == 0:
                    s.qta[h, :, chunk(b)] = both.astype(BF)
                    tall = jnp.concatenate([value, jnp.zeros_like(value)], axis=0)
                    s.qn[h, chunk(b), :] = jnp.transpose(tall).astype(BF)
                else:
                    s.kta[h, :, chunk(b)] = both.astype(BF)
                    s.kn[h, chunk(b), :] = jnp.transpose(both).astype(BF)
            value = raw[2 * W + h * HD : 2 * W + (h + 1) * HD]
            s.vt[h * HD : (h + 1) * HD, chunk(b)] = value.astype(BF)
            s.vn[h, chunk(b), :] = jnp.transpose(jnp.concatenate([value, ones], axis=0)).astype(BF)

    first_norm(0)
    load_wo.wait()
    pl.semaphore_wait(barrier, len(peers))
    for copy in wo_sends:
        copy.start()
    s.vec[...] = jnp.zeros_like(s.vec)
    s.gacc[...] = jnp.zeros_like(s.gacc)
    s.gcol[0:W, :] = jnp.transpose(jnp.broadcast_to(s.qg[...].reshape(1, W), (128, W)))
    s.gcol[W:, :] = jnp.transpose(jnp.broadcast_to(s.kg[...].reshape(1, W), (128, W)))
    def window(b):
        return range(max(b - 1, 0), min(b + 2, CH))

    def self_score(b, h):
        query = s.qta[h, 0:HD, chunk(b)].astype(F32)
        key = s.kta[h, 0:HD, chunk(b)].astype(F32)
        return query, key, jnp.sum(query * key, axis=0, keepdims=True)

    units = [(b, i) for b in range(CH) for i in window(b)]

    def attend(b):
        pad_row = padded(b)
        pairs = [(h, i) for h in range(HEADS) for i in window(b)]
        scores = [nn(s.kn[h, chunk(i), :], s.qta[h, :, chunk(b)]) for h, i in pairs]
        totals, outs = [], []
        for h in range(HEADS):
            own = jnp.exp2(self_score(b, h)[2]) * pad_row
            totals.append(own)
            outs.append(s.vt[h * HD : (h + 1) * HD, chunk(b)].astype(F32) * own)
        for (h, i), score in zip(pairs, scores):
            weight = jnp.exp2(score)
            totals[h] = totals[h] + jnp.sum(weight, axis=0, keepdims=True)
            weight = weight.astype(BF)
            s.wgt[h, units.index((b, i))] = weight
            outs[h] = outs[h] + nn(s.vt[h * HD : (h + 1) * HD, chunk(i)], weight)
        for h in range(HEADS):
            inv = 1.0 / totals[h]
            s.inv[h, :, chunk(b)] = inv
            out = outs[h] * inv
            s.mixf[h * HD : (h + 1) * HD, chunk(b)] = out
            s.mixed[at(n * W + h * HD, HD, HD), chunk(b)] = out.astype(BF)

    def send_mixed(b):
        mix_z(b).start()
        mix_mate(b).start()

    load_w.wait()
    for load in load_rest:
        load.wait()
    for load in loads[6:]:
        load.start()
    project(0)
    project(1)
    attend(0)
    send_mixed(0)
    project(2)
    project(3)
    for b in range(1, CH):
        attend(b)
        send_mixed(b)

    load_dy.wait()
    load_dn.wait()
    s.gact[0 : T // 2, :] = nt(s.dy[0 : T // 2, :], s.dn[...])
    k.await_recvs(other_wo, wo_recv + 1)
    wo_pass.start()
    s.gact[T // 2 :, :] = nt(s.dy[T // 2 :, :], s.dn[...])
    load_up.wait()
    mix_z(0).wait_recv()
    mix_pass(0).start()
    k.await_recvs(s.wo.at[pl.ds(0, 2 * W)], wo_recv)

    def wait_mixed(b):
        k.await_recvs(s.mixed.at[pl.ds(0, 2 * W), chunk(b)], mix_sem + b)

    def out_product(b):
        s.big0[...] = tn(s.mixed[:, chunk(b)], s.wo[...])

    def pass_mixed(b):
        mix_z(b).wait_recv()
        mix_pass(b).start()

    def second_norm(b):
        for i in range(2):
            rows = slice(b * BLK + i * HALF, b * BLK + (i + 1) * HALF)
            hat, _ = moments(s.x[rows, :].astype(F32) + s.big0[i * HALF : (i + 1) * HALF, :])
            s.normed2[rows, :] = (hat * mg + msh).astype(BF)
        own = s.x[ar3.mine(b), :].astype(F32)
        s.mid[b] = own + s.big0[at(core * HALF, HALF, HALF), :]

    def gelu(b):
        for i in range(BLK // 8):
            out = slice(b * BLK + i * 8, b * BLK + (i + 1) * 8)
            pre = s.big1[i * 8 : (i + 1) * 8, :]
            square = pre * pre
            tanh = jnp.tanh(pre * (GELU_A + GELU_B * square))
            half = 0.5 + 0.5 * tanh
            slope = half + (0.5 * pre) * (1.0 - tanh * tanh) * (GELU_A + 3.0 * GELU_B * square)
            s.active[out, :] = (pre * half).astype(BF)
            s.gpre[out, :] = (s.gact[out, :] * slope).astype(BF)

    def mlp_part(b):
        rows = slice(b * BLK, (b + 1) * BLK)
        s.p2[rows, :] = nn(s.active[rows, :], s.dn[...]).astype(BF)

    def up_product(b):
        s.big1[...] = nn(s.normed2[b * BLK : (b + 1) * BLK, :], s.up[...])

    left, right = slice(0, D // 2), slice(D // 2, D)
    wait_mixed(0)
    out_product(0)
    pass_mixed(1)
    second_norm(0)
    up_product(0)
    for b in range(CH):
        rows = slice(b * BLK, (b + 1) * BLK)
        gelu(b)
        if 1 <= b <= SIDE:
            ar2.s1(b - 1)
        if b == 3:
            ar3.s2(2)
        if b == CH - 1:
            s.m1[:, left] = tn(s.active[...], s.dy[:, left]).astype(BF)
            wide(wide_1[:1], "step1")
            s.m1[:, right] = tn(s.active[...], s.dy[:, right]).astype(BF)
            wide(wide_1[1:], "step1")
        s.p3[rows, :] = nt(s.gpre[rows, :], s.up[...]).astype(BF)
        if b >= 1 and b + 1 < CH:
            second_norm(b + 1)
            if b + 1 >= SIDE:
                side_norm(b + 1).start()
        ar3.s1(b)
        if b == 0:
            wait_mixed(1)
            out_product(1)
            second_norm(1)
            pass_mixed(2)
            ar3.s2(0)
        if b + 1 < CH:
            up_product(b + 1)
            if b < SIDE:
                mlp_part(b)
        if b + 2 < CH:
            wait_mixed(b + 2)
            out_product(b + 2)
        if b + 3 < CH:
            pass_mixed(b + 3)
        if b == 1:
            ar3.s2(1)

    def second_back(b):
        ar3.d2(b).wait_recv()
        total = ar3.total(b)
        hat, rstd = moments(s.mid[b])
        s.vec[2:3, :] += 0.5 * jnp.sum(total * hat, axis=0, keepdims=True)
        s.vec[3:4, :] += 0.5 * jnp.sum(total, axis=0, keepdims=True)
        grad = s.dy[ar3.mine(b), :].astype(F32) + norm_back(total * mg, hat, rstd)
        s.gact[b * HALF : (b + 1) * HALF, :] = grad
        s.gattn[ar3.mine(b), :] = grad.astype(BF)
        ar3.d3(b).start()

    def key_sums(h, b):
        col = (b // 2 * HEADS + h) * 2 * HD
        return slice(T // 2 + b % 2 * BLK, T // 2 + (b % 2 + 1) * BLK), slice(col, col + 2 * HD)

    def head_back(grad, which, h, b):
        rows = slice(which * W + h * HD, which * W + (h + 1) * HD)
        hat = s.hat[rows, chunk(b)]
        s.gacc[rows, :] += grad * hat
        grad = grad * gain_col(which, h)
        grad = (
            grad
            - jnp.mean(grad, axis=0, keepdims=True)
            - hat * jnp.mean(grad * hat, axis=0, keepdims=True)
        )
        s.gproj[rows, chunk(b)] = (grad * s.rstd[which * HEADS + h, :, chunk(b)]).astype(BF)

    def attend_back(b):
        ar3.d3(b).wait_recv()
        grad_mixed = nt(s.wo[at(n * W, W, W), :], s.gattn[chunk(b), :])
        if b == CH - 1:
            s.m2[3 * W :, :] = nn(s.mixed[at(n * W, W, W), :], s.gattn[...]).astype(BF)
        pad_row = padded(b)
        wides, pairs, grad_queries = [], [], []
        for h in range(HEADS):
            rows = slice(h * HD, (h + 1) * HD)
            grad_out = grad_mixed[rows].astype(BF).astype(F32)
            inv = s.inv[h, :, chunk(b)]
            delta = jnp.sum(grad_out * s.mixf[rows, chunk(b)], axis=0, keepdims=True)
            scaled = grad_out * inv
            low = delta * inv
            high = low.astype(BF).astype(F32)
            extra = jnp.where(subs == 0, -high, jnp.where(subs == 1, high - low, 0.0))
            wides.append(jnp.concatenate([scaled, extra], axis=0).astype(BF))
            tall = jnp.concatenate([jnp.zeros_like(scaled), scaled], axis=0)
            tall = jnp.transpose(tall).astype(BF)
            pairs.append(jnp.concatenate([s.qn[h, chunk(b), :], tall], axis=0))
            qf, kf, own = self_score(b, h)
            own_prob = jnp.exp2(own) * inv * pad_row
            own_grad = jnp.sum(grad_out * s.vt[rows, chunk(b)].astype(F32), axis=0, keepdims=True)
            own_score = own_prob * (own_grad - delta)
            s.dkx[rows, chunk(b)] = qf * own_score
            s.dvx[rows, chunk(b)] = grad_out * own_prob
            grad_queries.append(kf * own_score)
        tasks = [(h, i) for h in range(HEADS) for i in window(b)]
        products, ahead = {}, 3
        grad_scores = [[] for _ in range(HEADS)]
        for t in range(len(tasks) + ahead):
            if t < len(tasks):
                h, i = tasks[t]
                products[t] = nn(s.vn[h, chunk(i), :], wides[h])
            if t < ahead:
                continue
            h, i = tasks[t - ahead]
            weight = s.wgt[h, units.index((b, i))]
            grad_score = (weight.astype(F32) * products.pop(t - ahead)).astype(BF)
            grad_scores[h].append(grad_score)
            both = nn(jnp.concatenate([grad_score, weight], axis=1), pairs[h])
            if b == max(i - 1, 0):
                s.gact[key_sums(h, i)] = both
            else:
                s.gact[key_sums(h, i)] += both
            if i == window(b)[-1]:
                keys = s.kta[h, 0:HD, window(b)[0] * BLK : (i + 1) * BLK]
                grad_queries[h] = grad_queries[h] + nn(
                    keys, jnp.concatenate(grad_scores[h], axis=0)
                )
        for h in range(HEADS):
            head_back(grad_queries[h] * (0.125 / SC), 0, h, b)

    def keys_back(b):
        for h in range(HEADS):
            rows = slice(h * HD, (h + 1) * HD)
            both = jnp.transpose(s.gact[key_sums(h, b)])
            head_back((both[0:HD] + s.dkx[rows, chunk(b)]) * 0.125, 1, h, b)
            grad_value = both[HD:] + s.dvx[rows, chunk(b)]
            s.gproj[2 * W + h * HD : 2 * W + (h + 1) * HD, chunk(b)] = grad_value.astype(BF)

    def first_part(b):
        s.big0[...] = tn(s.gproj[:, chunk(b)], s.wt[...])
        for i in range(2):
            rows = slice(b * BLK + i * HALF, b * BLK + (i + 1) * HALF)
            part = s.big0[i * HALF : (i + 1) * HALF, :]
            s.p4[rows, :] = part.astype(BF)
            s.vec[0:1, :] += jnp.sum(part * s.hat1[rows, :].astype(F32), axis=0, keepdims=True)
            s.vec[1:2, :] += jnp.sum(part, axis=0, keepdims=True)
        ar4.s1(b)

    def side_mlp(b):
        side_pass(b).wait_recv()
        rows = slice(b * BLK, (b + 1) * BLK)
        s.big0[...] = nn(s.n2s[rows, :], s.up[...])
        for i in range(BLK // 8):
            out = slice(b * BLK + i * 8, b * BLK + (i + 1) * 8)
            pre = s.big0[i * 8 : (i + 1) * 8, :]
            half = 0.5 + 0.5 * jnp.tanh(pre * (GELU_A + GELU_B * (pre * pre)))
            s.active[out, :] = (pre * half).astype(BF)
        s.gpre[rows, :] = nn(s.active[rows, :], s.dn[...]).astype(BF)
        ar2.d1_side(b).start()

    def pass_side(b):
        side_norm(b).wait_recv()
        side_pass(b).start()

    second_back(0)
    ar3.s2(CH - 1)
    s.m0[:, left] = tn(s.normed2[...], s.gpre[:, left]).astype(BF)
    wide(wide_2[:1], "step1")
    s.m0[:, right] = tn(s.normed2[...], s.gpre[:, right]).astype(BF)
    wide(wide_2[1:], "step1")
    attend_back(0)
    second_back(1)
    wide(wide_1, "step1b")
    ar2.s2(0)
    mlp_part(2)
    attend_back(1)
    keys_back(0)
    second_back(2)
    wide(wide_2, "step1b")
    first_part(0)
    ar2.s2(1)
    attend_back(2)
    keys_back(1)
    second_back(3)
    wide(wide_1, "step2")
    first_part(1)
    attend_back(3)
    keys_back(2)
    keys_back(3)
    wide(wide_2, "step2")
    s.m2[0 : 3 * W, left] = nn(s.gproj[...], s.normed[:, left]).astype(BF)
    wide(wide_3[:1], "step1")
    wide(wide_1, "step3")
    s.m2[0 : 3 * W, right] = nn(s.gproj[...], s.normed[:, right]).astype(BF)
    wide(wide_3[1:], "step1")
    ar2.s1(2)
    first_part(2)
    first_part(3)
    for which in range(2):
        rows = slice(which * W, (which + 1) * W)
        both = s.gacc[rows, 0:128] + s.gacc[rows, 128:256]
        s.vec[4 + which : 5 + which, 0:W] = jnp.sum(jnp.transpose(both), axis=0, keepdims=True)
    s.vecs[...] = s.vec[...]
    vec_c.start()
    for b in range(SIDE, CH):
        pass_side(b)
    wide(wide_2, "step3")
    ar4.s2(0)
    wide(wide_1, "step4")
    wide(wide_3, "step1b")
    ar4.s2(1)
    mlp_part(CH - 1)
    ar2.s1(CH - 1)

    def layer_out(b):
        ar2.d2(b).wait_recv()
        s.r22[b] = (s.mid[b] + ar2.total(b)).astype(BF)
        ar2.d3(b).start()
        lo_copy(b).start()

    def grad_tokens(b):
        ar4.d2(b).wait_recv()
        hat, rstd = moments(s.x[ar4.mine(b), :].astype(F32))
        s.r24[b] = (s.gact[b * HALF : (b + 1) * HALF, :] + norm_back(ar4.total(b) * ag, hat, rstd)).astype(BF)
        ar4.d3(b).start()
        gt_copy(b).start()

    upper = lax.broadcasted_iota(jnp.int32, (8, D), 0) < 4
    vec_c.wait_recv()
    s.v1[...] = s.vec[...] + jnp.where(upper, s.rvz[0], 0.0)
    s.rvx[k.x] = s.v1[...]
    for copy in vec_x:
        copy.start()
    side_mlp(2)
    wide(wide_2, "step4")
    wide(wide_3, "step2")
    k.await_recvs(s.rvx.at[pl.ds(0, 3)], vec_sem + 1)
    s.v2[...] = (s.rvx[0] + s.rvx[1]) + (s.rvx[2] + s.rvx[3])
    s.rvy[k.y] = s.v2[...]
    for copy in vec_y:
        copy.start()
    wide(wide_1, "step5")
    for d in (1, 3):
        wide(wide_1, "step6", d)
    side_mlp(3)
    ar2.s2_side(2)
    wide(wide_2, "step5")
    for d in (1, 3):
        wide(wide_2, "step6", d)
    ar2.s2_side(3)
    wide(wide_3, "step3")
    k.await_recvs(s.rvy.at[pl.ds(0, 3)], vec_sem + 2)
    s.v3[...] = (s.rvy[0] + s.rvy[1]) + (s.rvy[2] + s.rvy[3])
    vec_z.start()
    ar4.s2(2)
    ar2.s2(2)
    ar2.s2(3)
    layer_out(0)
    layer_out(1)
    grad_tokens(0)
    wide(wide_3, "step4")
    wide(wide_1, "step7")
    vec_z.wait_recv()
    s.v4[...] = s.v3[...] + s.rvz[1]
    vec_l.start()
    ar4.s2(3)
    wide(wide_2, "step7")
    grad_tokens(1)
    wide(wide_3, "step5")
    layer_out(2)
    grad_tokens(2)
    layer_out(3)
    vec_l.wait_recv()
    vec_out[...] = s.v4[...] + jnp.where(upper, s.rvz[2], 0.0)
    grad_tokens(3)

    half = pl.ds(0, T // 2)
    k.copy(s.p2.at[half], lo_out.at[half], out_sem).wait()
    k.copy(s.p4.at[half], gt_out.at[half], out_sem + 1).wait()
    for item in (ar2, ar3, ar4, *wide_1, *wide_2, *wide_3):
        item.finish()
    k.await_sends(s.wo.at[pl.ds(0, 3 * W)], wo_send)
    k.await_sends(s.mixed.at[pl.ds(0, 3 * W)], mix_send)
    k.await_sends(s.n2s.at[pl.ds(0, (CH - SIDE) * BLK)], side_send)
    k.await_sends(s.big0.at[pl.ds(0, 72)], vec_send)


PARTS = 4


def finish(lo, gt, gup, gdn, g2, vec, lo_o, gt_o, qkv_o, qg_o, kg_o, out_o, gup_o, gdn_o, ag_o, as_o, mg_o, ms_o, low, high, same, sem_in, sem_out):
    size = D // PARTS
    pieces = []
    for i, (src, dst) in enumerate(((gup, gup_o), (gdn, gdn_o), (g2, None))):
        for p in range(PARTS):
            rows = pl.ds(p * size, size)
            if dst is None:
                to = qkv_o.at[p] if p < 3 else out_o
            else:
                to = dst.at[rows]
            load = pltpu.make_async_copy(src.at[rows], low.at[i, rows], sem_in.at[i, p])
            pieces.append((load, (i, rows), pltpu.make_async_copy(high.at[i, rows], to, sem_out.at[i, p])))
    for i, (src, dst) in enumerate(((gt, gt_o), (lo, lo_o))):
        load = pltpu.make_async_copy(src, same.at[i], sem_in.at[3 + i, 0])
        store = pltpu.make_async_copy(same.at[i], dst, sem_out.at[3 + i, 0])
        pieces.insert(0, (load, None, store))
    for load, _, _ in pieces:
        load.start()
    for ref, row, count in (
        (ag_o, 0, D),
        (as_o, 1, D),
        (mg_o, 2, D),
        (ms_o, 3, D),
        (qg_o, 4, W),
        (kg_o, 5, W),
    ):
        ref[...] = vec[row : row + 1, 0:count].reshape(count)
    for load, cast, store in pieces:
        load.wait()
        if cast is not None:
            high[cast] = low[cast].astype(F32)
        store.start()
    for _, _, store in pieces:
        store.wait()


def body(*args):
    any_spec = pl.BlockSpec(memory_space=pl.ANY)
    vmem = pl.BlockSpec(memory_space=pltpu.VMEM)
    args = list(args)
    args[4] = jnp.swapaxes(args[4], 1, 2).reshape(3 * W, D)
    out = pl.pallas_call(
        kernel,
        out_shape=(
            jax.ShapeDtypeStruct((T, D), BF),
            jax.ShapeDtypeStruct((T, D), BF),
            jax.ShapeDtypeStruct((D, F), BF),
            jax.ShapeDtypeStruct((F, D), BF),
            jax.ShapeDtypeStruct((4 * W, D), BF),
            jax.ShapeDtypeStruct((8, D), F32),
        ),
        in_specs=[any_spec] * 14,
        out_specs=(any_spec, any_spec, any_spec, any_spec, any_spec, vmem),
        scratch_shapes=[pltpu.VMEM(shape, dtype) for shape, dtype in SCRATCH.values()]
        + [
            pltpu.SMEM((1,), jnp.int32),
            pltpu.SemaphoreType.DMA((NSEND,)),
            pltpu.SemaphoreType.DMA((NRECV,)),
            pltpu.SemaphoreType.DMA((NLOC,)),
        ],
        compiler_params=pltpu.CompilerParams(
            collective_id=0, has_side_effects=True, vmem_limit_bytes=60 * 1024 * 1024
        ),
        cost_estimate=pl.CostEstimate(
            flops=14 * 10**9, bytes_accessed=20 * 2**20, transcendentals=8 * 2**20
        ),
    )(*args)
    layer, tokens, qkv, *rest = pl.pallas_call(
        finish,
        out_shape=(
            jax.ShapeDtypeStruct((T, D), BF),
            jax.ShapeDtypeStruct((T, D), BF),
            jax.ShapeDtypeStruct((3, W, D), F32),
            jax.ShapeDtypeStruct((W,), F32),
            jax.ShapeDtypeStruct((W,), F32),
            jax.ShapeDtypeStruct((W, D), F32),
            jax.ShapeDtypeStruct((D, F), F32),
            jax.ShapeDtypeStruct((F, D), F32),
            jax.ShapeDtypeStruct((D,), F32),
            jax.ShapeDtypeStruct((D,), F32),
            jax.ShapeDtypeStruct((D,), F32),
            jax.ShapeDtypeStruct((D,), F32),
        ),
        in_specs=[any_spec] * 5 + [vmem],
        out_specs=(any_spec, any_spec, any_spec, vmem, vmem, any_spec, any_spec, any_spec)
        + (vmem,) * 4,
        scratch_shapes=[
            pltpu.VMEM((3, D, D), BF),
            pltpu.VMEM((3, D, D), F32),
            pltpu.VMEM((2, T, D), BF),
            pltpu.SemaphoreType.DMA((5, PARTS)),
            pltpu.SemaphoreType.DMA((5, PARTS)),
        ],
        compiler_params=pltpu.CompilerParams(vmem_limit_bytes=60 * 1024 * 1024),
        cost_estimate=pl.CostEstimate(flops=0, bytes_accessed=17 * 2**20, transcendentals=0),
    )(*out)
    return (layer, tokens, jnp.swapaxes(qkv, 1, 2), *rest)


def solution(mesh):
    placed = (
        P("wide", None),
        P("wide", None),
        P("wide", None),
        P("wide"),
        P(None, None, "narrow"),
        P("narrow"),
        P("narrow"),
        P("narrow", None),
        P(None, "narrow"),
        P("narrow", None),
        P(),
        P(),
        P(),
        P(),
    )
    return jax.shard_map(
        body,
        mesh=mesh,
        in_specs=placed,
        out_specs=(
            P("wide", None),
            P("wide", None),
            P(None, None, "narrow"),
            P("narrow"),
            P("narrow"),
            P("narrow", None),
            P(None, "narrow"),
            P("narrow", None),
            P(),
            P(),
            P(),
            P(),
        ),
        check_vma=False,
    )
```

```python
import jax
import jax.numpy as jnp
from jax import lax
from jax.experimental import pallas as pl
from jax.experimental.pallas import tpu as pltpu
from jax.sharding import PartitionSpec as P

T = 1024
D = 768
HEADS = 3
HD = 64
W = HEADS * HD
F = 768
BLK = 256
CH = T // BLK
HALF = BLK // 2
BIG = 512.0
MINUS = 31
LOG2E = 1.4426950408889634
SC = 0.125 * LOG2E
EPS = 1e-06
GELU_A = 0.7978845608028654
GELU_B = 0.044715 * GELU_A

BF = jnp.bfloat16
F32 = jnp.float32
MESH = pl.DeviceIdType.MESH


def nn(a, b):
    return lax.dot_general(a, b, (((1,), (0,)), ((), ())), preferred_element_type=F32)


def nt(a, b):
    return lax.dot_general(a, b, (((1,), (1,)), ((), ())), preferred_element_type=F32)


def tn(a, b):
    return lax.dot_general(a, b, (((0,), (0,)), ((), ())), preferred_element_type=F32)


def at(start, size, unit):
    return pl.ds(pl.multiple_of(start, unit), size)


def chunk(b):
    return at(b * BLK, BLK, BLK)


def moments(values):
    centre = values - jnp.mean(values, axis=-1, keepdims=True)
    rstd = lax.rsqrt(jnp.mean(centre * centre, axis=-1, keepdims=True) + EPS)
    return centre * rstd, rstd


def norm_back(grad, hat, rstd):
    return rstd * (
        grad
        - jnp.mean(grad, axis=-1, keepdims=True)
        - hat * jnp.mean(grad * hat, axis=-1, keepdims=True)
    )


SCRATCH = dict(
    seg=((1, T), jnp.int32),
    qg=((W,), F32),
    kg=((W,), F32),
    ag=((D,), F32),
    ash=((D,), F32),
    mg=((D,), F32),
    msh=((D,), F32),
    x=((T, D), BF),
    dy=((T, D), BF),
    wt=((3 * W, D), BF),
    wo=((4 * W, D), BF),
    up=((D, F), BF),
    dn=((F, D), BF),
    normed=((T, D), BF),
    hat1=((T, D), BF),
    qta=((HEADS, 2 * HD, T), BF),
    kta=((HEADS, 2 * HD, T), BF),
    vt=((W, T), BF),
    qn=((HEADS, T, 2 * HD), BF),
    kn=((HEADS, T, 2 * HD), BF),
    vn=((HEADS, T, 2 * HD), BF),
    hat=((2 * W, T), F32),
    rstd=((6, 1, T), F32),
    gcol=((2 * W, 128), F32),
    mixed=((4 * W, T), BF),
    mixf=((W, T), F32),
    mid=((CH, HALF, D), F32),
    wgt=((HEADS, 10, BLK, BLK), BF),
    inv=((HEADS, 1, T), F32),
    normed2=((T, D), BF),
    active=((T, F), BF),
    gpre=((T, F), BF),
    big0=((BLK, D), F32),
    gact=((T, F), F32),
    n2s=((T, D), BF),
    r12s=((CH, HALF, D), BF),
    big1=((BLK, D), F32),
    p2=((T, D), BF),
    p3=((T, D), BF),
    p4=((T, D), BF),
    r12=((CH, HALF, D), BF),
    r13=((CH, HALF, D), BF),
    r14=((CH, HALF, D), BF),
    r22=((CH, HALF, D), BF),
    r23=((CH, HALF, D), BF),
    r24=((CH, HALF, D), BF),
    gattn=((T, D), BF),
    dkx=((W, T), F32),
    dvx=((W, T), F32),
    gproj=((3 * W, T), BF),
    gacc=((2 * W, BLK), F32),
    m0=((D, F), BF),
    m1=((F, D), BF),
    m2=((4 * W, D), BF),
    vec=((8, D), F32),
    vecs=((8, D), F32),
    rvx=((4, 8, D), F32),
    rvy=((4, 8, D), F32),
    rvz=((3, 8, D), F32),
    v1=((8, D), F32),
    v2=((8, D), F32),
    v3=((8, D), F32),
    v4=((8, D), F32),
)
SIDE = 2
RELAYED = "abcd"
for _s, _w in ((_c, D // 2) for _c in "abcdef"):
    SCRATCH["rs1" + _s] = ((4, 96, _w), BF)
    SCRATCH["ra" + _s] = ((2, 96, _w), BF)
    SCRATCH["rb" + _s] = ((2, 96, _w), BF)
    SCRATCH["s1" + _s] = ((192, _w), BF)
    SCRATCH["rs2" + _s] = ((3, 48, _w), BF)
    SCRATCH["s2" + _s] = ((48, _w), BF)
    SCRATCH["rz" + _s] = ((48, _w), BF)
    SCRATCH["rr" + _s] = ((192, _w), BF)
    if _s in RELAYED:
        SCRATCH["nb" + _s] = ((2, 192, _w), BF)

NSEND, NRECV, NLOC = 20, 95, 25


class Wide:
    def __init__(self, k, send, name, mat, cols, out, first, second):
        self.k, self.s, self.mat, self.cols, self.out = k, k.s, mat, cols, out
        self.name = name
        self.first, self.second = first, second
        self.u, self.t = k.coord(first), k.coord(second)
        self.relayed = name in RELAYED
        self.send = send
        self.recv = k.recvs(7 if self.relayed else 8)
        self.local = k.locals(1)

    def ref(self, what):
        return getattr(self.s, what + self.name)

    def half(self, q, i):
        return at(lax.rem(self.u + q + 4, 4) * 192 + i * 96, 96, 96)

    def rs1(self, i):
        k = self.k
        if i < 4:
            q, part = ((2, 0), (2, 1), (1, 1), (-1, 0))[i]
            src = self.mat.at[self.half(q, part), self.cols]
        else:
            src = self.ref("rb").at[i - 4]
        dst = self.ref("ra").at[i] if i < 2 else self.ref("rs1").at[i - 2]
        return k.remote(
            src,
            dst,
            self.send,
            self.recv + (0 if i < 2 else 1),
            k.along(self.first, 1 if i % 2 == 0 else 3),
        )

    def rs2(self, d):
        k = self.k
        q = lax.rem(self.t + d, 4)
        return k.remote(
            self.ref("s1").at[at(q * 48, 48, 48)],
            self.ref("rs2").at[d - 1],
            self.send + 1,
            self.recv + 2,
            k.along(self.second, d),
        )

    def zz(self):
        return self.k.remote(self.ref("s2"), self.ref("rz"), self.send + 1, self.recv + 3, self.k.zhi)

    def ag2(self, d):
        piece = self.ref("rr").at[at(self.t * 48, 48, 48)]
        recv = self.recv + 4 + (0 if self.relayed else d - 1)
        return self.k.remote(piece, piece, self.send + 1, recv, self.k.along(self.second, d))

    def rows_out(self, u, start=0, size=192):
        return self.out.at[at(lax.rem(u + 4, 4) * 192 + start, size, 96), self.cols]

    def ag1(self, d):
        dst = self.ref("nb").at[0 if d == 1 else 1]
        return self.k.remote(
            self.ref("rr"), dst, self.send + 2, self.recv + 5, self.k.along(self.first, d)
        )

    def piece(self, d, e):
        start = lax.rem(self.t + 4 - e, 4) * 48
        return self.k.remote(
            self.ref("rr").at[at(start, 48, 48)],
            self.out.at[at(self.u * 192 + start, 48, 48), self.cols],
            self.send + 2,
            self.recv + 7,
            self.k.along(self.first, d),
        )

    def forward(self, d):
        u, start = (self.u - 1, 0) if d == 1 else (self.u + 1, 96)
        src = self.ref("nb").at[0 if d == 1 else 1, pl.ds(start, 96)]
        return self.k.remote(
            src,
            self.rows_out(u, start, 96),
            self.send + 2,
            self.recv + 6,
            self.k.along(self.first, d),
        )

    def own(self, i=0):
        if i == 0:
            return self.k.copy(self.ref("rr"), self.rows_out(self.u), self.local)
        u = self.u - 1 if i == 1 else self.u + 1
        return self.k.copy(self.ref("nb").at[i - 1], self.rows_out(u), self.local)

    def step1(self):
        for i in range(4):
            self.rs1(i).start()

    def step1b(self):
        self.k.await_recvs(self.ref("ra"), self.recv)
        for i, (q, part) in enumerate(((1, 0), (-1, 1))):
            own = self.mat[self.half(q, part), self.cols].astype(F32)
            self.ref("rb")[i] = (own + self.ref("ra")[i].astype(F32)).astype(BF)
            self.rs1(4 + i).start()

    def step2(self):
        self.k.await_recvs(self.ref("rs1"), self.recv + 1)
        rs1, s1 = self.ref("rs1"), self.ref("s1")
        for i, (one, two) in enumerate(((1, 2), (0, 3))):
            total = self.mat[self.half(0, i), self.cols].astype(F32)
            total = total + (rs1[one].astype(F32) + rs1[two].astype(F32))
            s1[i * 96 : (i + 1) * 96, :] = total.astype(BF)
        for d in (2, 1, 3):
            self.rs2(d).start()

    def step3(self):
        self.k.await_recvs(self.ref("rs2"), self.recv + 2)
        total = self.ref("s1")[at(self.t * 48, 48, 48), :].astype(F32)
        for d in range(3):
            total = total + self.ref("rs2")[d].astype(F32)
        self.ref("s2")[...] = total.astype(BF)
        self.zz().start()

    def step4(self):
        self.zz().wait_recv()
        total = self.ref("s2")[...].astype(F32) + self.ref("rz")[...].astype(F32)
        self.ref("rr")[at(self.t * 48, 48, 48), :] = total.astype(BF)
        for d in (2, 1, 3):
            self.ag2(d).start()
        if not self.relayed:
            for d in (2, 1, 3):
                self.piece(d, 0).start()

    def step5(self):
        if self.relayed:
            self.k.await_recvs(self.ref("rr").at[pl.ds(0, 144)], self.recv + 4)
        else:
            for e in (1, 3, 2):
                self.ag2(e).wait_recv()
                for d in (2, 1, 3):
                    self.piece(d, e).start()
        self.own().start()

    def step6(self, d):
        self.ag1(d).start()

    def step7(self):
        self.k.await_recvs(self.ref("nb"), self.recv + 5)
        for d in (1, 3):
            self.forward(d).start()
        for i in (1, 2):
            self.own(i).start()

    def finish(self):
        k = self.k
        most = (pl.ds(0, 576), self.cols)
        if self.relayed:
            k.await_recvs(self.out.at[pl.ds(0, 192), self.cols], self.recv + 6)
            k.copy(self.mat.at[most], self.out.at[most], self.local).wait()
        else:
            k.await_recvs(self.out.at[most], self.recv + 7)
            self.own().wait()
        if self.first == "x":
            k.await_sends(self.mat.at[pl.ds(0, 576)], self.send)
            k.await_sends(self.mat.at[pl.ds(0, 336)], self.send + 1)
            k.await_sends(self.mat.at[pl.ds(0, 576)], self.send + 2)


class Narrow:
    def __init__(self, k, part, r1, r2, result, joint=True, side=None):
        self.k, self.part, self.r1, self.r2, self.result = k, part, r1, r2, result
        self.side = side
        self.joint = joint
        self.send = k.sends(2 if side is None else 3)
        self.recv = k.recvs((2 * CH + 1 if joint else 3 * CH) + (0 if side is None else CH - SIDE))

    def mine(self, b):
        return at(b * BLK + self.k.core * HALF, HALF, HALF)

    def theirs(self, b):
        return at(b * BLK + (1 - self.k.core) * HALF, HALF, HALF)

    def d1(self, b):
        return self.k.remote(
            self.part.at[self.theirs(b)], self.r1.at[b], self.send, self.recv + b, self.k.mate
        )

    def d2(self, b):
        if self.side is None or b < SIDE:
            src, device = self.part, self.k.zlo
        else:
            src, device = self.side[0], self.k.side
        return self.k.remote(
            src.at[self.mine(b)], self.r2.at[b], self.send, self.recv + CH + b, device
        )

    def d3(self, b):
        src, dst = self.result(b, self.mine(b))
        recv = self.recv + 2 * CH + (0 if self.joint else b)
        return self.k.remote(src, dst, self.send + 1, recv, self.k.mate)

    def s1(self, b):
        self.d1(b).start()

    def s2(self, b):
        self.d1(b).wait_recv()
        total = self.part[self.mine(b), :].astype(F32) + self.r1[b].astype(F32)
        self.part[self.mine(b), :] = total.astype(BF)
        if self.side is None or b < SIDE:
            self.d2(b).start()

    def d1_side(self, b):
        part, r1 = self.side
        return self.k.remote(
            part.at[self.theirs(b)],
            r1.at[b],
            self.send + 2,
            self.recv + 2 * CH + 1 + b - SIDE,
            self.k.mate,
        )

    def s2_side(self, b):
        part, r1 = self.side
        self.d1_side(b).wait_recv()
        total = part[self.mine(b), :].astype(F32) + r1[b].astype(F32)
        part[self.mine(b), :] = total.astype(BF)
        self.d2(b).start()

    def total(self, b):
        return self.part[self.mine(b), :].astype(F32) + self.r2[b].astype(F32)

    def finish(self):
        k, half = self.k, self.part.at[pl.ds(0, T // 2)]
        if self.joint:
            k.await_recvs(half, self.recv + 2 * CH)
        k.await_sends(self.part, self.send)
        k.await_sends(half, self.send + 1)
        if self.side is not None:
            k.await_sends(self.part.at[pl.ds(0, (CH - SIDE) * HALF)], self.send + 2)


class Names:
    pass


class Kernel:
    def __init__(self, s, send, recv, loc):
        self.s, self.send, self.recv, self.loc = s, send, recv, loc
        self.taken = {}
        w = lax.axis_index("wide")
        n = lax.axis_index("narrow")
        self.w, self.n = w, n
        self.x = lax.rem(w, 4)
        self.y = lax.rem(lax.div(w, 4), 4)
        self.z = lax.div(w, 16)
        self.core = lax.rem(n, 2)
        self.n1 = n + 1 - 2 * self.core
        self.n2 = lax.rem(n + 2, 4)
        self.mate = (w, self.n1)
        self.zlo = (w, self.n2)
        self.zhi = (lax.rem(w + 16, 32), n)
        self.side = (lax.rem(w + 16, 32), self.n2)

    def coord(self, axis):
        return self.x if axis == "x" else self.y

    def along(self, axis, d):
        if axis == "x":
            return (self.w - self.x + lax.rem(self.x + d, 4), self.n)
        return (self.w - 4 * self.y + 4 * lax.rem(self.y + d, 4), self.n)

    def take(self, kind, count, most):
        start = self.taken.get(kind, 0)
        self.taken[kind] = start + count
        assert start + count <= most, (kind, start + count, most)
        return start

    def sends(self, count):
        return self.take("send", count, NSEND)

    def recvs(self, count):
        return self.take("recv", count, NRECV)

    def locals(self, count):
        return self.take("local", count, NLOC)

    def remote(self, src, dst, send, recv, device):
        return pltpu.make_async_remote_copy(
            src_ref=src,
            dst_ref=dst,
            send_sem=self.send.at[send],
            recv_sem=self.recv.at[recv],
            device_id=device,
            device_id_type=MESH,
        )

    def await_sends(self, ref, send):
        self.remote(ref, ref, send, 0, self.mate).wait_send()

    def await_recvs(self, ref, recv):
        self.remote(ref, ref, 0, recv, self.mate).wait_recv()

    def copy(self, src, dst, sem):
        return pltpu.make_async_copy(src, dst, self.loc.at[sem])


def kernel(
    x_in,
    dy_in,
    seg_in,
    pad_in,
    wt_in,
    qg_in,
    kg_in,
    wo_in,
    up_in,
    dn_in,
    ag_in,
    as_in,
    mg_in,
    ms_in,
    lo_out,
    gt_out,
    gup_out,
    gdn_out,
    g2_out,
    vec_out,
    *scratch,
):
    s = Names()
    for name, ref in zip(SCRATCH, scratch):
        setattr(s, name, ref)
    pad_smem, *semaphores = scratch[len(SCRATCH) :]
    k = Kernel(s, *semaphores)
    n, core = k.n, k.core

    own_wo = s.wo.at[at(n * W, W, W)]
    pieces = [pl.ds(b * BLK, BLK) for b in range(CH)]
    loads = [
        (x_in.at[pieces[0]], s.x.at[pieces[0]]),
        (wt_in, s.wt),
        (wo_in, own_wo),
        *[(x_in.at[rows], s.x.at[rows]) for rows in pieces[1:]],
        (up_in, s.up),
        (dn_in, s.dn),
        (dy_in, s.dy),
    ]
    load_sem = k.locals(len(loads))
    loads = [k.copy(src, dst, load_sem + i) for i, (src, dst) in enumerate(loads)]
    smalls = [
        (ag_in, s.ag),
        (as_in, s.ash),
        (qg_in, s.qg),
        (kg_in, s.kg),
        (seg_in, s.seg),
        (pad_in, pad_smem),
        (mg_in, s.mg),
        (ms_in, s.msh),
    ]
    small_sem = k.locals(len(smalls))
    smalls = [k.copy(src, dst, small_sem + i) for i, (src, dst) in enumerate(smalls)]
    loads[0].start()
    for load in smalls + loads[1:6]:
        load.start()
    load_x, load_w, load_wo, *load_rest, load_up, load_dn, load_dy = loads

    barrier = pltpu.get_barrier_semaphore()
    peers = [k.mate, k.zlo, k.zhi, k.side]
    peers += [k.along(axis, d) for axis in "xy" for d in (1, 2, 3)]
    for peer in peers:
        pl.semaphore_signal(barrier, inc=1, device_id=peer, device_id_type=MESH)

    wo_send, wo_recv = k.sends(1), k.recvs(2)
    own_low = s.wo.at[at(n * W, W // 3, W // 3)]
    own_high = s.wo.at[at(n * W + W // 3, 2 * W // 3, W // 3)]
    other_wo = s.wo.at[at(k.n2 * W, W, W)]
    wo_sends = [
        k.remote(own_wo, own_wo, wo_send, wo_recv, k.mate),
        k.remote(own_low, own_low, wo_send, wo_recv + 1, k.zlo),
        k.remote(own_high, own_high, wo_send, wo_recv + 1, k.side),
    ]
    wo_pass = k.remote(other_wo, other_wo, wo_send, wo_recv, k.mate)
    mix_send, mix_sem = k.sends(1), k.recvs(2 * CH)

    def mix_mate(b):
        ref = s.mixed.at[at(n * W, W, W), chunk(b)]
        return k.remote(ref, ref, mix_send, mix_sem + b, k.mate)

    def mix_z(b):
        ref = s.mixed.at[at(n * W, W, W), chunk(b)]
        return k.remote(ref, ref, mix_send, mix_sem + CH + b, k.zlo)

    def mix_pass(b):
        ref = s.mixed.at[at(k.n2 * W, W, W), chunk(b)]
        return k.remote(ref, ref, mix_send, mix_sem + b, k.mate)

    ar2 = Narrow(k, s.p2, s.r12, s.r22, lambda b, rows: (s.r22.at[b], lo_out.at[rows]), side=(s.gpre, s.r12s))
    ar3 = Narrow(k, s.p3, s.r13, s.r23, lambda b, rows: (s.gattn.at[rows], s.gattn.at[rows]), joint=False)
    ar4 = Narrow(k, s.p4, s.r14, s.r24, lambda b, rows: (s.r24.at[b], gt_out.at[rows]))
    low_cols, high_cols = pl.ds(0, D // 2), pl.ds(D // 2, D // 2)
    wide_sends = [k.sends(3) for _ in range(3)]
    wide_1 = Wide(k, wide_sends[0], "a", s.m1, low_cols, gdn_out, "x", "y"), Wide(k, wide_sends[0], "b", s.m1, high_cols, gdn_out, "y", "x")
    wide_2 = Wide(k, wide_sends[1], "c", s.m0, low_cols, gup_out, "x", "y"), Wide(k, wide_sends[1], "d", s.m0, high_cols, gup_out, "y", "x")
    wide_3 = Wide(k, wide_sends[2], "e", s.m2, low_cols, g2_out, "x", "y"), Wide(k, wide_sends[2], "f", s.m2, high_cols, g2_out, "y", "x")

    def wide(pair, step, *args):
        for item in pair:
            getattr(item, step)(*args)

    vec_send, vec_sem = k.sends(1), k.recvs(5)
    vec_c = k.remote(s.vecs, s.rvz.at[0], vec_send, vec_sem, k.mate)
    vec_x = [
        k.remote(s.v1, s.rvx.at[k.x], vec_send, vec_sem + 1, k.along("x", d)) for d in (1, 2, 3)
    ]
    vec_y = [
        k.remote(s.v2, s.rvy.at[k.y], vec_send, vec_sem + 2, k.along("y", d)) for d in (1, 2, 3)
    ]
    vec_z = k.remote(s.v3, s.rvz.at[1], vec_send, vec_sem + 3, k.zhi)
    vec_l = k.remote(s.v4, s.rvz.at[2], vec_send, vec_sem + 4, k.zlo)
    out_sem = k.locals(2)

    side_send, side_sem = k.sends(1), k.recvs(2 * (CH - SIDE))

    def side_norm(b):
        rows = ar2.mine(b)
        return k.remote(s.normed2.at[rows], s.n2s.at[rows], side_send, side_sem + b - SIDE, k.side)

    def side_pass(b):
        rows = ar2.mine(b)
        return k.remote(s.n2s.at[rows], s.n2s.at[rows], side_send, side_sem + CH - SIDE + b - SIDE, k.mate)

    def lo_copy(b):
        return k.copy(s.r22.at[b], lo_out.at[ar2.mine(b)], out_sem)

    def gt_copy(b):
        return k.copy(s.r24.at[b], gt_out.at[ar4.mine(b)], out_sem + 1)


    for load in smalls:
        load.wait()
    load_x.wait()

    ag = s.ag[...].reshape(1, D)
    ash = s.ash[...].reshape(1, D)
    mg = s.mg[...].reshape(1, D)
    msh = s.msh[...].reshape(1, D)

    def gain_col(c, h):
        col = s.gcol[c * W + h * HD : c * W + (h + 1) * HD, :]
        return jnp.concatenate([col, col], axis=1)

    lanes = lax.broadcasted_iota(jnp.int32, (1, BLK), 1)
    subs = lax.broadcasted_iota(jnp.int32, (HD, BLK), 0)

    limit = T - pad_smem[0]

    def padded(b):
        return jnp.where(lanes + b * BLK >= limit, 1.0, 0.0)

    def first_norm(b):
        for i in range(2):
            rows = slice(b * BLK + i * HALF, b * BLK + (i + 1) * HALF)
            hat, _ = moments(s.x[rows, :].astype(F32))
            s.hat1[rows, :] = hat.astype(BF)
            s.normed[rows, :] = (hat * ag + ash).astype(BF)

    def project(b):
        raw = nt(s.wt[...], s.normed[chunk(b), :])
        if b + 1 < CH:
            first_norm(b + 1)
        same = jnp.where(subs == s.seg[:, chunk(b)], 1.0, 0.0)
        same_valid = same * (1.0 - padded(b))
        query_rows = jnp.where(subs == MINUS, -BIG, BIG * same)
        key_rows = jnp.where(subs == MINUS, 1.0, same_valid)
        ones = jnp.where(subs < 2, 1.0, 0.0)
        for h in range(HEADS):
            for which in range(2):
                rows = slice(which * W + h * HD, which * W + (h + 1) * HD)
                value = raw[rows]
                centre = value - jnp.mean(value, axis=0, keepdims=True)
                rstd = lax.rsqrt(jnp.mean(centre * centre, axis=0, keepdims=True) + EPS)
                hat = centre * rstd
                s.hat[rows, chunk(b)] = hat
                s.rstd[which * HEADS + h, :, chunk(b)] = rstd
                value = hat * gain_col(which, h) * (1.0, SC)[which]
                both = jnp.concatenate([value, (query_rows, key_rows)[which]], axis=0)
                if which == 0:
                    s.qta[h, :, chunk(b)] = both.astype(BF)
                    tall = jnp.concatenate([value, jnp.zeros_like(value)], axis=0)
                    s.qn[h, chunk(b), :] = jnp.transpose(tall).astype(BF)
                else:
                    s.kta[h, :, chunk(b)] = both.astype(BF)
                    s.kn[h, chunk(b), :] = jnp.transpose(both).astype(BF)
            value = raw[2 * W + h * HD : 2 * W + (h + 1) * HD]
            s.vt[h * HD : (h + 1) * HD, chunk(b)] = value.astype(BF)
            s.vn[h, chunk(b), :] = jnp.transpose(jnp.concatenate([value, ones], axis=0)).astype(BF)

    first_norm(0)
    load_wo.wait()
    pl.semaphore_wait(barrier, len(peers))
    for copy in wo_sends:
        copy.start()
    s.vec[...] = jnp.zeros_like(s.vec)
    s.gacc[...] = jnp.zeros_like(s.gacc)
    s.gcol[0:W, :] = jnp.transpose(jnp.broadcast_to(s.qg[...].reshape(1, W), (128, W)))
    s.gcol[W:, :] = jnp.transpose(jnp.broadcast_to(s.kg[...].reshape(1, W), (128, W)))
    def window(b):
        return range(max(b - 1, 0), min(b + 2, CH))

    def self_score(b, h):
        query = s.qta[h, 0:HD, chunk(b)].astype(F32)
        key = s.kta[h, 0:HD, chunk(b)].astype(F32)
        return query, key, jnp.sum(query * key, axis=0, keepdims=True)

    units = [(b, i) for b in range(CH) for i in window(b)]

    def attend(b):
        pad_row = padded(b)
        pairs = [(h, i) for h in range(HEADS) for i in window(b)]
        scores = [nn(s.kn[h, chunk(i), :], s.qta[h, :, chunk(b)]) for h, i in pairs]
        totals, outs = [], []
        for h in range(HEADS):
            own = jnp.exp2(self_score(b, h)[2]) * pad_row
            totals.append(own)
            outs.append(s.vt[h * HD : (h + 1) * HD, chunk(b)].astype(F32) * own)
        for (h, i), score in zip(pairs, scores):
            weight = jnp.exp2(score)
            totals[h] = totals[h] + jnp.sum(weight, axis=0, keepdims=True)
            weight = weight.astype(BF)
            s.wgt[h, units.index((b, i))] = weight
            outs[h] = outs[h] + nn(s.vt[h * HD : (h + 1) * HD, chunk(i)], weight)
        for h in range(HEADS):
            inv = 1.0 / totals[h]
            s.inv[h, :, chunk(b)] = inv
            out = outs[h] * inv
            s.mixf[h * HD : (h + 1) * HD, chunk(b)] = out
            s.mixed[at(n * W + h * HD, HD, HD), chunk(b)] = out.astype(BF)

    def send_mixed(b):
        mix_z(b).start()
        mix_mate(b).start()

    load_w.wait()
    for load in load_rest:
        load.wait()
    for load in loads[6:]:
        load.start()
    project(0)
    project(1)
    attend(0)
    send_mixed(0)
    project(2)
    project(3)
    for b in range(1, CH):
        attend(b)
        send_mixed(b)

    load_dy.wait()
    load_dn.wait()
    s.gact[0 : T // 2, :] = nt(s.dy[0 : T // 2, :], s.dn[...])
    k.await_recvs(other_wo, wo_recv + 1)
    wo_pass.start()
    mix_z(0).wait_recv()
    mix_pass(0).start()
    s.gact[T // 2 :, :] = nt(s.dy[T // 2 :, :], s.dn[...])
    load_up.wait()
    k.await_recvs(s.wo.at[pl.ds(0, 2 * W)], wo_recv)

    def wait_mixed(b):
        k.await_recvs(s.mixed.at[pl.ds(0, 2 * W), chunk(b)], mix_sem + b)

    def out_product(b):
        s.big0[...] = tn(s.mixed[:, chunk(b)], s.wo[...])

    def pass_mixed(b):
        mix_z(b).wait_recv()
        mix_pass(b).start()

    def second_norm(b):
        for i in range(2):
            rows = slice(b * BLK + i * HALF, b * BLK + (i + 1) * HALF)
            hat, _ = moments(s.x[rows, :].astype(F32) + s.big0[i * HALF : (i + 1) * HALF, :])
            s.normed2[rows, :] = (hat * mg + msh).astype(BF)
        own = s.x[ar3.mine(b), :].astype(F32)
        s.mid[b] = own + s.big0[at(core * HALF, HALF, HALF), :]

    def gelu(b):
        for i in range(BLK // 8):
            out = slice(b * BLK + i * 8, b * BLK + (i + 1) * 8)
            pre = s.big1[i * 8 : (i + 1) * 8, :]
            square = pre * pre
            tanh = jnp.tanh(pre * (GELU_A + GELU_B * square))
            half = 0.5 + 0.5 * tanh
            slope = half + (0.5 * pre) * (1.0 - tanh * tanh) * (GELU_A + 3.0 * GELU_B * square)
            s.active[out, :] = (pre * half).astype(BF)
            s.gpre[out, :] = (s.gact[out, :] * slope).astype(BF)

    def mlp_part(b):
        rows = slice(b * BLK, (b + 1) * BLK)
        s.p2[rows, :] = nn(s.active[rows, :], s.dn[...]).astype(BF)

    def up_product(b):
        s.big1[...] = nn(s.normed2[b * BLK : (b + 1) * BLK, :], s.up[...])

    left, right = slice(0, D // 2), slice(D // 2, D)
    wait_mixed(0)
    out_product(0)
    pass_mixed(1)
    second_norm(0)
    up_product(0)
    for b in range(CH):
        rows = slice(b * BLK, (b + 1) * BLK)
        gelu(b)
        if 1 <= b <= SIDE:
            ar2.s1(b - 1)
        if b == 3:
            ar3.s2(2)
        if b == CH - 1:
            s.m1[:, left] = tn(s.active[...], s.dy[:, left]).astype(BF)
            wide(wide_1[:1], "step1")
            s.m1[:, right] = tn(s.active[...], s.dy[:, right]).astype(BF)
            wide(wide_1[1:], "step1")
        s.p3[rows, :] = nt(s.gpre[rows, :], s.up[...]).astype(BF)
        if b >= 1 and b + 1 < CH:
            second_norm(b + 1)
            if b + 1 >= SIDE:
                side_norm(b + 1).start()
        ar3.s1(b)
        if b == 0:
            wait_mixed(1)
            out_product(1)
            second_norm(1)
            pass_mixed(2)
            ar3.s2(0)
        if b + 1 < CH:
            up_product(b + 1)
            if b < SIDE:
                mlp_part(b)
        if b + 2 < CH:
            wait_mixed(b + 2)
            out_product(b + 2)
        if b + 3 < CH:
            pass_mixed(b + 3)
        if b == 1:
            ar3.s2(1)

    def second_back(b):
        ar3.d2(b).wait_recv()
        total = ar3.total(b)
        hat, rstd = moments(s.mid[b])
        s.vec[2:3, :] += 0.5 * jnp.sum(total * hat, axis=0, keepdims=True)
        s.vec[3:4, :] += 0.5 * jnp.sum(total, axis=0, keepdims=True)
        grad = s.dy[ar3.mine(b), :].astype(F32) + norm_back(total * mg, hat, rstd)
        s.gact[b * HALF : (b + 1) * HALF, :] = grad
        s.gattn[ar3.mine(b), :] = grad.astype(BF)
        ar3.d3(b).start()

    def key_sums(h, b):
        col = (b // 2 * HEADS + h) * 2 * HD
        return slice(T // 2 + b % 2 * BLK, T // 2 + (b % 2 + 1) * BLK), slice(col, col + 2 * HD)

    def head_back(grad, which, h, b):
        rows = slice(which * W + h * HD, which * W + (h + 1) * HD)
        hat = s.hat[rows, chunk(b)]
        s.gacc[rows, :] += grad * hat
        grad = grad * gain_col(which, h)
        grad = (
            grad
            - jnp.mean(grad, axis=0, keepdims=True)
            - hat * jnp.mean(grad * hat, axis=0, keepdims=True)
        )
        s.gproj[rows, chunk(b)] = (grad * s.rstd[which * HEADS + h, :, chunk(b)]).astype(BF)

    def attend_back(b):
        ar3.d3(b).wait_recv()
        grad_mixed = nt(s.wo[at(n * W, W, W), :], s.gattn[chunk(b), :])
        if b == CH - 1:
            s.m2[3 * W :, :] = nn(s.mixed[at(n * W, W, W), :], s.gattn[...]).astype(BF)
        pad_row = padded(b)
        wides, pairs, grad_queries = [], [], []
        for h in range(HEADS):
            rows = slice(h * HD, (h + 1) * HD)
            grad_out = grad_mixed[rows].astype(BF).astype(F32)
            inv = s.inv[h, :, chunk(b)]
            delta = jnp.sum(grad_out * s.mixf[rows, chunk(b)], axis=0, keepdims=True)
            scaled = grad_out * inv
            low = delta * inv
            high = low.astype(BF).astype(F32)
            extra = jnp.where(subs == 0, -high, jnp.where(subs == 1, high - low, 0.0))
            wides.append(jnp.concatenate([scaled, extra], axis=0).astype(BF))
            tall = jnp.concatenate([jnp.zeros_like(scaled), scaled], axis=0)
            tall = jnp.transpose(tall).astype(BF)
            pairs.append(jnp.concatenate([s.qn[h, chunk(b), :], tall], axis=0))
            qf, kf, own = self_score(b, h)
            own_prob = jnp.exp2(own) * inv * pad_row
            own_grad = jnp.sum(grad_out * s.vt[rows, chunk(b)].astype(F32), axis=0, keepdims=True)
            own_score = own_prob * (own_grad - delta)
            s.dkx[rows, chunk(b)] = qf * own_score
            s.dvx[rows, chunk(b)] = grad_out * own_prob
            grad_queries.append(kf * own_score)
        tasks = [(h, i) for h in range(HEADS) for i in window(b)]
        products, ahead = {}, 3
        grad_scores = [[] for _ in range(HEADS)]
        for t in range(len(tasks) + ahead):
            if t < len(tasks):
                h, i = tasks[t]
                products[t] = nn(s.vn[h, chunk(i), :], wides[h])
            if t < ahead:
                continue
            h, i = tasks[t - ahead]
            weight = s.wgt[h, units.index((b, i))]
            grad_score = (weight.astype(F32) * products.pop(t - ahead)).astype(BF)
            grad_scores[h].append(grad_score)
            both = nn(jnp.concatenate([grad_score, weight], axis=1), pairs[h])
            if b == max(i - 1, 0):
                s.gact[key_sums(h, i)] = both
            else:
                s.gact[key_sums(h, i)] += both
            if i == window(b)[-1]:
                keys = s.kta[h, 0:HD, window(b)[0] * BLK : (i + 1) * BLK]
                grad_queries[h] = grad_queries[h] + nn(
                    keys, jnp.concatenate(grad_scores[h], axis=0)
                )
        for h in range(HEADS):
            head_back(grad_queries[h] * (0.125 / SC), 0, h, b)

    def keys_back(b):
        for h in range(HEADS):
            rows = slice(h * HD, (h + 1) * HD)
            both = jnp.transpose(s.gact[key_sums(h, b)])
            head_back((both[0:HD] + s.dkx[rows, chunk(b)]) * 0.125, 1, h, b)
            grad_value = both[HD:] + s.dvx[rows, chunk(b)]
            s.gproj[2 * W + h * HD : 2 * W + (h + 1) * HD, chunk(b)] = grad_value.astype(BF)

    def first_part(b):
        s.big0[...] = tn(s.gproj[:, chunk(b)], s.wt[...])
        for i in range(2):
            rows = slice(b * BLK + i * HALF, b * BLK + (i + 1) * HALF)
            part = s.big0[i * HALF : (i + 1) * HALF, :]
            s.p4[rows, :] = part.astype(BF)
            s.vec[0:1, :] += jnp.sum(part * s.hat1[rows, :].astype(F32), axis=0, keepdims=True)
            s.vec[1:2, :] += jnp.sum(part, axis=0, keepdims=True)
        ar4.s1(b)

    def side_mlp(b):
        side_pass(b).wait_recv()
        rows = slice(b * BLK, (b + 1) * BLK)
        s.big0[...] = nn(s.n2s[rows, :], s.up[...])
        for i in range(BLK // 8):
            out = slice(b * BLK + i * 8, b * BLK + (i + 1) * 8)
            pre = s.big0[i * 8 : (i + 1) * 8, :]
            half = 0.5 + 0.5 * jnp.tanh(pre * (GELU_A + GELU_B * (pre * pre)))
            s.active[out, :] = (pre * half).astype(BF)
        s.gpre[rows, :] = nn(s.active[rows, :], s.dn[...]).astype(BF)
        ar2.d1_side(b).start()

    def pass_side(b):
        side_norm(b).wait_recv()
        side_pass(b).start()

    second_back(0)
    s.m0[:, left] = tn(s.normed2[...], s.gpre[:, left]).astype(BF)
    wide(wide_2[:1], "step1")
    ar3.s2(CH - 1)
    s.m0[:, right] = tn(s.normed2[...], s.gpre[:, right]).astype(BF)
    wide(wide_2[1:], "step1")
    attend_back(0)
    second_back(1)
    wide(wide_1, "step1b")
    ar2.s2(0)
    mlp_part(2)
    attend_back(1)
    keys_back(0)
    second_back(2)
    wide(wide_2, "step1b")
    first_part(0)
    ar2.s2(1)
    attend_back(2)
    keys_back(1)
    second_back(3)
    wide(wide_1, "step2")
    first_part(1)
    attend_back(3)
    keys_back(2)
    keys_back(3)
    wide(wide_2, "step2")
    s.m2[0 : 3 * W, left] = nn(s.gproj[...], s.normed[:, left]).astype(BF)
    wide(wide_3[:1], "step1")
    wide(wide_1, "step3")
    s.m2[0 : 3 * W, right] = nn(s.gproj[...], s.normed[:, right]).astype(BF)
    wide(wide_3[1:], "step1")
    ar2.s1(2)
    first_part(2)
    first_part(3)
    for which in range(2):
        rows = slice(which * W, (which + 1) * W)
        both = s.gacc[rows, 0:128] + s.gacc[rows, 128:256]
        s.vec[4 + which : 5 + which, 0:W] = jnp.sum(jnp.transpose(both), axis=0, keepdims=True)
    s.vecs[...] = s.vec[...]
    vec_c.start()
    for b in range(SIDE, CH):
        pass_side(b)
    wide(wide_2, "step3")
    ar4.s2(0)
    wide(wide_3, "step1b")
    wide(wide_1, "step4")
    ar4.s2(1)
    mlp_part(CH - 1)
    ar2.s1(CH - 1)

    def layer_out(b):
        ar2.d2(b).wait_recv()
        s.r22[b] = (s.mid[b] + ar2.total(b)).astype(BF)
        ar2.d3(b).start()
        lo_copy(b).start()

    def grad_tokens(b):
        ar4.d2(b).wait_recv()
        hat, rstd = moments(s.x[ar4.mine(b), :].astype(F32))
        s.r24[b] = (s.gact[b * HALF : (b + 1) * HALF, :] + norm_back(ar4.total(b) * ag, hat, rstd)).astype(BF)
        ar4.d3(b).start()
        gt_copy(b).start()

    upper = lax.broadcasted_iota(jnp.int32, (8, D), 0) < 4
    vec_c.wait_recv()
    s.v1[...] = s.vec[...] + jnp.where(upper, s.rvz[0], 0.0)
    s.rvx[k.x] = s.v1[...]
    for copy in vec_x:
        copy.start()
    side_mlp(2)
    wide(wide_3, "step2")
    wide(wide_2, "step4")
    wide(wide_1, "step5")
    for d in (1, 3):
        wide(wide_1, "step6", d)
    side_mlp(3)
    ar2.s2_side(2)
    k.await_recvs(s.rvx.at[pl.ds(0, 3)], vec_sem + 1)
    s.v2[...] = (s.rvx[0] + s.rvx[1]) + (s.rvx[2] + s.rvx[3])
    s.rvy[k.y] = s.v2[...]
    for copy in vec_y:
        copy.start()
    wide(wide_2, "step5")
    for d in (1, 3):
        wide(wide_2, "step6", d)
    ar2.s2_side(3)
    wide(wide_3, "step3")
    ar4.s2(2)
    ar2.s2(2)
    ar2.s2(3)
    layer_out(0)
    layer_out(1)
    grad_tokens(0)
    wide(wide_3, "step4")
    wide(wide_1, "step7")
    k.await_recvs(s.rvy.at[pl.ds(0, 3)], vec_sem + 2)
    s.v3[...] = (s.rvy[0] + s.rvy[1]) + (s.rvy[2] + s.rvy[3])
    vec_z.start()
    ar4.s2(3)
    wide(wide_2, "step7")
    grad_tokens(1)
    wide(wide_3, "step5")
    vec_z.wait_recv()
    s.v4[...] = s.v3[...] + s.rvz[1]
    vec_l.start()
    layer_out(2)
    grad_tokens(2)
    layer_out(3)
    vec_l.wait_recv()
    vec_out[...] = s.v4[...] + jnp.where(upper, s.rvz[2], 0.0)
    grad_tokens(3)

    half = pl.ds(0, T // 2)
    k.copy(s.p2.at[half], lo_out.at[half], out_sem).wait()
    k.copy(s.p4.at[half], gt_out.at[half], out_sem + 1).wait()
    for item in (ar2, ar3, ar4, *wide_1, *wide_2, *wide_3):
        item.finish()
    k.await_sends(s.wo.at[pl.ds(0, 3 * W)], wo_send)
    k.await_sends(s.mixed.at[pl.ds(0, 3 * W)], mix_send)
    k.await_sends(s.n2s.at[pl.ds(0, (CH - SIDE) * BLK)], side_send)
    k.await_sends(s.big0.at[pl.ds(0, 72)], vec_send)


PARTS = 4


def finish(lo, gt, gup, gdn, g2, vec, lo_o, gt_o, qkv_o, qg_o, kg_o, out_o, gup_o, gdn_o, ag_o, as_o, mg_o, ms_o, low, high, same, sem_in, sem_out):
    size = D // PARTS
    pieces = []
    for i, (src, dst) in enumerate(((gup, gup_o), (gdn, gdn_o), (g2, None))):
        for p in range(PARTS):
            rows = pl.ds(p * size, size)
            if dst is None:
                to = qkv_o.at[p] if p < 3 else out_o
            else:
                to = dst.at[rows]
            load = pltpu.make_async_copy(src.at[rows], low.at[i, rows], sem_in.at[i, p])
            pieces.append((load, (i, rows), pltpu.make_async_copy(high.at[i, rows], to, sem_out.at[i, p])))
    for i, (src, dst) in enumerate(((gt, gt_o), (lo, lo_o))):
        load = pltpu.make_async_copy(src, same.at[i], sem_in.at[3 + i, 0])
        store = pltpu.make_async_copy(same.at[i], dst, sem_out.at[3 + i, 0])
        pieces.insert(0, (load, None, store))
    for load, _, _ in pieces:
        load.start()
    for ref, row, count in (
        (ag_o, 0, D),
        (as_o, 1, D),
        (mg_o, 2, D),
        (ms_o, 3, D),
        (qg_o, 4, W),
        (kg_o, 5, W),
    ):
        ref[...] = vec[row : row + 1, 0:count].reshape(count)
    for load, cast, store in pieces:
        load.wait()
        if cast is not None:
            high[cast] = low[cast].astype(F32)
        store.start()
    for _, _, store in pieces:
        store.wait()


def body(*args):
    any_spec = pl.BlockSpec(memory_space=pl.ANY)
    vmem = pl.BlockSpec(memory_space=pltpu.VMEM)
    args = list(args)
    args[4] = jnp.swapaxes(args[4], 1, 2).reshape(3 * W, D)
    out = pl.pallas_call(
        kernel,
        out_shape=(
            jax.ShapeDtypeStruct((T, D), BF),
            jax.ShapeDtypeStruct((T, D), BF),
            jax.ShapeDtypeStruct((D, F), BF),
            jax.ShapeDtypeStruct((F, D), BF),
            jax.ShapeDtypeStruct((4 * W, D), BF),
            jax.ShapeDtypeStruct((8, D), F32),
        ),
        in_specs=[any_spec] * 14,
        out_specs=(any_spec, any_spec, any_spec, any_spec, any_spec, vmem),
        scratch_shapes=[pltpu.VMEM(shape, dtype) for shape, dtype in SCRATCH.values()]
        + [
            pltpu.SMEM((1,), jnp.int32),
            pltpu.SemaphoreType.DMA((NSEND,)),
            pltpu.SemaphoreType.DMA((NRECV,)),
            pltpu.SemaphoreType.DMA((NLOC,)),
        ],
        compiler_params=pltpu.CompilerParams(
            collective_id=0, has_side_effects=True, vmem_limit_bytes=60 * 1024 * 1024
        ),
        cost_estimate=pl.CostEstimate(
            flops=14 * 10**9, bytes_accessed=20 * 2**20, transcendentals=8 * 2**20
        ),
    )(*args)
    layer, tokens, qkv, *rest = pl.pallas_call(
        finish,
        out_shape=(
            jax.ShapeDtypeStruct((T, D), BF),
            jax.ShapeDtypeStruct((T, D), BF),
            jax.ShapeDtypeStruct((3, W, D), F32),
            jax.ShapeDtypeStruct((W,), F32),
            jax.ShapeDtypeStruct((W,), F32),
            jax.ShapeDtypeStruct((W, D), F32),
            jax.ShapeDtypeStruct((D, F), F32),
            jax.ShapeDtypeStruct((F, D), F32),
            jax.ShapeDtypeStruct((D,), F32),
            jax.ShapeDtypeStruct((D,), F32),
            jax.ShapeDtypeStruct((D,), F32),
            jax.ShapeDtypeStruct((D,), F32),
        ),
        in_specs=[any_spec] * 5 + [vmem],
        out_specs=(any_spec, any_spec, any_spec, vmem, vmem, any_spec, any_spec, any_spec)
        + (vmem,) * 4,
        scratch_shapes=[
            pltpu.VMEM((3, D, D), BF),
            pltpu.VMEM((3, D, D), F32),
            pltpu.VMEM((2, T, D), BF),
            pltpu.SemaphoreType.DMA((5, PARTS)),
            pltpu.SemaphoreType.DMA((5, PARTS)),
        ],
        compiler_params=pltpu.CompilerParams(vmem_limit_bytes=60 * 1024 * 1024),
        cost_estimate=pl.CostEstimate(flops=0, bytes_accessed=17 * 2**20, transcendentals=0),
    )(*out)
    return (layer, tokens, jnp.swapaxes(qkv, 1, 2), *rest)


def solution(mesh):
    placed = (
        P("wide", None),
        P("wide", None),
        P("wide", None),
        P("wide"),
        P(None, None, "narrow"),
        P("narrow"),
        P("narrow"),
        P("narrow", None),
        P(None, "narrow"),
        P("narrow", None),
        P(),
        P(),
        P(),
        P(),
    )
    return jax.shard_map(
        body,
        mesh=mesh,
        in_specs=placed,
        out_specs=(
            P("wide", None),
            P("wide", None),
            P(None, None, "narrow"),
            P("narrow"),
            P("narrow"),
            P("narrow", None),
            P(None, "narrow"),
            P("narrow", None),
            P(),
            P(),
            P(),
            P(),
        ),
        check_vma=False,
    )
```

```python
import jax
import jax.numpy as jnp
from jax import lax
from jax.experimental import pallas as pl
from jax.experimental.pallas import tpu as pltpu
from jax.sharding import PartitionSpec as P

T = 1024
D = 768
HEADS = 3
HD = 64
W = HEADS * HD
F = 768
BLK = 256
CH = T // BLK
HALF = BLK // 2
BIG = 512.0
MINUS = 31
LOG2E = 1.4426950408889634
SC = 0.125 * LOG2E
EPS = 1e-06
GELU_A = 0.7978845608028654
GELU_B = 0.044715 * GELU_A

BF = jnp.bfloat16
F32 = jnp.float32
MESH = pl.DeviceIdType.MESH


def nn(a, b):
    return lax.dot_general(a, b, (((1,), (0,)), ((), ())), preferred_element_type=F32)


def nt(a, b):
    return lax.dot_general(a, b, (((1,), (1,)), ((), ())), preferred_element_type=F32)


def tn(a, b):
    return lax.dot_general(a, b, (((0,), (0,)), ((), ())), preferred_element_type=F32)


def at(start, size, unit):
    return pl.ds(pl.multiple_of(start, unit), size)


def chunk(b):
    return at(b * BLK, BLK, BLK)


def moments(values):
    centre = values - jnp.mean(values, axis=-1, keepdims=True)
    rstd = lax.rsqrt(jnp.mean(centre * centre, axis=-1, keepdims=True) + EPS)
    return centre * rstd, rstd


def norm_back(grad, hat, rstd):
    return rstd * (
        grad
        - jnp.mean(grad, axis=-1, keepdims=True)
        - hat * jnp.mean(grad * hat, axis=-1, keepdims=True)
    )


SCRATCH = dict(
    seg=((1, T), jnp.int32),
    qg=((W,), F32),
    kg=((W,), F32),
    ag=((D,), F32),
    ash=((D,), F32),
    mg=((D,), F32),
    msh=((D,), F32),
    x=((T, D), BF),
    dy=((T, D), BF),
    wt=((3 * W, D), BF),
    wo=((4 * W, D), BF),
    up=((D, F), BF),
    dn=((F, D), BF),
    normed=((T, D), BF),
    hat1=((T, D), BF),
    qta=((HEADS, 2 * HD, T), BF),
    kta=((HEADS, 2 * HD, T), BF),
    vt=((W, T), BF),
    qn=((HEADS, T, 2 * HD), BF),
    kn=((HEADS, T, 2 * HD), BF),
    vn=((HEADS, T, 2 * HD), BF),
    hat=((2 * W, T), F32),
    rstd=((6, 1, T), F32),
    gcol=((2 * W, 128), F32),
    mixed=((4 * W, T), BF),
    mixf=((W, T), F32),
    mid=((CH, HALF, D), F32),
    wgt=((HEADS, 10, BLK, BLK), BF),
    inv=((HEADS, 1, T), F32),
    normed2=((T, D), BF),
    active=((T, F), BF),
    gpre=((T, F), BF),
    big0=((BLK, D), F32),
    gact=((T, F), F32),
    n2s=((T, D), BF),
    r12s=((CH, HALF, D), BF),
    big1=((BLK, D), F32),
    p2=((T, D), BF),
    p3=((T, D), BF),
    p4=((T, D), BF),
    r12=((CH, HALF, D), BF),
    r13=((CH, HALF, D), BF),
    r14=((CH, HALF, D), BF),
    r22=((CH, HALF, D), BF),
    r23=((CH, HALF, D), BF),
    r24=((CH, HALF, D), BF),
    gattn=((T, D), BF),
    dkx=((W, T), F32),
    dvx=((W, T), F32),
    gproj=((3 * W, T), BF),
    gacc=((2 * W, BLK), F32),
    m0=((D, F), BF),
    m1=((F, D), BF),
    m2=((4 * W, D), BF),
    vec=((8, D), F32),
    vecs=((8, D), F32),
    rvx=((4, 8, D), F32),
    rvy=((4, 8, D), F32),
    rvz=((3, 8, D), F32),
    v1=((8, D), F32),
    v2=((8, D), F32),
    v3=((8, D), F32),
    v4=((8, D), F32),
)
SIDE = 2
RELAYED = "abcd"
for _s, _w in ((_c, D // 2) for _c in "abcdef"):
    SCRATCH["rs1" + _s] = ((4, 96, _w), BF)
    SCRATCH["ra" + _s] = ((2, 96, _w), BF)
    SCRATCH["rb" + _s] = ((2, 96, _w), BF)
    SCRATCH["s1" + _s] = ((192, _w), BF)
    SCRATCH["rs2" + _s] = ((3, 48, _w), BF)
    SCRATCH["s2" + _s] = ((48, _w), BF)
    SCRATCH["rz" + _s] = ((48, _w), BF)
    SCRATCH["rr" + _s] = ((192, _w), BF)
    if _s in RELAYED:
        SCRATCH["nb" + _s] = ((2, 192, _w), BF)

NSEND, NRECV, NLOC = 20, 78, 17


class Wide:
    def __init__(self, k, send, recv, local, name, mat, cols, out, first, second):
        self.k, self.s, self.mat, self.cols, self.out = k, k.s, mat, cols, out
        self.name = name
        self.first, self.second = first, second
        self.u, self.t = k.coord(first), k.coord(second)
        self.relayed = name in RELAYED
        self.send = send
        self.lead = first == "x"
        self.recv, self.own_recv = recv, None if self.relayed else k.recvs(3)
        self.local = local

    def await_both(self, rows, recv):
        if self.lead:
            self.k.await_recvs(self.mat.at[pl.ds(0, rows)], self.recv + recv)

    def ref(self, what):
        return getattr(self.s, what + self.name)

    def half(self, q, i):
        return at(lax.rem(self.u + q + 4, 4) * 192 + i * 96, 96, 96)

    def rs1(self, i):
        k = self.k
        if i < 4:
            q, part = ((2, 0), (2, 1), (1, 1), (-1, 0))[i]
            src = self.mat.at[self.half(q, part), self.cols]
        else:
            src = self.ref("rb").at[i - 4]
        dst = self.ref("ra").at[i] if i < 2 else self.ref("rs1").at[i - 2]
        return k.remote(
            src,
            dst,
            self.send,
            self.recv + (0 if i < 2 else 1),
            k.along(self.first, 1 if i % 2 == 0 else 3),
        )

    def rs2(self, d):
        k = self.k
        q = lax.rem(self.t + d, 4)
        return k.remote(
            self.ref("s1").at[at(q * 48, 48, 48)],
            self.ref("rs2").at[d - 1],
            self.send + 1,
            self.recv + 2,
            k.along(self.second, d),
        )

    def zz(self):
        return self.k.remote(self.ref("s2"), self.ref("rz"), self.send + 1, self.recv + 3, self.k.zhi)

    def ag2(self, d):
        piece = self.ref("rr").at[at(self.t * 48, 48, 48)]
        recv = self.recv + 4 if self.relayed else self.own_recv + d - 1
        return self.k.remote(piece, piece, self.send + 1, recv, self.k.along(self.second, d))

    def rows_out(self, u, start=0, size=192):
        return self.out.at[at(lax.rem(u + 4, 4) * 192 + start, size, 96), self.cols]

    def ag1(self, d):
        dst = self.ref("nb").at[0 if d == 1 else 1]
        return self.k.remote(
            self.ref("rr"), dst, self.send + 2, self.recv + 5, self.k.along(self.first, d)
        )

    def piece(self, d, e):
        start = lax.rem(self.t + 4 - e, 4) * 48
        return self.k.remote(
            self.ref("rr").at[at(start, 48, 48)],
            self.out.at[at(self.u * 192 + start, 48, 48), self.cols],
            self.send + 2,
            self.recv + 6,
            self.k.along(self.first, d),
        )

    def forward(self, d):
        u, start = (self.u - 1, 0) if d == 1 else (self.u + 1, 96)
        src = self.ref("nb").at[0 if d == 1 else 1, pl.ds(start, 96)]
        return self.k.remote(
            src,
            self.rows_out(u, start, 96),
            self.send + 2,
            self.recv + 6,
            self.k.along(self.first, d),
        )

    def own(self, i=0):
        if i == 0:
            return self.k.copy(self.ref("rr"), self.rows_out(self.u), self.local)
        u = self.u - 1 if i == 1 else self.u + 1
        return self.k.copy(self.ref("nb").at[i - 1], self.rows_out(u), self.local)

    def step1(self):
        for i in range(4):
            self.rs1(i).start()

    def step1b(self):
        self.await_both(192, 0)
        for i, (q, part) in enumerate(((1, 0), (-1, 1))):
            own = self.mat[self.half(q, part), self.cols].astype(F32)
            self.ref("rb")[i] = (own + self.ref("ra")[i].astype(F32)).astype(BF)
            self.rs1(4 + i).start()

    def step2(self):
        self.await_both(384, 1)
        rs1, s1 = self.ref("rs1"), self.ref("s1")
        for i, (one, two) in enumerate(((1, 2), (0, 3))):
            total = self.mat[self.half(0, i), self.cols].astype(F32)
            total = total + (rs1[one].astype(F32) + rs1[two].astype(F32))
            s1[i * 96 : (i + 1) * 96, :] = total.astype(BF)
        for d in (2, 1, 3):
            self.rs2(d).start()

    def step3(self):
        self.await_both(144, 2)
        total = self.ref("s1")[at(self.t * 48, 48, 48), :].astype(F32)
        for d in range(3):
            total = total + self.ref("rs2")[d].astype(F32)
        self.ref("s2")[...] = total.astype(BF)
        self.zz().start()

    def step4(self):
        self.await_both(48, 3)
        total = self.ref("s2")[...].astype(F32) + self.ref("rz")[...].astype(F32)
        self.ref("rr")[at(self.t * 48, 48, 48), :] = total.astype(BF)
        for d in (2, 1, 3):
            self.ag2(d).start()
        if not self.relayed:
            for d in (2, 1, 3):
                self.piece(d, 0).start()

    def step5(self):
        if self.relayed:
            self.await_both(144, 4)
        else:
            for e in (1, 3, 2):
                self.ag2(e).wait_recv()
                for d in (2, 1, 3):
                    self.piece(d, e).start()
        self.own().start()

    def step6(self, d):
        self.ag1(d).start()

    def step7(self):
        self.await_both(384, 5)
        for d in (1, 3):
            self.forward(d).start()
        for i in (1, 2):
            self.own(i).start()

    def finish(self):
        k = self.k
        most = (pl.ds(0, 576), self.cols)
        if self.relayed:
            self.await_both(192, 6)
            k.copy(self.mat.at[most], self.out.at[most], self.local).wait()
        else:
            self.await_both(576, 6)
            self.own().wait()
        if self.first == "x":
            k.await_sends(self.mat.at[pl.ds(0, 576)], self.send)
            k.await_sends(self.mat.at[pl.ds(0, 336)], self.send + 1)
            k.await_sends(self.mat.at[pl.ds(0, 576)], self.send + 2)


class Narrow:
    def __init__(self, k, part, r1, r2, result, joint=True, side=None):
        self.k, self.part, self.r1, self.r2, self.result = k, part, r1, r2, result
        self.side = side
        self.joint = joint
        self.send = k.sends(2 if side is None else 3)
        self.recv = k.recvs((2 * CH + 1 if joint else 3 * CH) + (0 if side is None else CH - SIDE))

    def mine(self, b):
        return at(b * BLK + self.k.core * HALF, HALF, HALF)

    def theirs(self, b):
        return at(b * BLK + (1 - self.k.core) * HALF, HALF, HALF)

    def d1(self, b):
        return self.k.remote(
            self.part.at[self.theirs(b)], self.r1.at[b], self.send, self.recv + b, self.k.mate
        )

    def d2(self, b):
        if self.side is None or b < SIDE:
            src, device = self.part, self.k.zlo
        else:
            src, device = self.side[0], self.k.side
        return self.k.remote(
            src.at[self.mine(b)], self.r2.at[b], self.send, self.recv + CH + b, device
        )

    def d3(self, b):
        src, dst = self.result(b, self.mine(b))
        recv = self.recv + 2 * CH + (0 if self.joint else b)
        return self.k.remote(src, dst, self.send + 1, recv, self.k.mate)

    def s1(self, b):
        self.d1(b).start()

    def s2(self, b):
        self.d1(b).wait_recv()
        total = self.part[self.mine(b), :].astype(F32) + self.r1[b].astype(F32)
        self.part[self.mine(b), :] = total.astype(BF)
        if self.side is None or b < SIDE:
            self.d2(b).start()

    def d1_side(self, b):
        part, r1 = self.side
        return self.k.remote(
            part.at[self.theirs(b)],
            r1.at[b],
            self.send + 2,
            self.recv + 2 * CH + 1 + b - SIDE,
            self.k.mate,
        )

    def s2_side(self, b):
        part, r1 = self.side
        self.d1_side(b).wait_recv()
        total = part[self.mine(b), :].astype(F32) + r1[b].astype(F32)
        part[self.mine(b), :] = total.astype(BF)
        self.d2(b).start()

    def total(self, b):
        return self.part[self.mine(b), :].astype(F32) + self.r2[b].astype(F32)

    def finish(self):
        k, half = self.k, self.part.at[pl.ds(0, T // 2)]
        if self.joint:
            k.await_recvs(half, self.recv + 2 * CH)
        k.await_sends(self.part, self.send)
        k.await_sends(half, self.send + 1)
        if self.side is not None:
            k.await_sends(self.part.at[pl.ds(0, (CH - SIDE) * HALF)], self.send + 2)


class Names:
    pass


class Kernel:
    def __init__(self, s, send, recv, loc):
        self.s, self.send, self.recv, self.loc = s, send, recv, loc
        self.taken = {}
        w = lax.axis_index("wide")
        n = lax.axis_index("narrow")
        self.w, self.n = w, n
        self.x = lax.rem(w, 4)
        self.y = lax.rem(lax.div(w, 4), 4)
        self.z = lax.div(w, 16)
        self.core = lax.rem(n, 2)
        self.n1 = n + 1 - 2 * self.core
        self.n2 = lax.rem(n + 2, 4)
        self.mate = (w, self.n1)
        self.zlo = (w, self.n2)
        self.zhi = (lax.rem(w + 16, 32), n)
        self.side = (lax.rem(w + 16, 32), self.n2)

    def coord(self, axis):
        return self.x if axis == "x" else self.y

    def along(self, axis, d):
        if axis == "x":
            return (self.w - self.x + lax.rem(self.x + d, 4), self.n)
        return (self.w - 4 * self.y + 4 * lax.rem(self.y + d, 4), self.n)

    def take(self, kind, count, most):
        start = self.taken.get(kind, 0)
        self.taken[kind] = start + count
        assert start + count <= most, (kind, start + count, most)
        return start

    def sends(self, count):
        return self.take("send", count, NSEND)

    def recvs(self, count):
        return self.take("recv", count, NRECV)

    def locals(self, count):
        return self.take("local", count, NLOC)

    def remote(self, src, dst, send, recv, device):
        return pltpu.make_async_remote_copy(
            src_ref=src,
            dst_ref=dst,
            send_sem=self.send.at[send],
            recv_sem=self.recv.at[recv],
            device_id=device,
            device_id_type=MESH,
        )

    def await_sends(self, ref, send):
        self.remote(ref, ref, send, 0, self.mate).wait_send()

    def await_recvs(self, ref, recv):
        self.remote(ref, ref, 0, recv, self.mate).wait_recv()

    def copy(self, src, dst, sem):
        return pltpu.make_async_copy(src, dst, self.loc.at[sem])


def kernel(
    x_in,
    dy_in,
    seg_in,
    pad_in,
    wt_in,
    qg_in,
    kg_in,
    wo_in,
    up_in,
    dn_in,
    ag_in,
    as_in,
    mg_in,
    ms_in,
    lo_out,
    gt_out,
    gup_out,
    gdn_out,
    g2_out,
    vec_out,
    *scratch,
):
    s = Names()
    for name, ref in zip(SCRATCH, scratch):
        setattr(s, name, ref)
    pad_smem, *semaphores = scratch[len(SCRATCH) :]
    k = Kernel(s, *semaphores)
    n, core = k.n, k.core

    own_wo = s.wo.at[at(n * W, W, W)]
    pieces = [pl.ds(b * BLK, BLK) for b in range(CH)]
    loads = [
        (x_in.at[pieces[0]], s.x.at[pieces[0]]),
        (wt_in, s.wt),
        (wo_in, own_wo),
        *[(x_in.at[rows], s.x.at[rows]) for rows in pieces[1:]],
        (up_in, s.up),
        (dn_in, s.dn),
        (dy_in, s.dy),
    ]
    load_sem = k.locals(len(loads))
    loads = [k.copy(src, dst, load_sem + i) for i, (src, dst) in enumerate(loads)]
    smalls = [
        (ag_in, s.ag),
        (as_in, s.ash),
        (qg_in, s.qg),
        (kg_in, s.kg),
        (seg_in, s.seg),
        (pad_in, pad_smem),
        (mg_in, s.mg),
        (ms_in, s.msh),
    ]
    small_sem = k.locals(len(smalls))
    smalls = [k.copy(src, dst, small_sem + i) for i, (src, dst) in enumerate(smalls)]
    loads[0].start()
    for load in smalls + loads[1:6]:
        load.start()
    load_x, load_w, load_wo, *load_rest, load_up, load_dn, load_dy = loads

    barrier = pltpu.get_barrier_semaphore()
    peers = [k.mate, k.zlo, k.zhi, k.side]
    peers += [k.along(axis, d) for axis in "xy" for d in (1, 2, 3)]
    for peer in peers:
        pl.semaphore_signal(barrier, inc=1, device_id=peer, device_id_type=MESH)

    wo_send, wo_recv = k.sends(1), k.recvs(2)
    own_low = s.wo.at[at(n * W, W // 3, W // 3)]
    own_high = s.wo.at[at(n * W + W // 3, 2 * W // 3, W // 3)]
    other_wo = s.wo.at[at(k.n2 * W, W, W)]
    wo_sends = [
        k.remote(own_wo, own_wo, wo_send, wo_recv, k.mate),
        k.remote(own_low, own_low, wo_send, wo_recv + 1, k.zlo),
        k.remote(own_high, own_high, wo_send, wo_recv + 1, k.side),
    ]
    wo_pass = k.remote(other_wo, other_wo, wo_send, wo_recv, k.mate)
    mix_send, mix_sem = k.sends(1), k.recvs(2 * CH)

    def mix_mate(b):
        ref = s.mixed.at[at(n * W, W, W), chunk(b)]
        return k.remote(ref, ref, mix_send, mix_sem + b, k.mate)

    def mix_z(b):
        ref = s.mixed.at[at(n * W, W, W), chunk(b)]
        return k.remote(ref, ref, mix_send, mix_sem + CH + b, k.zlo)

    def mix_pass(b):
        ref = s.mixed.at[at(k.n2 * W, W, W), chunk(b)]
        return k.remote(ref, ref, mix_send, mix_sem + b, k.mate)

    ar2 = Narrow(k, s.p2, s.r12, s.r22, lambda b, rows: (s.r22.at[b], lo_out.at[rows]), side=(s.gpre, s.r12s))
    ar3 = Narrow(k, s.p3, s.r13, s.r23, lambda b, rows: (s.gattn.at[rows], s.gattn.at[rows]), joint=False)
    ar4 = Narrow(k, s.p4, s.r14, s.r24, lambda b, rows: (s.r24.at[b], gt_out.at[rows]))
    low_cols, high_cols = pl.ds(0, D // 2), pl.ds(D // 2, D // 2)
    wide_sems = [(k.sends(3), k.recvs(7)) for _ in range(3)]
    wide_1 = Wide(k, *wide_sems[0], 2, "a", s.m1, low_cols, gdn_out, "x", "y"), Wide(k, *wide_sems[0], 3, "b", s.m1, high_cols, gdn_out, "y", "x")
    wide_2 = Wide(k, *wide_sems[1], 4, "c", s.m0, low_cols, gup_out, "x", "y"), Wide(k, *wide_sems[1], 5, "d", s.m0, high_cols, gup_out, "y", "x")
    wide_3 = Wide(k, *wide_sems[2], 6, "e", s.m2, low_cols, g2_out, "x", "y"), Wide(k, *wide_sems[2], 7, "f", s.m2, high_cols, g2_out, "y", "x")

    def wide(pair, step, *args):
        for item in pair:
            getattr(item, step)(*args)

    vec_send, vec_sem = k.sends(1), k.recvs(5)
    vec_c = k.remote(s.vecs, s.rvz.at[0], vec_send, vec_sem, k.mate)
    vec_x = [
        k.remote(s.v1, s.rvx.at[k.x], vec_send, vec_sem + 1, k.along("x", d)) for d in (1, 2, 3)
    ]
    vec_y = [
        k.remote(s.v2, s.rvy.at[k.y], vec_send, vec_sem + 2, k.along("y", d)) for d in (1, 2, 3)
    ]
    vec_z = k.remote(s.v3, s.rvz.at[1], vec_send, vec_sem + 3, k.zhi)
    vec_l = k.remote(s.v4, s.rvz.at[2], vec_send, vec_sem + 4, k.zlo)
    out_sem = 0

    side_send, side_sem = k.sends(1), k.recvs(2 * (CH - SIDE))

    def side_norm(b):
        rows = ar2.mine(b)
        return k.remote(s.normed2.at[rows], s.n2s.at[rows], side_send, side_sem + b - SIDE, k.side)

    def side_pass(b):
        rows = ar2.mine(b)
        return k.remote(s.n2s.at[rows], s.n2s.at[rows], side_send, side_sem + CH - SIDE + b - SIDE, k.mate)

    def lo_copy(b):
        return k.copy(s.r22.at[b], lo_out.at[ar2.mine(b)], out_sem)

    def gt_copy(b):
        return k.copy(s.r24.at[b], gt_out.at[ar4.mine(b)], out_sem + 1)


    for load in smalls:
        load.wait()
    load_x.wait()

    ag = s.ag[...].reshape(1, D)
    ash = s.ash[...].reshape(1, D)
    mg = s.mg[...].reshape(1, D)
    msh = s.msh[...].reshape(1, D)

    def gain_col(c, h):
        col = s.gcol[c * W + h * HD : c * W + (h + 1) * HD, :]
        return jnp.concatenate([col, col], axis=1)

    lanes = lax.broadcasted_iota(jnp.int32, (1, BLK), 1)
    subs = lax.broadcasted_iota(jnp.int32, (HD, BLK), 0)

    limit = T - pad_smem[0]

    def padded(b):
        return jnp.where(lanes + b * BLK >= limit, 1.0, 0.0)

    def first_norm(b):
        for i in range(2):
            rows = slice(b * BLK + i * HALF, b * BLK + (i + 1) * HALF)
            hat, _ = moments(s.x[rows, :].astype(F32))
            s.hat1[rows, :] = hat.astype(BF)
            s.normed[rows, :] = (hat * ag + ash).astype(BF)

    def project(b):
        raw = nt(s.wt[...], s.normed[chunk(b), :])
        if b + 1 < CH:
            first_norm(b + 1)
        same = jnp.where(subs == s.seg[:, chunk(b)], 1.0, 0.0)
        same_valid = same * (1.0 - padded(b))
        query_rows = jnp.where(subs == MINUS, -BIG, BIG * same)
        key_rows = jnp.where(subs == MINUS, 1.0, same_valid)
        ones = jnp.where(subs < 2, 1.0, 0.0)
        for h in range(HEADS):
            for which in range(2):
                rows = slice(which * W + h * HD, which * W + (h + 1) * HD)
                value = raw[rows]
                centre = value - jnp.mean(value, axis=0, keepdims=True)
                rstd = lax.rsqrt(jnp.mean(centre * centre, axis=0, keepdims=True) + EPS)
                hat = centre * rstd
                s.hat[rows, chunk(b)] = hat
                s.rstd[which * HEADS + h, :, chunk(b)] = rstd
                value = hat * gain_col(which, h) * (1.0, SC)[which]
                both = jnp.concatenate([value, (query_rows, key_rows)[which]], axis=0)
                if which == 0:
                    s.qta[h, :, chunk(b)] = both.astype(BF)
                    tall = jnp.concatenate([value, jnp.zeros_like(value)], axis=0)
                    s.qn[h, chunk(b), :] = jnp.transpose(tall).astype(BF)
                else:
                    s.kta[h, :, chunk(b)] = both.astype(BF)
                    s.kn[h, chunk(b), :] = jnp.transpose(both).astype(BF)
            value = raw[2 * W + h * HD : 2 * W + (h + 1) * HD]
            s.vt[h * HD : (h + 1) * HD, chunk(b)] = value.astype(BF)
            s.vn[h, chunk(b), :] = jnp.transpose(jnp.concatenate([value, ones], axis=0)).astype(BF)

    first_norm(0)
    load_wo.wait()
    pl.semaphore_wait(barrier, len(peers))
    for copy in wo_sends:
        copy.start()
    s.vec[...] = jnp.zeros_like(s.vec)
    s.gacc[...] = jnp.zeros_like(s.gacc)
    s.gcol[0:W, :] = jnp.transpose(jnp.broadcast_to(s.qg[...].reshape(1, W), (128, W)))
    s.gcol[W:, :] = jnp.transpose(jnp.broadcast_to(s.kg[...].reshape(1, W), (128, W)))
    def window(b):
        return range(max(b - 1, 0), min(b + 2, CH))

    def self_score(b, h):
        query = s.qta[h, 0:HD, chunk(b)].astype(F32)
        key = s.kta[h, 0:HD, chunk(b)].astype(F32)
        return query, key, jnp.sum(query * key, axis=0, keepdims=True)

    units = [(b, i) for b in range(CH) for i in window(b)]

    def attend(b):
        pad_row = padded(b)
        pairs = [(h, i) for h in range(HEADS) for i in window(b)]
        scores = [nn(s.kn[h, chunk(i), :], s.qta[h, :, chunk(b)]) for h, i in pairs]
        totals, outs = [], []
        for h in range(HEADS):
            own = jnp.exp2(self_score(b, h)[2]) * pad_row
            totals.append(own)
            outs.append(s.vt[h * HD : (h + 1) * HD, chunk(b)].astype(F32) * own)
        for (h, i), score in zip(pairs, scores):
            weight = jnp.exp2(score)
            totals[h] = totals[h] + jnp.sum(weight, axis=0, keepdims=True)
            weight = weight.astype(BF)
            s.wgt[h, units.index((b, i))] = weight
            outs[h] = outs[h] + nn(s.vt[h * HD : (h + 1) * HD, chunk(i)], weight)
        for h in range(HEADS):
            inv = 1.0 / totals[h]
            s.inv[h, :, chunk(b)] = inv
            out = outs[h] * inv
            s.mixf[h * HD : (h + 1) * HD, chunk(b)] = out
            s.mixed[at(n * W + h * HD, HD, HD), chunk(b)] = out.astype(BF)

    def send_mixed(b):
        mix_z(b).start()
        mix_mate(b).start()

    load_w.wait()
    for load in load_rest:
        load.wait()
    for load in loads[6:]:
        load.start()
    project(0)
    project(1)
    attend(0)
    send_mixed(0)
    project(2)
    project(3)
    for b in range(1, CH):
        attend(b)
        send_mixed(b)

    load_dy.wait()
    load_dn.wait()
    s.gact[0 : T // 2, :] = nt(s.dy[0 : T // 2, :], s.dn[...])
    k.await_recvs(other_wo, wo_recv + 1)
    wo_pass.start()
    mix_z(0).wait_recv()
    mix_pass(0).start()
    s.gact[T // 2 :, :] = nt(s.dy[T // 2 :, :], s.dn[...])
    load_up.wait()
    k.await_recvs(s.wo.at[pl.ds(0, 2 * W)], wo_recv)

    def wait_mixed(b):
        k.await_recvs(s.mixed.at[pl.ds(0, 2 * W), chunk(b)], mix_sem + b)

    def out_product(b):
        s.big0[...] = tn(s.mixed[:, chunk(b)], s.wo[...])

    def pass_mixed(b):
        mix_z(b).wait_recv()
        mix_pass(b).start()

    def second_norm(b):
        for i in range(2):
            rows = slice(b * BLK + i * HALF, b * BLK + (i + 1) * HALF)
            hat, _ = moments(s.x[rows, :].astype(F32) + s.big0[i * HALF : (i + 1) * HALF, :])
            s.normed2[rows, :] = (hat * mg + msh).astype(BF)
        own = s.x[ar3.mine(b), :].astype(F32)
        s.mid[b] = own + s.big0[at(core * HALF, HALF, HALF), :]

    def gelu(b):
        for i in range(BLK // 8):
            out = slice(b * BLK + i * 8, b * BLK + (i + 1) * 8)
            pre = s.big1[i * 8 : (i + 1) * 8, :]
            square = pre * pre
            tanh = jnp.tanh(pre * (GELU_A + GELU_B * square))
            half = 0.5 + 0.5 * tanh
            slope = half + (0.5 * pre) * (1.0 - tanh * tanh) * (GELU_A + 3.0 * GELU_B * square)
            s.active[out, :] = (pre * half).astype(BF)
            s.gpre[out, :] = (s.gact[out, :] * slope).astype(BF)

    def mlp_part(b):
        rows = slice(b * BLK, (b + 1) * BLK)
        s.p2[rows, :] = nn(s.active[rows, :], s.dn[...]).astype(BF)

    def up_product(b):
        s.big1[...] = nn(s.normed2[b * BLK : (b + 1) * BLK, :], s.up[...])

    left, right = slice(0, D // 2), slice(D // 2, D)
    wait_mixed(0)
    out_product(0)
    pass_mixed(1)
    second_norm(0)
    up_product(0)
    for b in range(CH):
        rows = slice(b * BLK, (b + 1) * BLK)
        gelu(b)
        if 1 <= b <= SIDE:
            ar2.s1(b - 1)
        if b == 3:
            ar3.s2(2)
        if b == CH - 1:
            s.m1[:, left] = tn(s.active[...], s.dy[:, left]).astype(BF)
            wide(wide_1[:1], "step1")
            s.m1[:, right] = tn(s.active[...], s.dy[:, right]).astype(BF)
            wide(wide_1[1:], "step1")
        s.p3[rows, :] = nt(s.gpre[rows, :], s.up[...]).astype(BF)
        if b >= 1 and b + 1 < CH:
            second_norm(b + 1)
            if b + 1 >= SIDE:
                side_norm(b + 1).start()
        ar3.s1(b)
        if b == 0:
            wait_mixed(1)
            out_product(1)
            second_norm(1)
            pass_mixed(2)
            ar3.s2(0)
        if b + 1 < CH:
            up_product(b + 1)
            if b < SIDE:
                mlp_part(b)
        if b + 2 < CH:
            wait_mixed(b + 2)
            out_product(b + 2)
        if b + 3 < CH:
            pass_mixed(b + 3)
        if b == 1:
            ar3.s2(1)

    def second_back(b):
        ar3.d2(b).wait_recv()
        total = ar3.total(b)
        hat, rstd = moments(s.mid[b])
        s.vec[2:3, :] += 0.5 * jnp.sum(total * hat, axis=0, keepdims=True)
        s.vec[3:4, :] += 0.5 * jnp.sum(total, axis=0, keepdims=True)
        grad = s.dy[ar3.mine(b), :].astype(F32) + norm_back(total * mg, hat, rstd)
        s.gact[b * HALF : (b + 1) * HALF, :] = grad
        s.gattn[ar3.mine(b), :] = grad.astype(BF)
        ar3.d3(b).start()

    def key_sums(h, b):
        col = (b // 2 * HEADS + h) * 2 * HD
        return slice(T // 2 + b % 2 * BLK, T // 2 + (b % 2 + 1) * BLK), slice(col, col + 2 * HD)

    def head_back(grad, which, h, b):
        rows = slice(which * W + h * HD, which * W + (h + 1) * HD)
        hat = s.hat[rows, chunk(b)]
        s.gacc[rows, :] += grad * hat
        grad = grad * gain_col(which, h)
        grad = (
            grad
            - jnp.mean(grad, axis=0, keepdims=True)
            - hat * jnp.mean(grad * hat, axis=0, keepdims=True)
        )
        s.gproj[rows, chunk(b)] = (grad * s.rstd[which * HEADS + h, :, chunk(b)]).astype(BF)

    def attend_back(b):
        ar3.d3(b).wait_recv()
        grad_mixed = nt(s.wo[at(n * W, W, W), :], s.gattn[chunk(b), :])
        if b == CH - 1:
            s.m2[3 * W :, :] = nn(s.mixed[at(n * W, W, W), :], s.gattn[...]).astype(BF)
        pad_row = padded(b)
        wides, pairs, grad_queries = [], [], []
        for h in range(HEADS):
            rows = slice(h * HD, (h + 1) * HD)
            grad_out = grad_mixed[rows].astype(BF).astype(F32)
            inv = s.inv[h, :, chunk(b)]
            delta = jnp.sum(grad_out * s.mixf[rows, chunk(b)], axis=0, keepdims=True)
            scaled = grad_out * inv
            low = delta * inv
            high = low.astype(BF).astype(F32)
            extra = jnp.where(subs == 0, -high, jnp.where(subs == 1, high - low, 0.0))
            wides.append(jnp.concatenate([scaled, extra], axis=0).astype(BF))
            tall = jnp.concatenate([jnp.zeros_like(scaled), scaled], axis=0)
            tall = jnp.transpose(tall).astype(BF)
            pairs.append(jnp.concatenate([s.qn[h, chunk(b), :], tall], axis=0))
            qf, kf, own = self_score(b, h)
            own_prob = jnp.exp2(own) * inv * pad_row
            own_grad = jnp.sum(grad_out * s.vt[rows, chunk(b)].astype(F32), axis=0, keepdims=True)
            own_score = own_prob * (own_grad - delta)
            s.dkx[rows, chunk(b)] = qf * own_score
            s.dvx[rows, chunk(b)] = grad_out * own_prob
            grad_queries.append(kf * own_score)
        tasks = [(h, i) for h in range(HEADS) for i in window(b)]
        products, ahead = {}, 3
        grad_scores = [[] for _ in range(HEADS)]
        for t in range(len(tasks) + ahead):
            if t < len(tasks):
                h, i = tasks[t]
                products[t] = nn(s.vn[h, chunk(i), :], wides[h])
            if t < ahead:
                continue
            h, i = tasks[t - ahead]
            weight = s.wgt[h, units.index((b, i))]
            grad_score = (weight.astype(F32) * products.pop(t - ahead)).astype(BF)
            grad_scores[h].append(grad_score)
            both = nn(jnp.concatenate([grad_score, weight], axis=1), pairs[h])
            if b == max(i - 1, 0):
                s.gact[key_sums(h, i)] = both
            else:
                s.gact[key_sums(h, i)] += both
            if i == window(b)[-1]:
                keys = s.kta[h, 0:HD, window(b)[0] * BLK : (i + 1) * BLK]
                grad_queries[h] = grad_queries[h] + nn(
                    keys, jnp.concatenate(grad_scores[h], axis=0)
                )
        for h in range(HEADS):
            head_back(grad_queries[h] * (0.125 / SC), 0, h, b)

    def keys_back(b):
        for h in range(HEADS):
            rows = slice(h * HD, (h + 1) * HD)
            both = jnp.transpose(s.gact[key_sums(h, b)])
            head_back((both[0:HD] + s.dkx[rows, chunk(b)]) * 0.125, 1, h, b)
            grad_value = both[HD:] + s.dvx[rows, chunk(b)]
            s.gproj[2 * W + h * HD : 2 * W + (h + 1) * HD, chunk(b)] = grad_value.astype(BF)

    def first_part(b):
        s.big0[...] = tn(s.gproj[:, chunk(b)], s.wt[...])
        for i in range(2):
            rows = slice(b * BLK + i * HALF, b * BLK + (i + 1) * HALF)
            part = s.big0[i * HALF : (i + 1) * HALF, :]
            s.p4[rows, :] = part.astype(BF)
            s.vec[0:1, :] += jnp.sum(part * s.hat1[rows, :].astype(F32), axis=0, keepdims=True)
            s.vec[1:2, :] += jnp.sum(part, axis=0, keepdims=True)
        ar4.s1(b)

    def side_mlp(b):
        side_pass(b).wait_recv()
        rows = slice(b * BLK, (b + 1) * BLK)
        s.big0[...] = nn(s.n2s[rows, :], s.up[...])
        for i in range(BLK // 8):
            out = slice(b * BLK + i * 8, b * BLK + (i + 1) * 8)
            pre = s.big0[i * 8 : (i + 1) * 8, :]
            half = 0.5 + 0.5 * jnp.tanh(pre * (GELU_A + GELU_B * (pre * pre)))
            s.active[out, :] = (pre * half).astype(BF)
        s.gpre[rows, :] = nn(s.active[rows, :], s.dn[...]).astype(BF)
        ar2.d1_side(b).start()

    def pass_side(b):
        side_norm(b).wait_recv()
        side_pass(b).start()

    second_back(0)
    s.m0[:, left] = tn(s.normed2[...], s.gpre[:, left]).astype(BF)
    wide(wide_2[:1], "step1")
    ar3.s2(CH - 1)
    s.m0[:, right] = tn(s.normed2[...], s.gpre[:, right]).astype(BF)
    wide(wide_2[1:], "step1")
    attend_back(0)
    second_back(1)
    wide(wide_1, "step1b")
    ar2.s2(0)
    mlp_part(2)
    attend_back(1)
    keys_back(0)
    second_back(2)
    wide(wide_2, "step1b")
    first_part(0)
    ar2.s2(1)
    attend_back(2)
    keys_back(1)
    second_back(3)
    wide(wide_1, "step2")
    first_part(1)
    attend_back(3)
    keys_back(2)
    keys_back(3)
    wide(wide_2, "step2")
    s.m2[0 : 3 * W, left] = nn(s.gproj[...], s.normed[:, left]).astype(BF)
    wide(wide_3[:1], "step1")
    s.m2[0 : 3 * W, right] = nn(s.gproj[...], s.normed[:, right]).astype(BF)
    wide(wide_3[1:], "step1")
    wide(wide_1, "step3")
    ar2.s1(2)
    first_part(2)
    first_part(3)
    for which in range(2):
        rows = slice(which * W, (which + 1) * W)
        both = s.gacc[rows, 0:128] + s.gacc[rows, 128:256]
        s.vec[4 + which : 5 + which, 0:W] = jnp.sum(jnp.transpose(both), axis=0, keepdims=True)
    s.vecs[...] = s.vec[...]
    vec_c.start()
    for b in range(SIDE, CH):
        pass_side(b)
    wide(wide_2, "step3")
    ar4.s2(0)
    wide(wide_3, "step1b")
    wide(wide_1, "step4")
    ar4.s2(1)
    mlp_part(CH - 1)
    ar2.s1(CH - 1)

    def layer_out(b):
        ar2.d2(b).wait_recv()
        s.r22[b] = (s.mid[b] + ar2.total(b)).astype(BF)
        ar2.d3(b).start()
        lo_copy(b).start()

    def grad_tokens(b):
        ar4.d2(b).wait_recv()
        hat, rstd = moments(s.x[ar4.mine(b), :].astype(F32))
        s.r24[b] = (s.gact[b * HALF : (b + 1) * HALF, :] + norm_back(ar4.total(b) * ag, hat, rstd)).astype(BF)
        ar4.d3(b).start()
        gt_copy(b).start()

    upper = lax.broadcasted_iota(jnp.int32, (8, D), 0) < 4
    vec_c.wait_recv()
    s.v1[...] = s.vec[...] + jnp.where(upper, s.rvz[0], 0.0)
    s.rvx[k.x] = s.v1[...]
    for copy in vec_x:
        copy.start()
    side_mlp(2)
    wide(wide_3, "step2")
    wide(wide_2, "step4")
    wide(wide_1, "step5")
    for d in (1, 3):
        wide(wide_1, "step6", d)
    side_mlp(3)
    ar2.s2_side(2)
    k.await_recvs(s.rvx.at[pl.ds(0, 3)], vec_sem + 1)
    s.v2[...] = (s.rvx[0] + s.rvx[1]) + (s.rvx[2] + s.rvx[3])
    s.rvy[k.y] = s.v2[...]
    for copy in vec_y:
        copy.start()
    ar2.s2_side(3)
    wide(wide_3, "step3")
    wide(wide_2, "step5")
    for d in (1, 3):
        wide(wide_2, "step6", d)
    ar4.s2(2)
    ar2.s2(2)
    ar2.s2(3)
    layer_out(0)
    layer_out(1)
    grad_tokens(0)
    wide(wide_3, "step4")
    wide(wide_1, "step7")
    k.await_recvs(s.rvy.at[pl.ds(0, 3)], vec_sem + 2)
    s.v3[...] = (s.rvy[0] + s.rvy[1]) + (s.rvy[2] + s.rvy[3])
    vec_z.start()
    ar4.s2(3)
    wide(wide_2, "step7")
    grad_tokens(1)
    wide(wide_3, "step5")
    vec_z.wait_recv()
    s.v4[...] = s.v3[...] + s.rvz[1]
    vec_l.start()
    layer_out(2)
    grad_tokens(2)
    layer_out(3)
    vec_l.wait_recv()
    vec_out[...] = s.v4[...] + jnp.where(upper, s.rvz[2], 0.0)
    grad_tokens(3)

    half = pl.ds(0, T // 2)
    k.copy(s.p2.at[half], lo_out.at[half], out_sem).wait()
    k.copy(s.p4.at[half], gt_out.at[half], out_sem + 1).wait()
    for item in (ar2, ar3, ar4, *wide_1, *wide_2, *wide_3):
        item.finish()
    k.await_sends(s.wo.at[pl.ds(0, 3 * W)], wo_send)
    k.await_sends(s.mixed.at[pl.ds(0, 3 * W)], mix_send)
    k.await_sends(s.n2s.at[pl.ds(0, (CH - SIDE) * BLK)], side_send)
    k.await_sends(s.big0.at[pl.ds(0, 72)], vec_send)


PARTS = 4


def finish(lo, gt, gup, gdn, g2, vec, lo_o, gt_o, qkv_o, qg_o, kg_o, out_o, gup_o, gdn_o, ag_o, as_o, mg_o, ms_o, low, high, same, sem_in, sem_out):
    size = D // PARTS
    pieces = []
    for i, (src, dst) in enumerate(((gup, gup_o), (gdn, gdn_o), (g2, None))):
        for p in range(PARTS):
            rows = pl.ds(p * size, size)
            if dst is None:
                to = qkv_o.at[p] if p < 3 else out_o
            else:
                to = dst.at[rows]
            load = pltpu.make_async_copy(src.at[rows], low.at[i, rows], sem_in.at[i, p])
            pieces.append((load, (i, rows), pltpu.make_async_copy(high.at[i, rows], to, sem_out.at[i, p])))
    for i, (src, dst) in enumerate(((gt, gt_o), (lo, lo_o))):
        load = pltpu.make_async_copy(src, same.at[i], sem_in.at[3 + i, 0])
        store = pltpu.make_async_copy(same.at[i], dst, sem_out.at[3 + i, 0])
        pieces.insert(0, (load, None, store))
    for load, _, _ in pieces:
        load.start()
    for ref, row, count in (
        (ag_o, 0, D),
        (as_o, 1, D),
        (mg_o, 2, D),
        (ms_o, 3, D),
        (qg_o, 4, W),
        (kg_o, 5, W),
    ):
        ref[...] = vec[row : row + 1, 0:count].reshape(count)
    for load, cast, store in pieces:
        load.wait()
        if cast is not None:
            high[cast] = low[cast].astype(F32)
        store.start()
    for _, _, store in pieces:
        store.wait()


def body(*args):
    any_spec = pl.BlockSpec(memory_space=pl.ANY)
    vmem = pl.BlockSpec(memory_space=pltpu.VMEM)
    args = list(args)
    args[4] = jnp.swapaxes(args[4], 1, 2).reshape(3 * W, D)
    out = pl.pallas_call(
        kernel,
        out_shape=(
            jax.ShapeDtypeStruct((T, D), BF),
            jax.ShapeDtypeStruct((T, D), BF),
            jax.ShapeDtypeStruct((D, F), BF),
            jax.ShapeDtypeStruct((F, D), BF),
            jax.ShapeDtypeStruct((4 * W, D), BF),
            jax.ShapeDtypeStruct((8, D), F32),
        ),
        in_specs=[any_spec] * 14,
        out_specs=(any_spec, any_spec, any_spec, any_spec, any_spec, vmem),
        scratch_shapes=[pltpu.VMEM(shape, dtype) for shape, dtype in SCRATCH.values()]
        + [
            pltpu.SMEM((1,), jnp.int32),
            pltpu.SemaphoreType.DMA((NSEND,)),
            pltpu.SemaphoreType.DMA((NRECV,)),
            pltpu.SemaphoreType.DMA((NLOC,)),
        ],
        compiler_params=pltpu.CompilerParams(
            collective_id=0, has_side_effects=True, vmem_limit_bytes=60 * 1024 * 1024
        ),
        cost_estimate=pl.CostEstimate(
            flops=14 * 10**9, bytes_accessed=20 * 2**20, transcendentals=8 * 2**20
        ),
    )(*args)
    layer, tokens, qkv, *rest = pl.pallas_call(
        finish,
        out_shape=(
            jax.ShapeDtypeStruct((T, D), BF),
            jax.ShapeDtypeStruct((T, D), BF),
            jax.ShapeDtypeStruct((3, W, D), F32),
            jax.ShapeDtypeStruct((W,), F32),
            jax.ShapeDtypeStruct((W,), F32),
            jax.ShapeDtypeStruct((W, D), F32),
            jax.ShapeDtypeStruct((D, F), F32),
            jax.ShapeDtypeStruct((F, D), F32),
            jax.ShapeDtypeStruct((D,), F32),
            jax.ShapeDtypeStruct((D,), F32),
            jax.ShapeDtypeStruct((D,), F32),
            jax.ShapeDtypeStruct((D,), F32),
        ),
        in_specs=[any_spec] * 5 + [vmem],
        out_specs=(any_spec, any_spec, any_spec, vmem, vmem, any_spec, any_spec, any_spec)
        + (vmem,) * 4,
        scratch_shapes=[
            pltpu.VMEM((3, D, D), BF),
            pltpu.VMEM((3, D, D), F32),
            pltpu.VMEM((2, T, D), BF),
            pltpu.SemaphoreType.DMA((5, PARTS)),
            pltpu.SemaphoreType.DMA((5, PARTS)),
        ],
        compiler_params=pltpu.CompilerParams(vmem_limit_bytes=60 * 1024 * 1024),
        cost_estimate=pl.CostEstimate(flops=0, bytes_accessed=17 * 2**20, transcendentals=0),
    )(*out)
    return (layer, tokens, jnp.swapaxes(qkv, 1, 2), *rest)


def solution(mesh):
    placed = (
        P("wide", None),
        P("wide", None),
        P("wide", None),
        P("wide"),
        P(None, None, "narrow"),
        P("narrow"),
        P("narrow"),
        P("narrow", None),
        P(None, "narrow"),
        P("narrow", None),
        P(),
        P(),
        P(),
        P(),
    )
    return jax.shard_map(
        body,
        mesh=mesh,
        in_specs=placed,
        out_specs=(
            P("wide", None),
            P("wide", None),
            P(None, None, "narrow"),
            P("narrow"),
            P("narrow"),
            P("narrow", None),
            P(None, "narrow"),
            P("narrow", None),
            P(),
            P(),
            P(),
            P(),
        ),
        check_vma=False,
    )
```
